32 devices in a mesh: batch: 16 (over z, y, x), tower: 2 (over core).
Axes of the slice: x: 2, y: 2, z: 4, core: 2. Of those that a mesh axis runs over, the one named last changes fastest.
Arguments:
- crop_pixels: bfloat16 [512, 13, 13, 384], P(('batch', 'tower')), may hold values from -6 to 6
- live_rows: int32 [32], P(('batch', 'tower')), may hold values from 1 to 16, 256 in all
- conv_weight: bfloat16 [2, 3, 3, 384, 256], replicated, may hold values from -0.109375 to 0.109375
- conv_bias: float32 [2, 256], replicated, may hold values from -3 to 3
- stitch_conv: float32 [2, 2, 256], replicated, may hold values from 0.2 to 1
- fc_weight: bfloat16 [2, 9216, 4096], P('tower', 'batch'), may hold values from -0.25 to 0.25
- fc_bias: float32 [2, 4096], P('tower'), may hold values from -3 to 3
- stitch_fc: float32 [2, 2, 4096], replicated, may hold values from 0.2 to 1
- cotangent: bfloat16 [2, 512, 4096], P('tower', 'batch'), may hold values from -6 to 6
Outputs:
- stitched_out: bfloat16 [2, 512, 4096], P('tower', 'batch')
- d_crops: bfloat16 [512, 13, 13, 384], P(('batch', 'tower'))
- d_conv_weight: float32 [2, 3, 3, 384, 256], replicated
- d_conv_bias: float32 [2, 256], replicated
- d_stitch_conv: float32 [2, 2, 256], replicated
- d_fc_weight: float32 [2, 9216, 4096], P('tower', 'batch')
- d_fc_bias: float32 [2, 4096], replicated
- d_stitch_fc: float32 [2, 2, 4096], replicated
The draws below stay inside these ranges and needn't reach their ends.
Inputs may be any that keep to these rules, and one draw needn't show every extreme that they name: Each device's first live_rows slots hold crops, the others are padding; the counts add up to half of all 512 slots, and some device has all 16 slots live.
All inputs are finite; a program needn't handle non-finite values.
Results may differ from the reference program's by a relative error of at most 0.0073.
Values may be sent and summed in bfloat16 or wider, within the bound.
A program may use at most 384 MiB of HBM per device.

```python
import math
import jax
import jax.numpy as jnp
import numpy as np
from jax import lax

CIN = 384
COUT = 256
FC = 4096
SIDE = 13
CAP = 16
POOL = 6
FEAT = 9216
ROWS = 512
N_BATCH = 16
N_TOWER = 2


def level_of(key, extent, shards, smallest, high):
    def one(dim, blocks):
        draws = jax.random.uniform(jax.random.fold_in(jax.random.fold_in(key, 6), dim), (blocks,), jnp.float32, smallest / len(shards), high / len(shards))
        return jnp.repeat(jnp.exp(draws), extent[dim] // blocks).reshape((-1,) + (1,) * (len(extent) - dim - 1))

    factor_of = one(*shards[0])
    for cut in shards[1:]:
        factor_of = factor_of * one(*cut)
    return factor_of


def length_profile(amount, total, most, lean):
    loads = [(1 << 20) // math.isqrt(rank ** lean) + 1 for rank in range(2, amount + 1)]
    spare, given = total - most - (amount - 1), [1] * (amount - 1)
    while spare > 0:
        candidates = [i for i in range(amount - 1) if given[i] < most]
        mass, budget = sum([loads[i] for i in candidates]), spare
        for i in candidates:
            more = min(most - given[i], max(1, budget * loads[i] // mass), spare)
            given[i] = given[i] + more
            spare = spare - more
    return np.array([most] + given)


def uneven(rng, number_of, total, limit, slope):
    if number_of == 2:
        one = jax.random.randint(rng, (), max(1, total - limit), min(limit, total - 1) + 1)
        return jnp.stack([one, total - one])
    tallies = jnp.asarray(length_profile(number_of, total, limit, slope), jnp.int32)
    pairs = (number_of - 1) // 2
    source_of, taker = tallies[1:1 + 2 * pairs:2], tallies[2:2 + 2 * pairs:2]
    slack = jnp.minimum(source_of - 1, limit - taker)
    moved = jax.random.randint(jax.random.fold_in(rng, 1), (pairs,), 0, 1 << 20) % (slack + 1)
    tallies = tallies.at[1:1 + 2 * pairs:2].set(source_of - moved).at[2:2 + 2 * pairs:2].set(taker + moved)
    return tallies[jax.random.permutation(jax.random.fold_in(rng, 2), number_of)]


def centred(stream_key, dims, spread, limit, shards=(), kind=jnp.bfloat16):
    loudness = level_of(stream_key, dims, shards, -0.22, 0.18) if shards else 1.0
    values = jax.random.normal(stream_key, dims, jnp.float32) * spread * loudness
    return jnp.minimum(jnp.maximum(values, -limit), limit).astype(kind)


def setup_inputs(seed: int = 0) -> dict:
    seeds = jax.random.split(jax.random.key(seed), 10)
    return {
        "crop_pixels": centred(seeds[0], (ROWS, SIDE, SIDE, CIN), 1.0, 6.0, ((0, 32),)),
        "live_rows": uneven(seeds[1], N_BATCH * N_TOWER, CAP // 2 * N_BATCH * N_TOWER, CAP, 2).astype(jnp.int32),
        "conv_weight": centred(seeds[2], (2, 3, 3, CIN, COUT), (9 * CIN) ** -0.5, 0.109375),
        "conv_bias": centred(seeds[3], (2, COUT), 0.5, 3.0, (), jnp.float32),
        "stitch_conv": jnp.clip(jax.random.uniform(seeds[4], (2, 2, COUT), jnp.float32, 0.2, 1.0), 0.2, 1.0),
        "fc_weight": centred(seeds[5], (2, FEAT, FC), (FEAT // 16) ** -0.5, 0.25, ((0, 2), (1, 16))),
        "fc_bias": centred(seeds[6], (2, FC), 0.5, 3.0, ((0, 2),), jnp.float32),
        "stitch_fc": jnp.clip(jax.random.uniform(seeds[7], (2, 2, FC), jnp.float32, 0.2, 1.0), 0.2, 1.0),
        "cotangent": centred(seeds[8], (2, ROWS, FC), 1.0, 6.0, ((0, 2), (1, 16))),
    }


@jax.custom_vjp
def low(v):
    return lax.optimization_barrier(v.astype(jnp.bfloat16)).astype(jnp.float32)

@jax.custom_vjp
def low_back(v):
    return v

def low_keep(v):
    return (low(v), None)

def low_pass(kept, grad):
    return (grad,)

def back_keep(v):
    return (v, None)

def back_low(kept, grad):
    return (low(grad),)
low.defvjp(low_keep, low_pass)
low_back.defvjp(back_keep, back_low)

def conv_tower(pixels, kernel):
    return lax.conv_general_dilated(pixels, kernel, (1, 1), 'SAME', dimension_numbers=('NHWC', 'HWIO', 'NHWC'), precision=lax.Precision.HIGHEST)

def mean_pool(values):
    span = 2 * POOL - 1
    total = jnp.zeros_like(values[:, 0:span:2, 0:span:2])
    for row_tap in range(3):
        for col_tap in range(3):
            total = total + values[:, row_tap:row_tap + span:2, col_tap:col_tap + span:2]
    return total / 9.0

def reference(crop_pixels, live_rows, conv_weight, conv_bias, stitch_conv, fc_weight, fc_bias, stitch_fc, cotangent):
    devices = N_BATCH * N_TOWER
    slot_index = jnp.arange(ROWS, dtype=jnp.int32)
    owner = (slot_index // CAP).astype(jnp.int32)
    alive_rows = (slot_index % CAP < live_rows[owner]).astype(jnp.float32)

    def forward(pixels, conv_w, conv_b, mix_conv, dense_w, dense_b, mix_dense):

        def tower_block(block_pixels):
            preact = jnp.stack([conv_tower(block_pixels, conv_w[tower_id]) for tower_id in range(2)], axis=3)
            preact = low_back(preact + conv_b[None, None, None])
            pooled = mean_pool(jax.nn.gelu(preact))
            mixed = jnp.stack([mix_conv[tower_id, 0] * pooled[:, :, :, 0] + mix_conv[tower_id, 1] * pooled[:, :, :, 1] for tower_id in range(2)], axis=1)
            return low(low_back(mixed.reshape(CAP, 2, FEAT)))
        blocks = pixels.reshape(devices, CAP, SIDE, SIDE, CIN)
        features = lax.map(jax.checkpoint(tower_block), blocks).reshape(ROWS, 2, FEAT)
        hidden = jnp.stack([jnp.dot(features[:, tower_id], dense_w[tower_id], precision=lax.Precision.HIGHEST) + dense_b[tower_id] for tower_id in range(2)], axis=0)
        hidden = low_back(hidden)
        gate = low(jax.nn.gelu(hidden))
        stitched = jnp.stack([mix_dense[tower_id, 0] * gate[0] + mix_dense[tower_id, 1] * gate[1] for tower_id in range(2)], axis=0)
        return stitched * alive_rows[None, :, None]
    primals = (crop_pixels.astype(jnp.float32), conv_weight.astype(jnp.float32), conv_bias, stitch_conv, fc_weight.astype(jnp.float32), fc_bias, stitch_fc)
    result, pullback = jax.vjp(forward, *primals)
    grads = pullback(cotangent.astype(jnp.float32))
    return (result.astype(jnp.bfloat16), grads[0].astype(jnp.bfloat16), grads[1], grads[2], grads[3], grads[4], grads[5], grads[6])
```

```python
import functools, math
import jax, jax.numpy as jnp
from jax import lax
from jax.experimental import pallas as pl
from jax.experimental.pallas import tpu as pltpu
from jax.sharding import PartitionSpec as P
F32, BF16 = jnp.float32, jnp.bfloat16
CG = math.sqrt(2.0 / math.pi)

def gelu_pair(v):
    sq = v * v
    t = jnp.tanh(v * (CG + (CG * 0.044715) * sq))
    half = 0.5 + 0.5 * t
    value = v * half
    slope = half + value * (1.0 - half) * (2.0 * CG + (6.0 * CG * 0.044715) * sq)
    return value, slope

def conv_fwd_kernel(rows_per, x_ref, w_ref, b_ref, mix_ref, feat_ref, pooled_ref, slope_ref, p_ref, stage, act, fbuf):
    slots, side, _, cin = x_ref.shape
    towers, _, cout = w_ref.shape
    pool = (side - 3) // 2 + 1
    pitch = 16
    lanes = cin // 128
    p_ref[0] = jnp.zeros(p_ref.shape[1:], BF16)
    p_ref[side + 1] = jnp.zeros(p_ref.shape[1:], BF16)
    def put(k, _):
        r = k // side
        i = k % side
        v = x_ref[r, i].astype(F32)
        for l in range(lanes):
            stage[l, pl.ds(pl.multiple_of(k * pitch, pitch), side), :] = v[:, l * 128:(l + 1) * 128]
        return 0
    lax.fori_loop(0, slots * side, put, 0, unroll=4)
    def take(i, _):
        p_ref[i + 1, 0] = jnp.zeros((slots, cin), BF16)
        p_ref[i + 1, side + 1] = jnp.zeros((slots, cin), BF16)
        for j in range(side):
            for l in range(lanes):
                v = stage[l, pl.ds(i * pitch + j, slots, stride=side * pitch), :]
                p_ref[i + 1, j + 1, :, l * 128:(l + 1) * 128] = v.astype(BF16)
        return 0
    lax.fori_loop(0, side, take, 0)
    rows = rows_per * side * slots
    def row(y):
        window = jnp.concatenate(
            [p_ref[pl.ds(y + a, rows_per), b:b + side].reshape(rows, cin) for a in range(3) for b in range(3)], axis=1)
        for t in range(towers):
            pre = jnp.dot(window, w_ref[t], preferred_element_type=F32) + b_ref[t][None]
            value, slope = gelu_pair(pre)
            act[pl.ds(y, rows_per), :, :, t * cout:(t + 1) * cout] = value.reshape(rows_per, side, slots, cout)
            slope_ref[pl.ds(y, rows_per), :, :, t * cout:(t + 1) * cout] = slope.astype(BF16).reshape(rows_per, side, slots, cout)
    lax.fori_loop(0, side // rows_per, lambda k, _: (row(k * rows_per), 0)[1], 0)
    for i in range(pool):
        s3 = act[2 * i] + act[2 * i + 1] + act[2 * i + 2]
        for j in range(pool):
            p9 = (s3[2 * j] + s3[2 * j + 1] + s3[2 * j + 2]) * (1.0 / 9.0)
            pooled_ref[i * pool + j] = p9
            for t in range(towers):
                m = mix_ref[t, 0][None] * p9[:, :cout] + mix_ref[t, 1][None] * p9[:, cout:]
                fbuf[t, :, (i * pool + j) * cout:(i * pool + j + 1) * cout] = m.astype(BF16)
    nb, per = feat_ref.shape[1], feat_ref.shape[3]
    for t in range(towers):
        for b in range(nb):
            feat_ref[t, b] = fbuf[t, :, b * per:(b + 1) * per]

def conv_fwd(x, w, bias, mix, nb, rows_per=1):
    slots, side, _, cin = x.shape
    towers, _, _, _, cout = w.shape
    pool = (side - 3) // 2 + 1
    nf = pool * pool * cout
    V = pl.BlockSpec(memory_space=pltpu.VMEM)
    return pl.pallas_call(
        functools.partial(conv_fwd_kernel, rows_per),
        out_shape=[jax.ShapeDtypeStruct((towers, nb, slots, nf // nb), BF16),
                   jax.ShapeDtypeStruct((pool * pool, slots, towers * cout), F32),
                   jax.ShapeDtypeStruct((side, side, slots, towers * cout), BF16),
                   jax.ShapeDtypeStruct((side + 2, side + 2, slots, cin), BF16)],
        in_specs=[V] * 4, out_specs=[V] * 4,
        scratch_shapes=[pltpu.VMEM((cin // 128, slots * side * 16, 128), F32),
                        pltpu.VMEM((side, side, slots, towers * cout), F32),
                        pltpu.VMEM((towers, slots, nf), BF16)],
        compiler_params=pltpu.CompilerParams(vmem_limit_bytes=60 * 2**20),
    )(x, w.reshape(towers, 9 * cin, cout), bias, mix)

def conv_bwd_kernel(dm_ref, pooled_ref, slope_ref, p_ref, w_ref, mix_ref, dx_ref, dw_ref, small_ref,
                    fbuf, z, dpad, d2, dt, stage):
    towers, nb, slots, per = dm_ref.shape
    side = slope_ref.shape[0]
    cout = w_ref.shape[2]
    cin = p_ref.shape[3]
    pool = (side - 3) // 2 + 1
    wide = towers * cout
    cells = side * side
    for t in range(towers):
        for b in range(nb):
            fbuf[t, :, b * per:(b + 1) * per] = dm_ref[t, b]
    z[0] = jnp.zeros(z.shape[1:], F32)
    z[pool + 1] = jnp.zeros(z.shape[1:], F32)
    acc = [[jnp.zeros((slots, cout), F32)] * 2 for _ in range(2)]
    for i in range(pool):
        z[i + 1, 0] = jnp.zeros(z.shape[2:], F32)
        z[i + 1, pool + 1] = jnp.zeros(z.shape[2:], F32)
        for j in range(pool):
            q = i * pool + j
            dm = [fbuf[t, :, q * cout:(q + 1) * cout].astype(F32) for t in range(towers)]
            for u in range(towers):
                pu = pooled_ref[q, :, u * cout:(u + 1) * cout]
                for t in range(towers):
                    acc[t][u] = acc[t][u] + dm[t] * pu
                z[i + 1, j + 1, :, u * cout:(u + 1) * cout] = (mix_ref[0, u][None] * dm[0] + mix_ref[1, u][None] * dm[1]) * (1.0 / 9.0)
    dpad[0] = jnp.zeros(dpad.shape[1:], BF16)
    dpad[side + 1] = jnp.zeros(dpad.shape[1:], BF16)
    d2[cells:] = jnp.zeros((d2.shape[0] - cells, slots, wide), BF16)
    def drow(y, src):
        dpad[y + 1, 0] = jnp.zeros((slots, wide), BF16)
        dpad[y + 1, side + 1] = jnp.zeros((slots, wide), BF16)
        for x in range(side):
            j = x // 2
            v = src(j + 1) if x % 2 else src(j) + src(j + 1)
            d = (v * slope_ref[y, x].astype(F32)).astype(BF16)
            dpad[y + 1, x + 1] = d
            d2[y * side + x] = d
    def pair(i, _):
        drow(2 * i, lambda j: z[i, j] + z[i + 1, j])
        drow(2 * i + 1, lambda j: z[i + 1, j])
        return 0
    lax.fori_loop(0, pool, pair, 0)
    drow(side - 1, lambda j: z[pool, j] + z[pool + 1, j])
    step = 256 // slots
    def flip(k, _):
        dt[:, pl.ds(pl.multiple_of(k * 256, 256), 256)] = d2[pl.ds(k * step, step)].reshape(256, wide).T
        return 0
    lax.fori_loop(0, d2.shape[0] // step, flip, 0)
    tail = (d2.shape[0] - cells) * slots
    for a in range(3):
        win = jnp.concatenate([p_ref[a:a + side, b:b + side].reshape(cells * slots, cin) for b in range(3)], axis=1)
        win = jnp.concatenate([win, jnp.zeros((tail, 3 * cin), BF16)], axis=0)
        dw_ref[a] = jnp.dot(dt[...], win, preferred_element_type=F32)
    ones = jnp.ones((d2.shape[0] * slots, 128), BF16)
    small_ref[:, 0:128] = jnp.dot(dt[...], ones, preferred_element_type=F32)
    rows = jnp.concatenate([jnp.concatenate([jnp.sum(acc[t][u], axis=0, keepdims=True) for u in range(2)], axis=1) for t in range(2)], axis=0)
    small_ref[:, 128:256] = jnp.concatenate([rows, jnp.zeros((126, wide), F32)], axis=0).T
    pitch = 16
    def xrow(y):
        lhs = jnp.concatenate([dpad[y + 2 - a, 2 - b:2 - b + side, :, t * cout:(t + 1) * cout].reshape(side * slots, cout)
                               for t in range(towers) for a in range(3) for b in range(3)], axis=1)
        rhs = jnp.concatenate([w_ref[t, (a * 3 + b) * cin:(a * 3 + b + 1) * cin, :]
                               for t in range(towers) for a in range(3) for b in range(3)], axis=1)
        out = lax.dot_general(lhs, rhs, (((1,), (1,)), ((), ())), preferred_element_type=F32).reshape(side, slots, cin)
        for x in range(side):
            for l in range(cin // 128):
                stage[l, pl.ds(y * pitch + x, slots, stride=side * pitch), :] = out[x, :, l * 128:(l + 1) * 128]
    lax.fori_loop(0, side, lambda y, _: (xrow(y), 0)[1], 0)
    def put(k, _):
        r = k // side
        i = k % side
        dx_ref[r, i] = jnp.concatenate([stage[l, pl.ds(pl.multiple_of(k * pitch, pitch), side), :] for l in range(cin // 128)], axis=1).astype(BF16)
        return 0
    lax.fori_loop(0, slots * side, put, 0, unroll=4)

def conv_bwd(dm, pooled, slope, p, w, mix):
    towers, nb, slots, per = dm.shape
    side = slope.shape[0]
    cin = p.shape[3]
    cout = w.shape[4]
    pool = (side - 3) // 2 + 1
    wide = towers * cout
    V = pl.BlockSpec(memory_space=pltpu.VMEM)
    cells = -(-side * side * slots // 256) * 256 // slots
    return pl.pallas_call(
        conv_bwd_kernel,
        out_shape=[jax.ShapeDtypeStruct((slots, side, side, cin), BF16),
                   jax.ShapeDtypeStruct((3, wide, 3 * cin), F32),
                   jax.ShapeDtypeStruct((wide, 256), F32)],
        in_specs=[V] * 6, out_specs=[V] * 3,
        scratch_shapes=[pltpu.VMEM((towers, slots, nb * per), BF16),
                        pltpu.VMEM((pool + 2, pool + 2, slots, wide), F32),
                        pltpu.VMEM((side + 2, side + 2, slots, wide), BF16),
                        pltpu.VMEM((cells, slots, wide), BF16),
                        pltpu.VMEM((wide, cells * slots), BF16),
                        pltpu.VMEM((cin // 128, slots * side * 16, 128), F32)],
        compiler_params=pltpu.CompilerParams(vmem_limit_bytes=62 * 2**20),
    )(dm, pooled, slope, p, w.reshape(towers, 9 * cin, cout), mix)


def swap(block):
    return lax.ppermute(block, "tower", [(0, 1), (1, 0)])


def shards(crop_pixels, live_rows, conv_weight, conv_bias, stitch_conv, fc_weight, fc_bias, stitch_fc, cotangent):
    slots = crop_pixels.shape[0]
    nb = lax.axis_size("batch")
    b, t = lax.axis_index("batch"), lax.axis_index("tower")
    rows = 2 * slots * nb
    live = rows // 2
    fc = fc_weight.shape[2]
    per = fc_weight.shape[1]
    cols = fc // nb
    w = fc_weight[0]
    feat, pooled, slope, padded = conv_fwd(crop_pixels, conv_weight, conv_bias, stitch_conv, nb)
    both = ("batch", "tower")
    counts = lax.all_gather(live_rows, both, axis=0, tiled=True)
    got = lax.all_to_all(feat.transpose(1, 0, 2, 3).reshape(2 * nb, slots, per), both, 0, 0).reshape(rows, per)
    slot = jnp.arange(rows, dtype=jnp.int32)
    start = jnp.cumsum(counts) - counts
    place = jnp.where(slot % slots < counts[slot // slots], start[slot // slots] + slot % slots, -1)
    spread = (place[:, None] == jnp.arange(live, dtype=jnp.int32)[None]).astype(BF16)
    compact = lambda x: lax.dot_general(spread, x, (((0,), (0,)), ((), ())), preferred_element_type=F32).astype(BF16)
    expand = lambda x: jnp.dot(spread, x, preferred_element_type=F32).astype(BF16)
    f = compact(got)
    part = jnp.dot(f, w, preferred_element_type=F32)
    hidden = lax.psum_scatter(part, "batch", scatter_dimension=1, tiled=True)
    hidden = hidden + lax.dynamic_slice_in_dim(fc_bias[0], b * cols, cols)[None]
    value, slope_fc = gelu_pair(hidden)
    gate = value.astype(BF16)
    cot = compact(lax.all_to_all(cotangent[0].reshape(2 * slots, nb, cols).transpose(1, 0, 2), "batch", 0, 0).reshape(rows, cols))
    gate_other, cot_other = swap(gate).astype(F32), swap(cot).astype(F32)
    gate_own, cot_own = gate.astype(F32), cot.astype(F32)
    mix = lax.dynamic_slice_in_dim(stitch_fc, b * cols, cols, axis=2)
    own = jnp.where(t == 0, mix[0, 0], mix[1, 1])
    cross = jnp.where(t == 0, mix[0, 1], mix[1, 0])
    back = jnp.where(t == 0, mix[1, 0], mix[0, 1])
    stitched = (own[None] * gate_own + cross[None] * gate_other).astype(BF16)
    stitched = lax.all_to_all(expand(stitched).reshape(nb, 2 * slots, cols), "batch", 0, 0)
    stitched = stitched.transpose(1, 0, 2).reshape(1, 2 * slots, fc)
    d_own = jnp.sum(cot_own * gate_own, axis=0)
    d_cross = jnp.sum(cot_own * gate_other, axis=0)
    dh = ((own[None] * cot_own + back[None] * cot_other) * slope_fc).astype(BF16)
    sums = jnp.stack([d_own, d_cross, jnp.sum(dh.astype(F32), axis=0)])
    sums = lax.all_gather(sums, both, axis=0).reshape(nb, 2, 3, cols).transpose(1, 2, 0, 3).reshape(2, 3, fc)
    d_stitch_fc = jnp.stack([sums[0, :2], sums[1, 1::-1]])
    d_fc_bias = sums[:, 2]
    dh = lax.all_gather(dh, "batch", axis=1, tiled=True)
    d_fc_weight = lax.dot_general(f, dh, (((0,), (0,)), ((), ())), preferred_element_type=F32)[None]
    df = lax.dot_general(dh, w, (((1,), (1,)), ((), ())), preferred_element_type=F32).astype(BF16)
    dm = lax.all_to_all(expand(df).reshape(2 * nb, slots, per), both, 0, 0)
    dm = dm.reshape(nb, 2, slots, per).transpose(1, 0, 2, 3)
    dx, dw, small = conv_bwd(dm, pooled, slope, padded, conv_weight, stitch_conv)
    dw = lax.psum(dw, both)
    cin, cout = conv_weight.shape[3:]
    dw = dw.reshape(3, 2, cout, 3, cin).transpose(1, 0, 3, 4, 2)
    small = lax.psum(small, both)
    d_conv_bias = small[:, 0].reshape(2, cout)
    d_stitch_conv = small[:, 128:130].T.reshape(2, 2, cout)
    return stitched, dx, dw, d_conv_bias, d_stitch_conv, d_fc_weight, d_fc_bias, d_stitch_fc


def solution(mesh):
    in_specs = (
        P(("batch", "tower"), None, None, None), P(("batch", "tower")), P(), P(), P(),
        P("tower", "batch", None), P("tower", None), P(), P("tower", "batch", None),
    )
    out_specs = (
        P("tower", "batch", None), P(("batch", "tower"), None, None, None), P(), P(), P(),
        P("tower", "batch", None), P(), P(),
    )
    return jax.shard_map(shards, mesh=mesh, in_specs=in_specs, out_specs=out_specs, check_vma=False)
```

```python
import functools, math
import jax, jax.numpy as jnp
from jax import lax
from jax.experimental import pallas as pl
from jax.experimental.pallas import tpu as pltpu
from jax.sharding import PartitionSpec as P
F32, BF16 = jnp.float32, jnp.bfloat16
CG = math.sqrt(2.0 / math.pi)

def gelu_pair(v):
    sq = v * v
    t = jnp.tanh(v * (CG + (CG * 0.044715) * sq))
    half = 0.5 + 0.5 * t
    value = v * half
    slope = half + value * (1.0 - half) * (2.0 * CG + (6.0 * CG * 0.044715) * sq)
    return value, slope

def conv_fwd_kernel(rows_per, live_ref, x_ref, w_ref, b_ref, mix_ref, feat_ref, pooled_ref, slope_ref, p_ref, stage, act, fbuf):
    slots, side, _, cin = x_ref.shape
    towers, _, cout = w_ref.shape
    pool = (side - 3) // 2 + 1
    pitch = 16
    lanes = cin // 128
    p_ref[0] = jnp.zeros(p_ref.shape[1:], BF16)
    p_ref[side + 1] = jnp.zeros(p_ref.shape[1:], BF16)
    def put(k, _):
        r = k // side
        i = k % side
        v = x_ref[r, i].astype(F32)
        for l in range(lanes):
            stage[l, pl.ds(pl.multiple_of(k * pitch, pitch), side), :] = v[:, l * 128:(l + 1) * 128]
        return 0
    lax.fori_loop(0, slots * side, put, 0, unroll=4)
    def take(i, _):
        p_ref[i + 1, 0] = jnp.zeros((slots, cin), BF16)
        p_ref[i + 1, side + 1] = jnp.zeros((slots, cin), BF16)
        for j in range(side):
            for l in range(lanes):
                v = stage[l, pl.ds(i * pitch + j, slots, stride=side * pitch), :]
                p_ref[i + 1, j + 1, :, l * 128:(l + 1) * 128] = v.astype(BF16)
        return 0
    lax.fori_loop(0, side, take, 0)
    rows = rows_per * side * slots
    def row(y):
        window = jnp.concatenate(
            [p_ref[pl.ds(y + a, rows_per), b:b + side].reshape(rows, cin) for a in range(3) for b in range(3)], axis=1)
        for t in range(towers):
            pre = jnp.dot(window, w_ref[t], preferred_element_type=F32) + b_ref[t][None]
            value, slope = gelu_pair(pre)
            act[pl.ds(y, rows_per), :, :, t * cout:(t + 1) * cout] = value.reshape(rows_per, side, slots, cout)
            slope_ref[pl.ds(y, rows_per), :, :, t * cout:(t + 1) * cout] = slope.astype(BF16).reshape(rows_per, side, slots, cout)
    lax.fori_loop(0, side // rows_per, lambda k, _: (row(k * rows_per), 0)[1], 0)
    for i in range(pool):
        s3 = act[2 * i] + act[2 * i + 1] + act[2 * i + 2]
        for j in range(pool):
            p9 = (s3[2 * j] + s3[2 * j + 1] + s3[2 * j + 2]) * (1.0 / 9.0)
            pooled_ref[i * pool + j] = p9
            for t in range(towers):
                m = mix_ref[t, 0][None] * p9[:, :cout] + mix_ref[t, 1][None] * p9[:, cout:]
                fbuf[t, :, (i * pool + j) * cout:(i * pool + j + 1) * cout] = m.astype(BF16)
    nb = feat_ref.shape[1]
    per = fbuf.shape[2] // nb
    flags = (lax.broadcasted_iota(jnp.int32, (slots, feat_ref.shape[3] - per), 0) < live_ref[0]).astype(F32).astype(BF16)
    for t in range(towers):
        for b in range(nb):
            feat_ref[t, b, :, :per] = fbuf[t, :, b * per:(b + 1) * per]
            feat_ref[t, b, :, per:] = flags

def conv_fwd(live, x, w, bias, mix, nb, rows_per=1):
    slots, side, _, cin = x.shape
    towers, _, _, _, cout = w.shape
    pool = (side - 3) // 2 + 1
    nf = pool * pool * cout
    V = pl.BlockSpec(memory_space=pltpu.VMEM)
    return pl.pallas_call(
        functools.partial(conv_fwd_kernel, rows_per),
        out_shape=[jax.ShapeDtypeStruct((towers, nb, slots, nf // nb // 128 * 128 + 128), BF16),
                   jax.ShapeDtypeStruct((pool * pool, slots, towers * cout), F32),
                   jax.ShapeDtypeStruct((side, side, slots, towers * cout), BF16),
                   jax.ShapeDtypeStruct((side + 2, side + 2, slots, cin), BF16)],
        in_specs=[pl.BlockSpec(memory_space=pltpu.SMEM)] + [V] * 4, out_specs=[V] * 4,
        scratch_shapes=[pltpu.VMEM((cin // 128, slots * side * 16, 128), F32),
                        pltpu.VMEM((side, side, slots, towers * cout), F32),
                        pltpu.VMEM((towers, slots, nf), BF16)],
        compiler_params=pltpu.CompilerParams(vmem_limit_bytes=60 * 2**20),
    )(live, x, w.reshape(towers, 9 * cin, cout), bias, mix)


MESH_ID = pl.DeviceIdType.MESH


def torus(nb):
    return {16: (4, 2, 2), 64: (4, 4, 4)}.get(nb, (nb, 1, 1))


class Place:
    def __init__(self, nb):
        self.dims = torus(nb)
        self.b, self.t = lax.axis_index("batch"), lax.axis_index("tower")
        d0, d1, d2 = self.dims
        self.at = (self.b // (d1 * d2), (self.b // d2) % d1, self.b % d2)

    def peer(self, dim, k):
        c = list(self.at)
        c[dim] = k
        return ((c[0] * self.dims[1] + c[1]) * self.dims[2] + c[2], self.t)


def send(src, dst, ssem, rsem, device):
    copy = pltpu.make_async_remote_copy(src_ref=src, dst_ref=dst, send_sem=ssem, recv_sem=rsem, device_id=device, device_id_type=MESH_ID)
    copy.start()
    return copy


def greet(nb, me):
    bar = pltpu.get_barrier_semaphore()
    total = 2 * nb
    def hail(k, _):
        d = lax.rem(me + k, total)
        pl.semaphore_signal(bar, inc=1, device_id=(d // 2, d % 2), device_id_type=MESH_ID)
        return 0
    lax.fori_loop(1, total, hail, 0)
    pl.semaphore_wait(bar, total - 1)


class Sum:
    def __init__(self, place, p, s, r1, t1, r2, t2, r3, g, ssem, rsem):
        self.place, self.p, self.q = place, p, 3 - p
        self.s, self.r1, self.t1, self.r2, self.t2, self.r3, self.g = s, r1, t1, r2, t2, r3, g
        self.ssem, self.rsem = ssem, rsem
        self.sent = []
        self.used = 0

    def pick(self, ref, k):
        return ref.at[:, :, k] if self.p == 2 else ref.at[:, k]

    def post(self, dim, src_of, dst_of):
        n = self.place.dims[dim]
        self.flight = []
        for j in range(1, n):
            k = lax.rem(self.place.at[dim] + j, n)
            i = self.used
            self.used += 1
            self.flight.append(send(src_of(k), dst_of(j - 1), self.ssem.at[i], self.rsem.at[i], self.place.peer(dim, k)))
        self.sent += self.flight

    def arrive(self):
        for c in self.flight:
            c.wait_recv()

    def add(self, mine, got, n):
        v = mine.astype(F32)
        for j in range(n):
            v = v + got[j].astype(F32)
        return v

    def send1(self):
        self.post(self.p, lambda k: self.pick(self.s, k), lambda j: self.r1.at[j])

    def send2(self):
        self.arrive()
        n = self.place.dims[self.p]
        self.t1[...] = self.add(self.pick(self.s, self.place.at[self.p])[...], self.r1, n - 1).astype(BF16)
        self.post(self.q, lambda k: self.t1.at[:, k], lambda j: self.r2.at[j])

    def send3(self):
        self.arrive()
        n = self.place.dims[self.q]
        self.t2[...] = self.add(self.t1[:, self.place.at[self.q]], self.r2, n - 1).astype(BF16)
        self.post(0, lambda k: self.t2.at[k], lambda j: self.r3.at[j])

    def result(self):
        self.arrive()
        return self.add(self.t2[self.place.at[0]], self.r3, self.place.dims[0] - 1)

    def gather1(self):
        mine = self.g.at[self.place.at[0], self.place.at[1], self.place.at[2]]
        self.post(0, lambda k: mine, lambda j: mine)

    def gather2(self):
        self.arrive()
        mine = self.g.at[:, self.place.at[1], self.place.at[2]]
        self.post(self.q, lambda k: mine, lambda j: mine)

    def gather3(self):
        self.arrive()
        mine = self.pick(self.g, self.place.at[self.p])
        self.post(self.p, lambda k: mine, lambda j: mine)

    def close(self):
        for c in self.sent:
            c.wait_send()


def hops(nb):
    return 2 * sum(d - 1 for d in torus(nb))


def fc_kernel(parts, nb, per, feat_ref, cot_ref, w_hbm, bias_ref, mix_ref,
              out_ref, f_ref, dh_ref, dm_ref, sums_ref,
              w, fin, cin, cgot, spread, s, r1, t1, r2, t2, r3, g, keep, gates, cots, wide, st, sgot, dsl, acc,
              wsem, fs, fr, cs, cr, xs, xr, ss, sr, ms, mr, gs, gr):
    place = Place(nb)
    b, t = place.b, place.t
    me = b * 2 + t
    total = 2 * nb
    slots = feat_ref.shape[2]
    rows = total * slots
    live = rows // 2
    cols = cin.shape[2]
    pair = 2 * slots
    load = pltpu.make_async_copy(w_hbm, w, wsem)
    load.start()
    greet(nb, me)
    def feature_copy(k):
        d = lax.rem(me + k, total)
        return pltpu.make_async_remote_copy(
            src_ref=feat_ref.at[d % 2, d // 2], dst_ref=fin.at[me], send_sem=fs.at[k], recv_sem=fr.at[k],
            device_id=(d // 2, d % 2), device_id_type=MESH_ID)
    lax.fori_loop(1, total, lambda k, _: (feature_copy(k).start(), 0)[1], 0)
    fin[me] = feat_ref[t, b]
    for k in range(nb):
        cin[k] = cot_ref[:, k * cols:(k + 1) * cols]
    def cot_copy(k):
        d = lax.rem(b + k, nb)
        return pltpu.make_async_remote_copy(
            src_ref=cin.at[d], dst_ref=cgot.at[b], send_sem=cs.at[k], recv_sem=cr.at[k],
            device_id=(d, t), device_id_type=MESH_ID)
    lax.fori_loop(1, nb, lambda k, _: (cot_copy(k).start(), 0)[1], 0)
    cgot[b] = cin[b]
    lax.fori_loop(1, total, lambda k, _: (feature_copy(k).wait_recv(), 0)[1], 0)
    got = fin[...].reshape(rows, fin.shape[2])
    flag = got[:, per:per + 1]
    lanes = jnp.broadcast_to(flag, (rows, 128))
    lower = (lax.broadcasted_iota(jnp.int32, (rows, rows), 1) < lax.broadcasted_iota(jnp.int32, (rows, rows), 0)).astype(BF16)
    index = jnp.dot(lower, lanes, preferred_element_type=F32)[:, :1].astype(jnp.int32)
    hit = (index == lax.broadcasted_iota(jnp.int32, (rows, live), 1)) & (flag.astype(F32) > 0.5)
    spread[...] = hit.astype(F32).astype(BF16)
    pack = lambda x: lax.dot_general(spread[...], x, (((0,), (0,)), ((), ())), preferred_element_type=F32)
    f_ref[...] = pack(got[:, :per]).astype(BF16)
    load.wait()
    for k in range(nb):
        i = (k // (place.dims[1] * place.dims[2]), (k // place.dims[2]) % place.dims[1], k % place.dims[2])
        s[i] = jnp.dot(f_ref[...], w[:, k * cols:(k + 1) * cols], preferred_element_type=F32).astype(BF16)
    size = live // (2 * parts)
    pieces = []
    for n in range(2 * parts):
        half = n % 2
        low = pl.ds(((n // 2) + half * parts) * size, size)
        pieces.append((Sum(place, 2 - half, s.at[:, :, :, low], r1.at[n], t1.at[n], r2.at[n], t2.at[n], r3.at[n],
                           g.at[:, :, :, low], gs.at[n], gr.at[n]), low))
    for piece, _ in pieces:
        piece.send1()
    lax.fori_loop(1, nb, lambda k, _: (cot_copy(k).wait_recv(), 0)[1], 0)
    cots[0] = pack(cgot[...].reshape(rows, cols)).astype(BF16)
    other = (b, 1 - t)
    cot_swap = send(cots.at[0], cots.at[1], xs.at[0], xr.at[0], other)
    stages = [lambda p, low: p.send2(), lambda p, low: p.send3()]
    def mixes(i, j):
        return mix_ref[i, j]
    first = t == 0
    own = jnp.where(first, mixes(0, 0), mixes(1, 1))
    cross = jnp.where(first, mixes(0, 1), mixes(1, 0))
    back = jnp.where(first, mixes(1, 0), mixes(0, 1))
    def finish(piece, low):
        value, slope = gelu_pair(piece.result() + bias_ref[...])
        gates[0, low, :] = value.astype(BF16)
        d_gate = own * cots[0, low, :].astype(F32) + back * cots[1, low, :].astype(F32)
        g[place.at[0], place.at[1], place.at[2], low, :] = (d_gate * slope).astype(BF16)
        piece.gather1()
    def phase3(piece, low):
        piece.gather2()
    def phase4(piece, low):
        piece.gather3()
    swapped = False
    todo = [lambda p, low: p.send2(), lambda p, low: p.send3(), finish]
    steps = len(pieces) // 2
    for step in range(steps + 2):
        for k in range(3):
            c = step - k
            if 0 <= c < steps:
                if k == 2 and not swapped:
                    cot_swap.wait_recv()
                    swapped = True
                for piece, low in pieces[2 * c:2 * c + 2]:
                    todo[k](piece, low)
    gate_swap = send(gates.at[0], gates.at[1], xs.at[1], xr.at[1], other)
    for piece, low in pieces[:2]:
        piece.gather2()
    gate_swap.wait_recv()
    gate, cot, gate_other = gates[0].astype(F32), cots[0].astype(F32), gates[1].astype(F32)
    mine = g.at[place.at[0], place.at[1], place.at[2]]
    zero = jnp.zeros((1, cols), F32)
    total_rows = [jnp.sum(cot * gate, axis=0, keepdims=True), jnp.sum(cot * gate_other, axis=0, keepdims=True),
                  jnp.sum(mine[...].astype(F32), axis=0, keepdims=True)]
    wide[me] = jnp.concatenate(total_rows + [zero] * 5, axis=0)
    def sums_copy(k):
        d = lax.rem(me + k, total)
        return pltpu.make_async_remote_copy(
            src_ref=wide.at[me], dst_ref=wide.at[me], send_sem=ms.at[k], recv_sem=mr.at[k],
            device_id=(d // 2, d % 2), device_id_type=MESH_ID)
    stitched = (own * gate + cross * gate_other).astype(BF16)
    st[...] = jnp.dot(spread[...], stitched, preferred_element_type=F32).astype(BF16).reshape(st.shape)
    def stitched_copy(k):
        d = lax.rem(b + k, nb)
        return pltpu.make_async_remote_copy(
            src_ref=st.at[d], dst_ref=sgot.at[b], send_sem=ss.at[k], recv_sem=sr.at[k],
            device_id=(d, t), device_id_type=MESH_ID)
    lax.fori_loop(1, total, lambda k, _: (sums_copy(k).start(), 0)[1], 0)
    lax.fori_loop(1, nb, lambda k, _: (stitched_copy(k).start(), 0)[1], 0)
    sgot[b] = st[b]
    for c in range(1, steps):
        for piece, low in pieces[2 * c:2 * c + 2]:
            piece.gather2()
        for piece, low in pieces[2 * c - 2:2 * c]:
            piece.gather3()
    for piece, low in pieces[-2:]:
        piece.gather3()
    for piece, low in pieces:
        piece.arrive()
    acc[...] = jnp.zeros(acc.shape, F32)
    for k in range(nb):
        i = (k // (place.dims[1] * place.dims[2]), (k // place.dims[2]) % place.dims[1], k % place.dims[2])
        acc[...] += lax.dot_general(g[i], w[:, k * cols:(k + 1) * cols], (((1,), (1,)), ((), ())), preferred_element_type=F32)
    df = jnp.dot(spread[...], acc[...].astype(BF16), preferred_element_type=F32).astype(BF16)
    dsl[:, :, :per] = df.reshape(total, slots, per)
    def grad_copy(k):
        d = lax.rem(me + k, total)
        return pltpu.make_async_remote_copy(
            src_ref=dsl.at[d], dst_ref=dm_ref.at[t, b], send_sem=fs.at[k + total], recv_sem=fr.at[k + total],
            device_id=(d // 2, d % 2), device_id_type=MESH_ID)
    lax.fori_loop(1, total, lambda k, _: (grad_copy(k).start(), 0)[1], 0)
    dm_ref[t, b] = dsl[me]
    for k in range(nb):
        i = (k // (place.dims[1] * place.dims[2]), (k // place.dims[2]) % place.dims[1], k % place.dims[2])
        dh_ref[:, k * cols:(k + 1) * cols] = g[i]
    lax.fori_loop(1, nb, lambda k, _: (stitched_copy(k).wait_recv(), 0)[1], 0)
    for k in range(nb):
        out_ref[0, :, k * cols:(k + 1) * cols] = sgot[k]
    lax.fori_loop(1, total, lambda k, _: (sums_copy(k).wait_recv(), 0)[1], 0)
    for k in range(nb):
        for u in range(2):
            sums_ref[u, :, k * cols:(k + 1) * cols] = wide[2 * k + u]
    lax.fori_loop(1, total, lambda k, _: (grad_copy(k).wait_recv(), 0)[1], 0)
    for piece, _ in pieces:
        piece.close()
    cot_swap.wait_send()
    gate_swap.wait_send()
    def drain(k, _):
        feature_copy(k).wait_send()
        grad_copy(k).wait_send()
        sums_copy(k).wait_send()
        return 0
    lax.fori_loop(1, total, drain, 0)
    def drain2(k, _):
        cot_copy(k).wait_send()
        stitched_copy(k).wait_send()
        return 0
    lax.fori_loop(1, nb, drain2, 0)


def fc_layer(feat, cot, w, bias, mix, nb, per, parts=2):
    _, _, slots, padded = feat.shape
    fc = w.shape[1]
    cols = fc // nb
    total = 2 * nb
    rows = total * slots
    live = rows // 2
    d0, d1, d2 = torus(nb)
    size = live // (2 * parts)
    V = pl.BlockSpec(memory_space=pltpu.VMEM)
    vm = lambda *shape: pltpu.VMEM(shape, BF16)
    dma = lambda *shape: pltpu.SemaphoreType.DMA(shape)
    n = 2 * parts
    return pl.pallas_call(
        functools.partial(fc_kernel, parts, nb, per),
        out_shape=[jax.ShapeDtypeStruct((1, 2 * slots, fc), BF16), jax.ShapeDtypeStruct((live, per), BF16),
                   jax.ShapeDtypeStruct((live, fc), BF16), jax.ShapeDtypeStruct((2, nb, slots, padded), BF16),
                   jax.ShapeDtypeStruct((2, 8, fc), F32)],
        in_specs=[V, V, pl.BlockSpec(memory_space=pl.ANY), V, V], out_specs=[V] * 5,
        scratch_shapes=[
            vm(per, fc), vm(total, slots, padded), vm(nb, 2 * slots, cols), vm(nb, 2 * slots, cols), vm(rows, live),
            vm(d0, d1, d2, live, cols), vm(n, d1 - 1, d0, d1, size, cols), vm(n, d0, d1, size, cols),
            vm(n, d1 - 1, d0, size, cols), vm(n, d0, size, cols), vm(n, d0 - 1, size, cols), vm(d0, d1, d2, live, cols),
            vm(16, 128), vm(2, live, cols), vm(2, live, cols), pltpu.VMEM((total, 8, cols), F32),
            vm(nb, 2 * slots, cols), vm(nb, 2 * slots, cols), vm(total, slots, padded), pltpu.VMEM((live, per), F32),
            pltpu.SemaphoreType.DMA, dma(2 * total), dma(2 * total), dma(nb), dma(nb), dma(2), dma(2), dma(nb), dma(nb),
            dma(total), dma(total), dma(n, hops(nb)), dma(n, hops(nb))],
        compiler_params=pltpu.CompilerParams(collective_id=1, has_side_effects=True, vmem_limit_bytes=60 * 2**20),
    )(feat, cot, w, bias, mix)

def conv_bwd_kernel(dm_ref, pooled_ref, slope_ref, p_ref, w_ref, mix_ref, dx_ref, dw_ref, small_ref,
                    fbuf, z, dpad, d2, dt, stage):
    towers, nb, slots, _ = dm_ref.shape
    per = fbuf.shape[2] // nb
    side = slope_ref.shape[0]
    cout = w_ref.shape[2]
    cin = p_ref.shape[3]
    pool = (side - 3) // 2 + 1
    wide = towers * cout
    cells = side * side
    for t in range(towers):
        for b in range(nb):
            fbuf[t, :, b * per:(b + 1) * per] = dm_ref[t, b, :, :per]
    z[0] = jnp.zeros(z.shape[1:], F32)
    z[pool + 1] = jnp.zeros(z.shape[1:], F32)
    acc = [[jnp.zeros((slots, cout), F32)] * 2 for _ in range(2)]
    for i in range(pool):
        z[i + 1, 0] = jnp.zeros(z.shape[2:], F32)
        z[i + 1, pool + 1] = jnp.zeros(z.shape[2:], F32)
        for j in range(pool):
            q = i * pool + j
            dm = [fbuf[t, :, q * cout:(q + 1) * cout].astype(F32) for t in range(towers)]
            for u in range(towers):
                pu = pooled_ref[q, :, u * cout:(u + 1) * cout]
                for t in range(towers):
                    acc[t][u] = acc[t][u] + dm[t] * pu
                z[i + 1, j + 1, :, u * cout:(u + 1) * cout] = (mix_ref[0, u][None] * dm[0] + mix_ref[1, u][None] * dm[1]) * (1.0 / 9.0)
    dpad[0] = jnp.zeros(dpad.shape[1:], BF16)
    dpad[side + 1] = jnp.zeros(dpad.shape[1:], BF16)
    d2[cells:] = jnp.zeros((d2.shape[0] - cells, slots, wide), BF16)
    def drow(y, src):
        dpad[y + 1, 0] = jnp.zeros((slots, wide), BF16)
        dpad[y + 1, side + 1] = jnp.zeros((slots, wide), BF16)
        for x in range(side):
            j = x // 2
            v = src(j + 1) if x % 2 else src(j) + src(j + 1)
            d = (v * slope_ref[y, x].astype(F32)).astype(BF16)
            dpad[y + 1, x + 1] = d
            d2[y * side + x] = d
    def pair(i, _):
        drow(2 * i, lambda j: z[i, j] + z[i + 1, j])
        drow(2 * i + 1, lambda j: z[i + 1, j])
        return 0
    lax.fori_loop(0, pool, pair, 0)
    drow(side - 1, lambda j: z[pool, j] + z[pool + 1, j])
    step = 256 // slots
    def flip(k, _):
        dt[:, pl.ds(pl.multiple_of(k * 256, 256), 256)] = d2[pl.ds(k * step, step)].reshape(256, wide).T
        return 0
    lax.fori_loop(0, d2.shape[0] // step, flip, 0)
    tail = (d2.shape[0] - cells) * slots
    for a in range(3):
        win = jnp.concatenate([p_ref[a:a + side, b:b + side].reshape(cells * slots, cin) for b in range(3)], axis=1)
        win = jnp.concatenate([win, jnp.zeros((tail, 3 * cin), BF16)], axis=0)
        dw_ref[a] = jnp.dot(dt[...], win, preferred_element_type=F32)
    ones = jnp.ones((d2.shape[0] * slots, 128), BF16)
    small_ref[:, 0:128] = jnp.dot(dt[...], ones, preferred_element_type=F32)
    rows = jnp.concatenate([jnp.concatenate([jnp.sum(acc[t][u], axis=0, keepdims=True) for u in range(2)], axis=1) for t in range(2)], axis=0)
    small_ref[:, 128:256] = jnp.concatenate([rows, jnp.zeros((126, wide), F32)], axis=0).T
    pitch = 16
    def xrow(y):
        lhs = jnp.concatenate([dpad[y + 2 - a, 2 - b:2 - b + side, :, t * cout:(t + 1) * cout].reshape(side * slots, cout)
                               for t in range(towers) for a in range(3) for b in range(3)], axis=1)
        rhs = jnp.concatenate([w_ref[t, (a * 3 + b) * cin:(a * 3 + b + 1) * cin, :]
                               for t in range(towers) for a in range(3) for b in range(3)], axis=1)
        out = lax.dot_general(lhs, rhs, (((1,), (1,)), ((), ())), preferred_element_type=F32).reshape(side, slots, cin)
        for x in range(side):
            for l in range(cin // 128):
                stage[l, pl.ds(y * pitch + x, slots, stride=side * pitch), :] = out[x, :, l * 128:(l + 1) * 128]
    lax.fori_loop(0, side, lambda y, _: (xrow(y), 0)[1], 0)
    def put(k, _):
        r = k // side
        i = k % side
        dx_ref[r, i] = jnp.concatenate([stage[l, pl.ds(pl.multiple_of(k * pitch, pitch), side), :] for l in range(cin // 128)], axis=1).astype(BF16)
        return 0
    lax.fori_loop(0, slots * side, put, 0, unroll=4)

def conv_bwd(dm, pooled, slope, p, w, mix, per):
    towers, nb, slots, _ = dm.shape
    side = slope.shape[0]
    cin = p.shape[3]
    cout = w.shape[4]
    pool = (side - 3) // 2 + 1
    wide = towers * cout
    V = pl.BlockSpec(memory_space=pltpu.VMEM)
    cells = -(-side * side * slots // 256) * 256 // slots
    return pl.pallas_call(
        conv_bwd_kernel,
        out_shape=[jax.ShapeDtypeStruct((slots, side, side, cin), BF16),
                   jax.ShapeDtypeStruct((3, wide, 3 * cin), F32),
                   jax.ShapeDtypeStruct((wide, 256), F32)],
        in_specs=[V] * 6, out_specs=[V] * 3,
        scratch_shapes=[pltpu.VMEM((towers, slots, nb * per), BF16),
                        pltpu.VMEM((pool + 2, pool + 2, slots, wide), F32),
                        pltpu.VMEM((side + 2, side + 2, slots, wide), BF16),
                        pltpu.VMEM((cells, slots, wide), BF16),
                        pltpu.VMEM((wide, cells * slots), BF16),
                        pltpu.VMEM((cin // 128, slots * side * 16, 128), F32)],
        compiler_params=pltpu.CompilerParams(vmem_limit_bytes=62 * 2**20),
    )(dm, pooled, slope, p, w.reshape(towers, 9 * cin, cout), mix)


def swap(block):
    return lax.ppermute(block, "tower", [(0, 1), (1, 0)])


def plain_shards(crop_pixels, live_rows, conv_weight, conv_bias, stitch_conv, fc_weight, fc_bias, stitch_fc, cotangent):
    slots = crop_pixels.shape[0]
    nb = lax.axis_size("batch")
    b, t = lax.axis_index("batch"), lax.axis_index("tower")
    rows = 2 * slots * nb
    live = rows // 2
    fc = fc_weight.shape[2]
    per = fc_weight.shape[1]
    cols = fc // nb
    w = fc_weight[0]
    feat, pooled, slope, padded = conv_fwd(live_rows, crop_pixels, conv_weight, conv_bias, stitch_conv, nb)
    both = ("batch", "tower")
    counts = lax.all_gather(live_rows, both, axis=0, tiled=True)
    got = lax.all_to_all(feat[..., :per].transpose(1, 0, 2, 3).reshape(2 * nb, slots, per), both, 0, 0).reshape(rows, per)
    slot = jnp.arange(rows, dtype=jnp.int32)
    start = jnp.cumsum(counts) - counts
    place = jnp.where(slot % slots < counts[slot // slots], start[slot // slots] + slot % slots, -1)
    spread = (place[:, None] == jnp.arange(live, dtype=jnp.int32)[None]).astype(BF16)
    compact = lambda x: lax.dot_general(spread, x, (((0,), (0,)), ((), ())), preferred_element_type=F32).astype(BF16)
    expand = lambda x: jnp.dot(spread, x, preferred_element_type=F32).astype(BF16)
    f = compact(got)
    part = jnp.dot(f, w, preferred_element_type=F32)
    hidden = lax.psum_scatter(part, "batch", scatter_dimension=1, tiled=True)
    hidden = hidden + lax.dynamic_slice_in_dim(fc_bias[0], b * cols, cols)[None]
    value, slope_fc = gelu_pair(hidden)
    gate = value.astype(BF16)
    cot = compact(lax.all_to_all(cotangent[0].reshape(2 * slots, nb, cols).transpose(1, 0, 2), "batch", 0, 0).reshape(rows, cols))
    gate_other, cot_other = swap(gate).astype(F32), swap(cot).astype(F32)
    gate_own, cot_own = gate.astype(F32), cot.astype(F32)
    mix = lax.dynamic_slice_in_dim(stitch_fc, b * cols, cols, axis=2)
    own = jnp.where(t == 0, mix[0, 0], mix[1, 1])
    cross = jnp.where(t == 0, mix[0, 1], mix[1, 0])
    back = jnp.where(t == 0, mix[1, 0], mix[0, 1])
    stitched = (own[None] * gate_own + cross[None] * gate_other).astype(BF16)
    stitched = lax.all_to_all(expand(stitched).reshape(nb, 2 * slots, cols), "batch", 0, 0)
    stitched = stitched.transpose(1, 0, 2).reshape(1, 2 * slots, fc)
    d_own = jnp.sum(cot_own * gate_own, axis=0)
    d_cross = jnp.sum(cot_own * gate_other, axis=0)
    dh = ((own[None] * cot_own + back[None] * cot_other) * slope_fc).astype(BF16)
    sums = jnp.stack([d_own, d_cross, jnp.sum(dh.astype(F32), axis=0)])
    sums = lax.all_gather(sums, both, axis=0).reshape(nb, 2, 3, cols).transpose(1, 2, 0, 3).reshape(2, 3, fc)
    d_stitch_fc = jnp.stack([sums[0, :2], sums[1, 1::-1]])
    d_fc_bias = sums[:, 2]
    dh = lax.all_gather(dh, "batch", axis=1, tiled=True)
    d_fc_weight = lax.dot_general(f, dh, (((0,), (0,)), ((), ())), preferred_element_type=F32)[None]
    df = lax.dot_general(dh, w, (((1,), (1,)), ((), ())), preferred_element_type=F32).astype(BF16)
    dm = lax.all_to_all(expand(df).reshape(2 * nb, slots, per), both, 0, 0)
    dm = dm.reshape(nb, 2, slots, per).transpose(1, 0, 2, 3)
    dx, dw, small = conv_bwd(dm, pooled, slope, padded, conv_weight, stitch_conv, per)
    dw = lax.psum(dw, both)
    cin, cout = conv_weight.shape[3:]
    dw = dw.reshape(3, 2, cout, 3, cin).transpose(1, 0, 3, 4, 2)
    small = lax.psum(small, both)
    d_conv_bias = small[:, 0].reshape(2, cout)
    d_stitch_conv = small[:, 128:130].T.reshape(2, 2, cout)
    return stitched, dx, dw, d_conv_bias, d_stitch_conv, d_fc_weight, d_fc_bias, d_stitch_fc


def shards(crop_pixels, live_rows, conv_weight, conv_bias, stitch_conv, fc_weight, fc_bias, stitch_fc, cotangent):
    slots = crop_pixels.shape[0]
    nb = lax.axis_size("batch")
    b = lax.axis_index("batch")
    fc = fc_weight.shape[2]
    per = fc_weight.shape[1]
    cols = fc // nb
    both = ("batch", "tower")
    feat, pooled, slope, padded = conv_fwd(live_rows, crop_pixels, conv_weight, conv_bias, stitch_conv, nb)
    bias = lax.dynamic_slice_in_dim(fc_bias, b * cols, cols, axis=1)
    mix = lax.dynamic_slice_in_dim(stitch_fc, b * cols, cols, axis=2).reshape(2, 2, 1, cols)
    stitched, f, dh, dm, sums = fc_layer(feat, cotangent[0], fc_weight[0], bias, mix, nb, per)
    d_fc_weight = lax.dot_general(f, dh, (((0,), (0,)), ((), ())), preferred_element_type=F32)[None]
    d_stitch_fc = jnp.stack([sums[0, :2], sums[1, 1::-1]])
    d_fc_bias = sums[:, 2]
    dx, dw, small = conv_bwd(dm, pooled, slope, padded, conv_weight, stitch_conv, per)
    dw = lax.psum(dw, both)
    cin, cout = conv_weight.shape[3:]
    dw = dw.reshape(3, 2, cout, 3, cin).transpose(1, 0, 3, 4, 2)
    small = lax.psum(small, both)
    d_conv_bias = small[:, 0].reshape(2, cout)
    d_stitch_conv = small[:, 128:130].T.reshape(2, 2, cout)
    return stitched, dx, dw, d_conv_bias, d_stitch_conv, d_fc_weight, d_fc_bias, d_stitch_fc


def solution(mesh):
    in_specs = (
        P(("batch", "tower"), None, None, None), P(("batch", "tower")), P(), P(), P(),
        P("tower", "batch", None), P("tower", None), P(), P("tower", "batch", None),
    )
    out_specs = (
        P("tower", "batch", None), P(("batch", "tower"), None, None, None), P(), P(), P(),
        P("tower", "batch", None), P(), P(),
    )
    body = shards if mesh.shape["batch"] == 16 else plain_shards
    return jax.shard_map(body, mesh=mesh, in_specs=in_specs, out_specs=out_specs, check_vma=False)
```

```python
import functools, math
import jax, jax.numpy as jnp
from jax import lax
from jax.experimental import pallas as pl
from jax.experimental.pallas import tpu as pltpu
from jax.sharding import PartitionSpec as P
F32, BF16 = jnp.float32, jnp.bfloat16
CG = math.sqrt(2.0 / math.pi)

def gelu_pair(v):
    sq = v * v
    t = jnp.tanh(v * (CG + (CG * 0.044715) * sq))
    half = 0.5 + 0.5 * t
    value = v * half
    slope = half + value * (1.0 - half) * (2.0 * CG + (6.0 * CG * 0.044715) * sq)
    return value, slope

def conv_fwd_kernel(rows_per, live_ref, x_ref, w_ref, b_ref, mix_ref, feat_ref, pooled_ref, slope_ref, p_ref, stage, act, fbuf):
    slots, side, _, cin = x_ref.shape
    towers, _, cout = w_ref.shape
    pool = (side - 3) // 2 + 1
    pitch = 16
    lanes = cin // 128
    p_ref[0] = jnp.zeros(p_ref.shape[1:], BF16)
    p_ref[side + 1] = jnp.zeros(p_ref.shape[1:], BF16)
    def put(k, _):
        r = k // side
        i = k % side
        v = x_ref[r, i].astype(F32)
        for l in range(lanes):
            stage[l, pl.ds(pl.multiple_of(k * pitch, pitch), side), :] = v[:, l * 128:(l + 1) * 128]
        return 0
    lax.fori_loop(0, slots * side, put, 0, unroll=4)
    def take(i, _):
        p_ref[i + 1, 0] = jnp.zeros((slots, cin), BF16)
        p_ref[i + 1, side + 1] = jnp.zeros((slots, cin), BF16)
        for j in range(side):
            for l in range(lanes):
                v = stage[l, pl.ds(i * pitch + j, slots, stride=side * pitch), :]
                p_ref[i + 1, j + 1, :, l * 128:(l + 1) * 128] = v.astype(BF16)
        return 0
    lax.fori_loop(0, side, take, 0)
    rows = rows_per * side * slots
    def row(y):
        window = jnp.concatenate(
            [p_ref[pl.ds(y + a, rows_per), b:b + side].reshape(rows, cin) for a in range(3) for b in range(3)], axis=1)
        for t in range(towers):
            pre = jnp.dot(window, w_ref[t], preferred_element_type=F32) + b_ref[t][None]
            value, slope = gelu_pair(pre)
            act[pl.ds(y, rows_per), :, :, t * cout:(t + 1) * cout] = value.reshape(rows_per, side, slots, cout)
            slope_ref[pl.ds(y, rows_per), :, :, t * cout:(t + 1) * cout] = slope.astype(BF16).reshape(rows_per, side, slots, cout)
    lax.fori_loop(0, side // rows_per, lambda k, _: (row(k * rows_per), 0)[1], 0)
    for i in range(pool):
        s3 = act[2 * i] + act[2 * i + 1] + act[2 * i + 2]
        for j in range(pool):
            p9 = (s3[2 * j] + s3[2 * j + 1] + s3[2 * j + 2]) * (1.0 / 9.0)
            pooled_ref[i * pool + j] = p9
            for t in range(towers):
                m = mix_ref[t, 0][None] * p9[:, :cout] + mix_ref[t, 1][None] * p9[:, cout:]
                fbuf[t, :, (i * pool + j) * cout:(i * pool + j + 1) * cout] = m.astype(BF16)
    nb = feat_ref.shape[1]
    per = fbuf.shape[2] // nb
    flags = (lax.broadcasted_iota(jnp.int32, (slots, feat_ref.shape[3] - per), 0) < live_ref[0]).astype(F32).astype(BF16)
    for t in range(towers):
        for b in range(nb):
            feat_ref[t, b, :, :per] = fbuf[t, :, b * per:(b + 1) * per]
            feat_ref[t, b, :, per:] = flags

def conv_fwd(live, x, w, bias, mix, nb, rows_per=1):
    slots, side, _, cin = x.shape
    towers, _, _, _, cout = w.shape
    pool = (side - 3) // 2 + 1
    nf = pool * pool * cout
    V = pl.BlockSpec(memory_space=pltpu.VMEM)
    return pl.pallas_call(
        functools.partial(conv_fwd_kernel, rows_per),
        out_shape=[jax.ShapeDtypeStruct((towers, nb, slots, nf // nb // 128 * 128 + 128), BF16),
                   jax.ShapeDtypeStruct((pool * pool, slots, towers * cout), F32),
                   jax.ShapeDtypeStruct((side, side, slots, towers * cout), BF16),
                   jax.ShapeDtypeStruct((side + 2, side + 2, slots, cin), BF16)],
        in_specs=[pl.BlockSpec(memory_space=pltpu.SMEM)] + [V] * 4, out_specs=[V] * 4,
        scratch_shapes=[pltpu.VMEM((cin // 128, slots * side * 16, 128), F32),
                        pltpu.VMEM((side, side, slots, towers * cout), F32),
                        pltpu.VMEM((towers, slots, nf), BF16)],
        compiler_params=pltpu.CompilerParams(vmem_limit_bytes=60 * 2**20),
    )(live, x, w.reshape(towers, 9 * cin, cout), bias, mix)


MESH_ID = pl.DeviceIdType.MESH


def torus(nb):
    return {16: (4, 2, 2), 64: (4, 4, 4)}.get(nb, (nb, 1, 1))


class Place:
    def __init__(self, nb):
        self.dims = torus(nb)
        self.b, self.t = lax.axis_index("batch"), lax.axis_index("tower")
        d0, d1, d2 = self.dims
        self.at = (self.b // (d1 * d2), (self.b // d2) % d1, self.b % d2)

    def peer(self, dim, k):
        c = list(self.at)
        c[dim] = k
        return ((c[0] * self.dims[1] + c[1]) * self.dims[2] + c[2], self.t)


def send(src, dst, ssem, rsem, device):
    copy = pltpu.make_async_remote_copy(src_ref=src, dst_ref=dst, send_sem=ssem, recv_sem=rsem, device_id=device, device_id_type=MESH_ID)
    copy.start()
    return copy


def greet(nb, me):
    bar = pltpu.get_barrier_semaphore()
    total = 2 * nb
    def hail(k, _):
        d = lax.rem(me + k, total)
        pl.semaphore_signal(bar, inc=1, device_id=(d // 2, d % 2), device_id_type=MESH_ID)
        return 0
    lax.fori_loop(1, total, hail, 0)
    pl.semaphore_wait(bar, total - 1)


class Sum:
    def __init__(self, place, p, s, r1, t1, r2, t2, r3, g, ssem, rsem):
        self.place, self.p, self.q = place, p, 3 - p
        self.s, self.r1, self.t1, self.r2, self.t2, self.r3, self.g = s, r1, t1, r2, t2, r3, g
        self.ssem, self.rsem = ssem, rsem
        self.sent = []
        self.used = 0

    def pick(self, ref, k):
        return ref.at[:, :, k] if self.p == 2 else ref.at[:, k]

    def post(self, dim, src_of, dst_of):
        n = self.place.dims[dim]
        self.flight = []
        for j in range(1, n):
            k = lax.rem(self.place.at[dim] + j, n)
            i = self.used
            self.used += 1
            self.flight.append(send(src_of(k), dst_of(j - 1), self.ssem.at[i], self.rsem.at[i], self.place.peer(dim, k)))
        self.sent += self.flight

    def arrive(self):
        for c in self.flight:
            c.wait_recv()

    def add(self, mine, got, n):
        v = mine.astype(F32)
        for j in range(n):
            v = v + got[j].astype(F32)
        return v

    def send1(self):
        self.post(self.p, lambda k: self.pick(self.s, k), lambda j: self.r1.at[j])

    def send2(self):
        self.arrive()
        n = self.place.dims[self.p]
        self.t1[...] = self.add(self.pick(self.s, self.place.at[self.p])[...], self.r1, n - 1).astype(BF16)
        self.post(self.q, lambda k: self.t1.at[:, k], lambda j: self.r2.at[j])

    def send3(self):
        self.arrive()
        n = self.place.dims[self.q]
        self.t2[...] = self.add(self.t1[:, self.place.at[self.q]], self.r2, n - 1).astype(BF16)
        self.post(0, lambda k: self.t2.at[k], lambda j: self.r3.at[j])

    def result(self):
        self.arrive()
        return self.add(self.t2[self.place.at[0]], self.r3, self.place.dims[0] - 1)

    def gather1(self):
        mine = self.g.at[self.place.at[0], self.place.at[1], self.place.at[2]]
        self.post(0, lambda k: mine, lambda j: mine)

    def gather2(self):
        self.arrive()
        mine = self.g.at[:, self.place.at[1], self.place.at[2]]
        self.post(self.q, lambda k: mine, lambda j: mine)

    def gather3(self):
        self.arrive()
        mine = self.pick(self.g, self.place.at[self.p])
        self.post(self.p, lambda k: mine, lambda j: mine)

    def close(self):
        for c in self.sent:
            c.wait_send()


def hops(nb):
    return 2 * sum(d - 1 for d in torus(nb))


def fc_kernel(parts, nb, per, feat_ref, cot_ref, w_hbm, bias_ref, mix_ref,
              out_ref, f_ref, g, dm_ref, sums_ref,
              w, fin, cin, cgot, spread, s, r1, t1, r2, t2, r3, gates, cots, wide, st, sgot, dsl, acc,
              wsem, fs, fr, cs, cr, xs, xr, ss, sr, ms, mr, gs, gr):
    place = Place(nb)
    b, t = place.b, place.t
    me = b * 2 + t
    total = 2 * nb
    slots = feat_ref.shape[2]
    rows = total * slots
    live = rows // 2
    cols = cin.shape[2]
    pair = 2 * slots
    load = pltpu.make_async_copy(w_hbm, w, wsem)
    load.start()
    greet(nb, me)
    def feature_copy(k):
        d = lax.rem(me + k, total)
        return pltpu.make_async_remote_copy(
            src_ref=feat_ref.at[d % 2, d // 2], dst_ref=fin.at[me], send_sem=fs.at[k], recv_sem=fr.at[k],
            device_id=(d // 2, d % 2), device_id_type=MESH_ID)
    lax.fori_loop(1, total, lambda k, _: (feature_copy(k).start(), 0)[1], 0)
    fin[me] = feat_ref[t, b]
    for k in range(nb):
        cin[k] = cot_ref[:, k * cols:(k + 1) * cols]
    def cot_copy(k):
        d = lax.rem(b + k, nb)
        return pltpu.make_async_remote_copy(
            src_ref=cin.at[d], dst_ref=cgot.at[b], send_sem=cs.at[k], recv_sem=cr.at[k],
            device_id=(d, t), device_id_type=MESH_ID)
    lax.fori_loop(1, nb, lambda k, _: (cot_copy(k).start(), 0)[1], 0)
    cgot[b] = cin[b]
    lax.fori_loop(1, total, lambda k, _: (feature_copy(k).wait_recv(), 0)[1], 0)
    got = fin[...].reshape(rows, fin.shape[2])
    flag = got[:, per:per + 1]
    lanes = jnp.broadcast_to(flag, (rows, 128))
    lower = (lax.broadcasted_iota(jnp.int32, (rows, rows), 1) < lax.broadcasted_iota(jnp.int32, (rows, rows), 0)).astype(BF16)
    index = jnp.dot(lower, lanes, preferred_element_type=F32)[:, :1].astype(jnp.int32)
    hit = (index == lax.broadcasted_iota(jnp.int32, (rows, live), 1)) & (flag.astype(F32) > 0.5)
    spread[...] = hit.astype(F32).astype(BF16)
    pack = lambda x: lax.dot_general(spread[...], x, (((0,), (0,)), ((), ())), preferred_element_type=F32)
    f_ref[...] = pack(got[:, :per]).astype(BF16)
    load.wait()
    for k in range(nb):
        i = (k // (place.dims[1] * place.dims[2]), (k // place.dims[2]) % place.dims[1], k % place.dims[2])
        s[i] = jnp.dot(f_ref[...], w[:, k * cols:(k + 1) * cols], preferred_element_type=F32).astype(BF16)
    size = live // (2 * parts)
    pieces = []
    for n in range(2 * parts):
        half = n % 2
        low = pl.ds(((n // 2) + half * parts) * size, size)
        pieces.append((Sum(place, 2 - half, s.at[:, :, :, low], r1.at[n], t1.at[n], r2.at[n], t2.at[n], r3.at[n],
                           g.at[:, :, :, low], gs.at[n], gr.at[n]), low))
    for piece, _ in pieces:
        piece.send1()
    lax.fori_loop(1, nb, lambda k, _: (cot_copy(k).wait_recv(), 0)[1], 0)
    cots[0] = pack(cgot[...].reshape(rows, cols)).astype(BF16)
    other = (b, 1 - t)
    cot_swap = send(cots.at[0], cots.at[1], xs.at[0], xr.at[0], other)
    stages = [lambda p, low: p.send2(), lambda p, low: p.send3()]
    def mixes(i, j):
        return mix_ref[i, j]
    first = t == 0
    own = jnp.where(first, mixes(0, 0), mixes(1, 1))
    cross = jnp.where(first, mixes(0, 1), mixes(1, 0))
    back = jnp.where(first, mixes(1, 0), mixes(0, 1))
    def finish(piece, low):
        value, slope = gelu_pair(piece.result() + bias_ref[...])
        gates[0, low, :] = value.astype(BF16)
        d_gate = own * cots[0, low, :].astype(F32) + back * cots[1, low, :].astype(F32)
        g[place.at[0], place.at[1], place.at[2], low, :] = (d_gate * slope).astype(BF16)
        piece.gather1()
    def phase3(piece, low):
        piece.gather2()
    def phase4(piece, low):
        piece.gather3()
    swapped = False
    todo = [lambda p, low: p.send2(), lambda p, low: p.send3(), finish]
    steps = len(pieces) // 2
    for step in range(steps + 2):
        for k in range(3):
            c = step - k
            if 0 <= c < steps:
                if k == 2 and not swapped:
                    cot_swap.wait_recv()
                    swapped = True
                for piece, low in pieces[2 * c:2 * c + 2]:
                    todo[k](piece, low)
    gate_swap = send(gates.at[0], gates.at[1], xs.at[1], xr.at[1], other)
    for piece, low in pieces[:2]:
        piece.gather2()
    gate_swap.wait_recv()
    gate, cot, gate_other = gates[0].astype(F32), cots[0].astype(F32), gates[1].astype(F32)
    mine = g.at[place.at[0], place.at[1], place.at[2]]
    zero = jnp.zeros((1, cols), F32)
    total_rows = [jnp.sum(cot * gate, axis=0, keepdims=True), jnp.sum(cot * gate_other, axis=0, keepdims=True),
                  jnp.sum(mine[...].astype(F32), axis=0, keepdims=True)]
    wide[me] = jnp.concatenate(total_rows + [zero] * 5, axis=0)
    def sums_copy(k):
        d = lax.rem(me + k, total)
        return pltpu.make_async_remote_copy(
            src_ref=wide.at[me], dst_ref=wide.at[me], send_sem=ms.at[k], recv_sem=mr.at[k],
            device_id=(d // 2, d % 2), device_id_type=MESH_ID)
    stitched = (own * gate + cross * gate_other).astype(BF16)
    st[...] = jnp.dot(spread[...], stitched, preferred_element_type=F32).astype(BF16).reshape(st.shape)
    def stitched_copy(k):
        d = lax.rem(b + k, nb)
        return pltpu.make_async_remote_copy(
            src_ref=st.at[d], dst_ref=sgot.at[b], send_sem=ss.at[k], recv_sem=sr.at[k],
            device_id=(d, t), device_id_type=MESH_ID)
    lax.fori_loop(1, total, lambda k, _: (sums_copy(k).start(), 0)[1], 0)
    lax.fori_loop(1, nb, lambda k, _: (stitched_copy(k).start(), 0)[1], 0)
    sgot[b] = st[b]
    for c in range(1, steps):
        for piece, low in pieces[2 * c:2 * c + 2]:
            piece.gather2()
        for piece, low in pieces[2 * c - 2:2 * c]:
            piece.gather3()
    for piece, low in pieces[-2:]:
        piece.gather3()
    for piece, low in pieces:
        piece.arrive()
    acc[...] = jnp.zeros(acc.shape, F32)
    for k in range(nb):
        i = (k // (place.dims[1] * place.dims[2]), (k // place.dims[2]) % place.dims[1], k % place.dims[2])
        acc[...] += lax.dot_general(g[i], w[:, k * cols:(k + 1) * cols], (((1,), (1,)), ((), ())), preferred_element_type=F32)
    df = jnp.dot(spread[...], acc[...].astype(BF16), preferred_element_type=F32).astype(BF16)
    dsl[:, :, :per] = df.reshape(total, slots, per)
    def grad_copy(k):
        d = lax.rem(me + k, total)
        return pltpu.make_async_remote_copy(
            src_ref=dsl.at[d], dst_ref=dm_ref.at[t, b], send_sem=fs.at[k + total], recv_sem=fr.at[k + total],
            device_id=(d // 2, d % 2), device_id_type=MESH_ID)
    lax.fori_loop(1, total, lambda k, _: (grad_copy(k).start(), 0)[1], 0)
    dm_ref[t, b] = dsl[me]
    lax.fori_loop(1, nb, lambda k, _: (stitched_copy(k).wait_recv(), 0)[1], 0)
    for k in range(nb):
        out_ref[0, :, k * cols:(k + 1) * cols] = sgot[k]
    lax.fori_loop(1, total, lambda k, _: (sums_copy(k).wait_recv(), 0)[1], 0)
    for k in range(nb):
        for u in range(2):
            sums_ref[u, :, k * cols:(k + 1) * cols] = wide[2 * k + u]
    lax.fori_loop(1, total, lambda k, _: (grad_copy(k).wait_recv(), 0)[1], 0)
    for piece, _ in pieces:
        piece.close()
    cot_swap.wait_send()
    gate_swap.wait_send()
    def drain(k, _):
        feature_copy(k).wait_send()
        grad_copy(k).wait_send()
        sums_copy(k).wait_send()
        return 0
    lax.fori_loop(1, total, drain, 0)
    def drain2(k, _):
        cot_copy(k).wait_send()
        stitched_copy(k).wait_send()
        return 0
    lax.fori_loop(1, nb, drain2, 0)


def fc_layer(feat, cot, w, bias, mix, nb, per, parts=2):
    _, _, slots, padded = feat.shape
    fc = w.shape[1]
    cols = fc // nb
    total = 2 * nb
    rows = total * slots
    live = rows // 2
    d0, d1, d2 = torus(nb)
    size = live // (2 * parts)
    V = pl.BlockSpec(memory_space=pltpu.VMEM)
    vm = lambda *shape: pltpu.VMEM(shape, BF16)
    dma = lambda *shape: pltpu.SemaphoreType.DMA(shape)
    n = 2 * parts
    return pl.pallas_call(
        functools.partial(fc_kernel, parts, nb, per),
        out_shape=[jax.ShapeDtypeStruct((1, 2 * slots, fc), BF16), jax.ShapeDtypeStruct((live, per), BF16),
                   jax.ShapeDtypeStruct((d0, d1, d2, live, cols), BF16), jax.ShapeDtypeStruct((2, nb, slots, padded), BF16),
                   jax.ShapeDtypeStruct((2, 8, fc), F32)],
        in_specs=[V, V, pl.BlockSpec(memory_space=pl.ANY), V, V], out_specs=[V] * 5,
        scratch_shapes=[
            vm(per, fc), vm(total, slots, padded), vm(nb, 2 * slots, cols), vm(nb, 2 * slots, cols), vm(rows, live),
            vm(d0, d1, d2, live, cols), vm(n, d1 - 1, d0, d1, size, cols), vm(n, d0, d1, size, cols),
            vm(n, d1 - 1, d0, size, cols), vm(n, d0, size, cols), vm(n, d0 - 1, size, cols),
            vm(2, live, cols), vm(2, live, cols), pltpu.VMEM((total, 8, cols), F32),
            vm(nb, 2 * slots, cols), vm(nb, 2 * slots, cols), vm(total, slots, padded), pltpu.VMEM((live, per), F32),
            pltpu.SemaphoreType.DMA, dma(2 * total), dma(2 * total), dma(nb), dma(nb), dma(2), dma(2), dma(nb), dma(nb),
            dma(total), dma(total), dma(n, hops(nb)), dma(n, hops(nb))],
        compiler_params=pltpu.CompilerParams(collective_id=1, has_side_effects=True, vmem_limit_bytes=60 * 2**20),
    )(feat, cot, w, bias, mix)

def bwd_kernel(per, dm_ref, pooled_ref, slope_ref, p_ref, w_ref, mix_ref, dx_ref, out_ref,
               fbuf, z, dpad, d2, dt, stage, keep, give, take, s, r1, t1, r2, t2, r3, cs, cr, gs, gr, stage_sums):
    towers, nb, slots, _ = dm_ref.shape
    place = Place(nb)
    b, t = place.b, place.t
    me = b * 2 + t
    side = slope_ref.shape[0]
    cout = w_ref.shape[2]
    cin = p_ref.shape[3]
    pool = (side - 3) // 2 + 1
    wide = towers * cout
    cells = side * side
    chunks = out_ref.shape[1]
    span = out_ref.shape[-1]
    greet(nb, me)
    for u in range(towers):
        for k in range(nb):
            fbuf[u, :, k * per:(k + 1) * per] = dm_ref[u, k, :, :per]
    z[0] = jnp.zeros(z.shape[1:], F32)
    z[pool + 1] = jnp.zeros(z.shape[1:], F32)
    acc = [[jnp.zeros((slots, cout), F32)] * 2 for _ in range(2)]
    for i in range(pool):
        z[i + 1, 0] = jnp.zeros(z.shape[2:], F32)
        z[i + 1, pool + 1] = jnp.zeros(z.shape[2:], F32)
        for j in range(pool):
            q = i * pool + j
            dm = [fbuf[u, :, q * cout:(q + 1) * cout].astype(F32) for u in range(towers)]
            for u in range(towers):
                pu = pooled_ref[q, :, u * cout:(u + 1) * cout]
                for v in range(towers):
                    acc[v][u] = acc[v][u] + dm[v] * pu
                z[i + 1, j + 1, :, u * cout:(u + 1) * cout] = (mix_ref[0, u][None] * dm[0] + mix_ref[1, u][None] * dm[1]) * (1.0 / 9.0)
    sums = [jnp.concatenate([jnp.sum(acc[v][u], axis=0, keepdims=True) for u in range(2)], axis=1) for v in range(2)]
    sums = jnp.concatenate([jnp.zeros((1, wide), F32)] + sums + [jnp.zeros((125, wide), F32)], axis=0).T
    dpad[0] = jnp.zeros(dpad.shape[1:], BF16)
    dpad[side + 1] = jnp.zeros(dpad.shape[1:], BF16)
    d2[cells:] = jnp.zeros((d2.shape[0] - cells, slots, wide), BF16)
    def drow(y, src):
        dpad[y + 1, 0] = jnp.zeros((slots, wide), BF16)
        dpad[y + 1, side + 1] = jnp.zeros((slots, wide), BF16)
        for x in range(side):
            j = x // 2
            v = src(j + 1) if x % 2 else src(j) + src(j + 1)
            d = (v * slope_ref[y, x].astype(F32)).astype(BF16)
            dpad[y + 1, x + 1] = d
            d2[y * side + x] = d
    def pair(i, _):
        drow(2 * i, lambda j: z[i, j] + z[i + 1, j])
        drow(2 * i + 1, lambda j: z[i + 1, j])
        return 0
    lax.fori_loop(0, pool, pair, 0)
    drow(side - 1, lambda j: z[pool, j] + z[pool + 1, j])
    step = 256 // slots
    def flip(k, _):
        dt[:, pl.ds(pl.multiple_of(k * 256, 256), 256)] = d2[pl.ds(k * step, step)].reshape(256, wide).T
        return 0
    lax.fori_loop(0, d2.shape[0] // step, flip, 0)
    depth = dt.shape[1]
    tail = depth - cells * slots
    other = (b, 1 - t)

    def window(n):
        cols = []
        low = n * span
        while low < (n + 1) * span:
            k = low // cin
            if k < 9:
                high = min((n + 1) * span, (k + 1) * cin)
                a, c = k // 3, k % 3
                cols.append(p_ref[a:a + side, c:c + side, :, low - k * cin:high - k * cin].reshape(cells * slots, high - low))
                low = high
            else:
                cols.append(jnp.ones((cells * slots, (n + 1) * span - low), BF16))
                low = (n + 1) * span
        win = cols[0] if len(cols) == 1 else jnp.concatenate(cols, axis=1)
        return jnp.concatenate([win, jnp.zeros((tail, span), BF16)], axis=0)

    pieces = [Sum(place, 2 - n % 2, s.at[n], r1.at[n], t1.at[n], r2.at[n], t2.at[n], r3.at[n], out_ref.at[t, n], gs.at[n], gr.at[n])
              for n in range(chunks)]
    core = {}

    def compute(n):
        win = window(n)
        def half(u):
            v = jnp.dot(dt[pl.ds(pl.multiple_of(u * cout, cout), cout), :], win, preferred_element_type=F32)
            if n == chunks - 1:
                rows = stage_sums[pl.ds(pl.multiple_of(u * cout, cout), cout), :]
                lane = lax.broadcasted_iota(jnp.int32, rows.shape, 1)
                v = jnp.concatenate([v[:, :span - 128], jnp.where(lane == 0, v[:, span - 128:], rows)], axis=1)
            return v
        give[n] = half(1 - t).astype(BF16)
        core[n] = send(give.at[n], take.at[n], cs.at[n, 0], cr.at[n, 0], other)
        keep[n % keep.shape[0]] = half(t)

    stage_sums[...] = sums

    def merge(n):
        core[n].wait_recv()
        s[n] = (keep[n % keep.shape[0]] + take[n].astype(F32)).astype(BF16).reshape(s.shape[1:])
        pieces[n].send1()

    def finish(n):
        out_ref[t, n, place.at[0], place.at[1], place.at[2]] = pieces[n].result().astype(BF16)
        pieces[n].gather1()

    back = {}
    def share(n):
        pieces[n].arrive()
        back[n] = send(out_ref.at[t, n], out_ref.at[t, n], cs.at[n, 1], cr.at[n, 1], other)

    pitch = 16
    def xrow(y):
        lhs = jnp.concatenate([dpad[y + 2 - a, 2 - c:2 - c + side, :, u * cout:(u + 1) * cout].reshape(side * slots, cout)
                               for u in range(towers) for a in range(3) for c in range(3)], axis=1)
        rhs = jnp.concatenate([w_ref[u, (a * 3 + c) * cin:(a * 3 + c + 1) * cin, :]
                               for u in range(towers) for a in range(3) for c in range(3)], axis=1)
        out = lax.dot_general(lhs, rhs, (((1,), (1,)), ((), ())), preferred_element_type=F32).reshape(side, slots, cin)
        for x in range(side):
            for l in range(cin // 128):
                stage[l, pl.ds(y * pitch + x, slots, stride=side * pitch), :] = out[x, :, l * 128:(l + 1) * 128]

    work = [merge, lambda n: pieces[n].send2(), lambda n: pieces[n].send3(), finish,
            lambda n: pieces[n].gather2(), lambda n: pieces[n].gather3(), share, lambda n: back[n].wait_recv()]
    rows_left = list(range(side))
    for step in range(chunks + 3 * (len(work) - 1) + 1):
        if step < chunks:
            compute(step)
        if step >= 14 and rows_left:
            xrow(rows_left.pop(0))
        for k, job in enumerate(work):
            n = step - 1 - 3 * k
            if 0 <= n < chunks:
                job(n)
    for y in rows_left:
        xrow(y)
    def put(k, _):
        r = k // side
        i = k % side
        dx_ref[r, i] = jnp.concatenate([stage[l, pl.ds(pl.multiple_of(k * pitch, pitch), side), :] for l in range(cin // 128)], axis=1).astype(BF16)
        return 0
    lax.fori_loop(0, slots * side, put, 0, unroll=4)
    for n in range(chunks):
        pieces[n].close()
        core[n].wait_send()
        back[n].wait_send()


def bwd_layer(dm, pooled, slope, p, w, mix, per):
    towers, nb, slots, _ = dm.shape
    side = slope.shape[0]
    cin = p.shape[3]
    cout = w.shape[4]
    pool = (side - 3) // 2 + 1
    wide = towers * cout
    span = 256
    chunks = (9 * cin + 128) // span
    d0, d1, d2 = torus(nb)
    V = pl.BlockSpec(memory_space=pltpu.VMEM)
    vm = lambda *shape: pltpu.VMEM(shape, BF16)
    dma = lambda *shape: pltpu.SemaphoreType.DMA(shape)
    cells = -(-side * side * slots // 256) * 256 // slots
    h = cout // nb
    return pl.pallas_call(
        functools.partial(bwd_kernel, per),
        out_shape=[jax.ShapeDtypeStruct((slots, side, side, cin), BF16),
                   jax.ShapeDtypeStruct((towers, chunks, d0, d1, d2, h, span), BF16)],
        in_specs=[V] * 6, out_specs=[V] * 2,
        scratch_shapes=[vm(towers, slots, nb * per), pltpu.VMEM((pool + 2, pool + 2, slots, wide), F32),
                        vm(side + 2, side + 2, slots, wide), vm(cells, slots, wide), vm(wide, cells * slots),
                        pltpu.VMEM((cin // 128, slots * side * 16, 128), F32), pltpu.VMEM((2, cout, span), F32),
                        vm(chunks, cout, span), vm(chunks, cout, span),
                        vm(chunks, d0, d1, d2, h, span), vm(chunks, d1 - 1, d0, d1, h, span), vm(chunks, d0, d1, h, span),
                        vm(chunks, d1 - 1, d0, h, span), vm(chunks, d0, h, span), vm(chunks, d0 - 1, h, span),
                        dma(chunks, 2), dma(chunks, 2), dma(chunks, hops(nb)), dma(chunks, hops(nb)), pltpu.VMEM((wide, 128), F32)],
        compiler_params=pltpu.CompilerParams(collective_id=2, has_side_effects=True, vmem_limit_bytes=62 * 2**20),
    )(dm, pooled, slope, p, w.reshape(towers, 9 * cin, cout), mix)


def write_kernel(taps, f_ref, g_ref, dw_ref, fc_ref, conv_ref):
    k = pl.program_id(0)
    fc_ref[0] = lax.dot_general(f_ref[...], g_ref[0], (((0,), (0,)), ((), ())), preferred_element_type=F32)
    conv_ref[0] = dw_ref[0, 0].astype(F32).T
    if taps > 1:
        conv_ref[1] = dw_ref[1, 0].astype(F32).T


def write_grads(f, g, dw, nb, cols, ktaps):
    live, per = f.shape
    towers, chunks, cout, span = dw.shape
    last = chunks - 1
    return pl.pallas_call(
        functools.partial(write_kernel, towers),
        grid=(nb,),
        out_shape=[jax.ShapeDtypeStruct((1, per, nb * cols), F32), jax.ShapeDtypeStruct((towers, ktaps, cout), F32)],
        in_specs=[pl.BlockSpec((live, per), lambda k: (0, 0)), pl.BlockSpec((1, live, cols), lambda k: (k, 0, 0)),
                  pl.BlockSpec((towers, 1, cout, span), lambda k: (0, jnp.minimum(k, last), 0, 0))],
        out_specs=[pl.BlockSpec((1, per, cols), lambda k: (0, 0, k)),
                   pl.BlockSpec((towers, span, cout), lambda k: (0, jnp.minimum(k, last), 0))],
        compiler_params=pltpu.CompilerParams(vmem_limit_bytes=32 * 2**20),
    )(f, g, dw)


def conv_bwd_kernel(dm_ref, pooled_ref, slope_ref, p_ref, w_ref, mix_ref, dx_ref, dw_ref, small_ref,
                    fbuf, z, dpad, d2, dt, stage):
    towers, nb, slots, _ = dm_ref.shape
    per = fbuf.shape[2] // nb
    side = slope_ref.shape[0]
    cout = w_ref.shape[2]
    cin = p_ref.shape[3]
    pool = (side - 3) // 2 + 1
    wide = towers * cout
    cells = side * side
    for t in range(towers):
        for b in range(nb):
            fbuf[t, :, b * per:(b + 1) * per] = dm_ref[t, b, :, :per]
    z[0] = jnp.zeros(z.shape[1:], F32)
    z[pool + 1] = jnp.zeros(z.shape[1:], F32)
    acc = [[jnp.zeros((slots, cout), F32)] * 2 for _ in range(2)]
    for i in range(pool):
        z[i + 1, 0] = jnp.zeros(z.shape[2:], F32)
        z[i + 1, pool + 1] = jnp.zeros(z.shape[2:], F32)
        for j in range(pool):
            q = i * pool + j
            dm = [fbuf[t, :, q * cout:(q + 1) * cout].astype(F32) for t in range(towers)]
            for u in range(towers):
                pu = pooled_ref[q, :, u * cout:(u + 1) * cout]
                for t in range(towers):
                    acc[t][u] = acc[t][u] + dm[t] * pu
                z[i + 1, j + 1, :, u * cout:(u + 1) * cout] = (mix_ref[0, u][None] * dm[0] + mix_ref[1, u][None] * dm[1]) * (1.0 / 9.0)
    dpad[0] = jnp.zeros(dpad.shape[1:], BF16)
    dpad[side + 1] = jnp.zeros(dpad.shape[1:], BF16)
    d2[cells:] = jnp.zeros((d2.shape[0] - cells, slots, wide), BF16)
    def drow(y, src):
        dpad[y + 1, 0] = jnp.zeros((slots, wide), BF16)
        dpad[y + 1, side + 1] = jnp.zeros((slots, wide), BF16)
        for x in range(side):
            j = x // 2
            v = src(j + 1) if x % 2 else src(j) + src(j + 1)
            d = (v * slope_ref[y, x].astype(F32)).astype(BF16)
            dpad[y + 1, x + 1] = d
            d2[y * side + x] = d
    def pair(i, _):
        drow(2 * i, lambda j: z[i, j] + z[i + 1, j])
        drow(2 * i + 1, lambda j: z[i + 1, j])
        return 0
    lax.fori_loop(0, pool, pair, 0)
    drow(side - 1, lambda j: z[pool, j] + z[pool + 1, j])
    step = 256 // slots
    def flip(k, _):
        dt[:, pl.ds(pl.multiple_of(k * 256, 256), 256)] = d2[pl.ds(k * step, step)].reshape(256, wide).T
        return 0
    lax.fori_loop(0, d2.shape[0] // step, flip, 0)
    tail = (d2.shape[0] - cells) * slots
    for a in range(3):
        win = jnp.concatenate([p_ref[a:a + side, b:b + side].reshape(cells * slots, cin) for b in range(3)], axis=1)
        win = jnp.concatenate([win, jnp.zeros((tail, 3 * cin), BF16)], axis=0)
        dw_ref[a] = jnp.dot(dt[...], win, preferred_element_type=F32)
    ones = jnp.ones((d2.shape[0] * slots, 128), BF16)
    small_ref[:, 0:128] = jnp.dot(dt[...], ones, preferred_element_type=F32)
    rows = jnp.concatenate([jnp.concatenate([jnp.sum(acc[t][u], axis=0, keepdims=True) for u in range(2)], axis=1) for t in range(2)], axis=0)
    small_ref[:, 128:256] = jnp.concatenate([rows, jnp.zeros((126, wide), F32)], axis=0).T
    pitch = 16
    def xrow(y):
        lhs = jnp.concatenate([dpad[y + 2 - a, 2 - b:2 - b + side, :, t * cout:(t + 1) * cout].reshape(side * slots, cout)
                               for t in range(towers) for a in range(3) for b in range(3)], axis=1)
        rhs = jnp.concatenate([w_ref[t, (a * 3 + b) * cin:(a * 3 + b + 1) * cin, :]
                               for t in range(towers) for a in range(3) for b in range(3)], axis=1)
        out = lax.dot_general(lhs, rhs, (((1,), (1,)), ((), ())), preferred_element_type=F32).reshape(side, slots, cin)
        for x in range(side):
            for l in range(cin // 128):
                stage[l, pl.ds(y * pitch + x, slots, stride=side * pitch), :] = out[x, :, l * 128:(l + 1) * 128]
    lax.fori_loop(0, side, lambda y, _: (xrow(y), 0)[1], 0)
    def put(k, _):
        r = k // side
        i = k % side
        dx_ref[r, i] = jnp.concatenate([stage[l, pl.ds(pl.multiple_of(k * pitch, pitch), side), :] for l in range(cin // 128)], axis=1).astype(BF16)
        return 0
    lax.fori_loop(0, slots * side, put, 0, unroll=4)

def conv_bwd(dm, pooled, slope, p, w, mix, per):
    towers, nb, slots, _ = dm.shape
    side = slope.shape[0]
    cin = p.shape[3]
    cout = w.shape[4]
    pool = (side - 3) // 2 + 1
    wide = towers * cout
    V = pl.BlockSpec(memory_space=pltpu.VMEM)
    cells = -(-side * side * slots // 256) * 256 // slots
    return pl.pallas_call(
        conv_bwd_kernel,
        out_shape=[jax.ShapeDtypeStruct((slots, side, side, cin), BF16),
                   jax.ShapeDtypeStruct((3, wide, 3 * cin), F32),
                   jax.ShapeDtypeStruct((wide, 256), F32)],
        in_specs=[V] * 6, out_specs=[V] * 3,
        scratch_shapes=[pltpu.VMEM((towers, slots, nb * per), BF16),
                        pltpu.VMEM((pool + 2, pool + 2, slots, wide), F32),
                        pltpu.VMEM((side + 2, side + 2, slots, wide), BF16),
                        pltpu.VMEM((cells, slots, wide), BF16),
                        pltpu.VMEM((wide, cells * slots), BF16),
                        pltpu.VMEM((cin // 128, slots * side * 16, 128), F32)],
        compiler_params=pltpu.CompilerParams(vmem_limit_bytes=62 * 2**20),
    )(dm, pooled, slope, p, w.reshape(towers, 9 * cin, cout), mix)


def swap(block):
    return lax.ppermute(block, "tower", [(0, 1), (1, 0)])


def plain_shards(crop_pixels, live_rows, conv_weight, conv_bias, stitch_conv, fc_weight, fc_bias, stitch_fc, cotangent):
    slots = crop_pixels.shape[0]
    nb = lax.axis_size("batch")
    b, t = lax.axis_index("batch"), lax.axis_index("tower")
    rows = 2 * slots * nb
    live = rows // 2
    fc = fc_weight.shape[2]
    per = fc_weight.shape[1]
    cols = fc // nb
    w = fc_weight[0]
    feat, pooled, slope, padded = conv_fwd(live_rows, crop_pixels, conv_weight, conv_bias, stitch_conv, nb)
    both = ("batch", "tower")
    counts = lax.all_gather(live_rows, both, axis=0, tiled=True)
    got = lax.all_to_all(feat[..., :per].transpose(1, 0, 2, 3).reshape(2 * nb, slots, per), both, 0, 0).reshape(rows, per)
    slot = jnp.arange(rows, dtype=jnp.int32)
    start = jnp.cumsum(counts) - counts
    place = jnp.where(slot % slots < counts[slot // slots], start[slot // slots] + slot % slots, -1)
    spread = (place[:, None] == jnp.arange(live, dtype=jnp.int32)[None]).astype(BF16)
    compact = lambda x: lax.dot_general(spread, x, (((0,), (0,)), ((), ())), preferred_element_type=F32).astype(BF16)
    expand = lambda x: jnp.dot(spread, x, preferred_element_type=F32).astype(BF16)
    f = compact(got)
    part = jnp.dot(f, w, preferred_element_type=F32)
    hidden = lax.psum_scatter(part, "batch", scatter_dimension=1, tiled=True)
    hidden = hidden + lax.dynamic_slice_in_dim(fc_bias[0], b * cols, cols)[None]
    value, slope_fc = gelu_pair(hidden)
    gate = value.astype(BF16)
    cot = compact(lax.all_to_all(cotangent[0].reshape(2 * slots, nb, cols).transpose(1, 0, 2), "batch", 0, 0).reshape(rows, cols))
    gate_other, cot_other = swap(gate).astype(F32), swap(cot).astype(F32)
    gate_own, cot_own = gate.astype(F32), cot.astype(F32)
    mix = lax.dynamic_slice_in_dim(stitch_fc, b * cols, cols, axis=2)
    own = jnp.where(t == 0, mix[0, 0], mix[1, 1])
    cross = jnp.where(t == 0, mix[0, 1], mix[1, 0])
    back = jnp.where(t == 0, mix[1, 0], mix[0, 1])
    stitched = (own[None] * gate_own + cross[None] * gate_other).astype(BF16)
    stitched = lax.all_to_all(expand(stitched).reshape(nb, 2 * slots, cols), "batch", 0, 0)
    stitched = stitched.transpose(1, 0, 2).reshape(1, 2 * slots, fc)
    d_own = jnp.sum(cot_own * gate_own, axis=0)
    d_cross = jnp.sum(cot_own * gate_other, axis=0)
    dh = ((own[None] * cot_own + back[None] * cot_other) * slope_fc).astype(BF16)
    sums = jnp.stack([d_own, d_cross, jnp.sum(dh.astype(F32), axis=0)])
    sums = lax.all_gather(sums, both, axis=0).reshape(nb, 2, 3, cols).transpose(1, 2, 0, 3).reshape(2, 3, fc)
    d_stitch_fc = jnp.stack([sums[0, :2], sums[1, 1::-1]])
    d_fc_bias = sums[:, 2]
    dh = lax.all_gather(dh, "batch", axis=1, tiled=True)
    d_fc_weight = lax.dot_general(f, dh, (((0,), (0,)), ((), ())), preferred_element_type=F32)[None]
    df = lax.dot_general(dh, w, (((1,), (1,)), ((), ())), preferred_element_type=F32).astype(BF16)
    dm = lax.all_to_all(expand(df).reshape(2 * nb, slots, per), both, 0, 0)
    dm = dm.reshape(nb, 2, slots, per).transpose(1, 0, 2, 3)
    dx, dw, small = conv_bwd(dm, pooled, slope, padded, conv_weight, stitch_conv, per)
    dw = lax.psum(dw, both)
    cin, cout = conv_weight.shape[3:]
    dw = dw.reshape(3, 2, cout, 3, cin).transpose(1, 0, 3, 4, 2)
    small = lax.psum(small, both)
    d_conv_bias = small[:, 0].reshape(2, cout)
    d_stitch_conv = small[:, 128:130].T.reshape(2, 2, cout)
    return stitched, dx, dw, d_conv_bias, d_stitch_conv, d_fc_weight, d_fc_bias, d_stitch_fc


def shards(crop_pixels, live_rows, conv_weight, conv_bias, stitch_conv, fc_weight, fc_bias, stitch_fc, cotangent):
    slots = crop_pixels.shape[0]
    nb = lax.axis_size("batch")
    b = lax.axis_index("batch")
    fc = fc_weight.shape[2]
    per = fc_weight.shape[1]
    cols = fc // nb
    cin, cout = conv_weight.shape[3:]
    live = slots * nb
    feat, pooled, slope, padded = conv_fwd(live_rows, crop_pixels, conv_weight, conv_bias, stitch_conv, nb)
    bias = lax.dynamic_slice_in_dim(fc_bias, b * cols, cols, axis=1)
    mix = lax.dynamic_slice_in_dim(stitch_fc, b * cols, cols, axis=2).reshape(2, 2, 1, cols)
    stitched, f, dh, dm, sums = fc_layer(feat, cotangent[0], fc_weight[0], bias, mix, nb, per)
    d_stitch_fc = jnp.stack([sums[0, :2], sums[1, 1::-1]])
    d_fc_bias = sums[:, 2]
    dx, dw = bwd_layer(dm, pooled, slope, padded, conv_weight, stitch_conv, per)
    dw = dw.reshape(2, dw.shape[1], cout, dw.shape[-1])
    d_fc_weight, d_kernel = write_grads(f, dh.reshape(nb, live, cols), dw, nb, cols, 9 * cin)
    small = dw[:, -1, :, 128:131].astype(F32)
    d_conv_bias = small[:, :, 0]
    d_stitch_conv = small[:, :, 1:].transpose(2, 0, 1)
    return stitched, dx, d_kernel.reshape(conv_weight.shape), d_conv_bias, d_stitch_conv, d_fc_weight, d_fc_bias, d_stitch_fc


def solution(mesh):
    in_specs = (
        P(("batch", "tower"), None, None, None), P(("batch", "tower")), P(), P(), P(),
        P("tower", "batch", None), P("tower", None), P(), P("tower", "batch", None),
    )
    out_specs = (
        P("tower", "batch", None), P(("batch", "tower"), None, None, None), P(), P(), P(),
        P("tower", "batch", None), P(), P(),
    )
    body = shards if mesh.shape["batch"] == 16 else plain_shards
    return jax.shard_map(body, mesh=mesh, in_specs=in_specs, out_specs=out_specs, check_vma=False)
```

```python
import functools, math
import jax, jax.numpy as jnp
from jax import lax
from jax.experimental import pallas as pl
from jax.experimental.pallas import tpu as pltpu
from jax.sharding import PartitionSpec as P
F32, BF16 = jnp.float32, jnp.bfloat16
CG = math.sqrt(2.0 / math.pi)

def gelu_pair(v):
    sq = v * v
    t = jnp.tanh(v * (CG + (CG * 0.044715) * sq))
    half = 0.5 + 0.5 * t
    value = v * half
    slope = half + value * (1.0 - half) * (2.0 * CG + (6.0 * CG * 0.044715) * sq)
    return value, slope

def conv_fwd_kernel(rows_per, live_ref, x_ref, w_ref, b_ref, mix_ref, feat_ref, pooled_ref, slope_ref, p_ref, stage, act, fbuf):
    slots, side, _, cin = x_ref.shape
    towers, _, cout = w_ref.shape
    pool = (side - 3) // 2 + 1
    pitch = 16
    lanes = cin // 128
    p_ref[0] = jnp.zeros(p_ref.shape[1:], BF16)
    p_ref[side + 1] = jnp.zeros(p_ref.shape[1:], BF16)
    def put(k, _):
        r = k // side
        i = k % side
        v = x_ref[r, i].astype(F32)
        for l in range(lanes):
            stage[l, pl.ds(pl.multiple_of(k * pitch, pitch), side), :] = v[:, l * 128:(l + 1) * 128]
        return 0
    lax.fori_loop(0, slots * side, put, 0, unroll=4)
    def take(i, _):
        p_ref[i + 1, 0] = jnp.zeros((slots, cin), BF16)
        p_ref[i + 1, side + 1] = jnp.zeros((slots, cin), BF16)
        for j in range(side):
            for l in range(lanes):
                v = stage[l, pl.ds(i * pitch + j, slots, stride=side * pitch), :]
                p_ref[i + 1, j + 1, :, l * 128:(l + 1) * 128] = v.astype(BF16)
        return 0
    lax.fori_loop(0, side, take, 0)
    rows = rows_per * side * slots
    def row(y):
        window = jnp.concatenate(
            [p_ref[pl.ds(y + a, rows_per), b:b + side].reshape(rows, cin) for a in range(3) for b in range(3)], axis=1)
        for t in range(towers):
            pre = jnp.dot(window, w_ref[t], preferred_element_type=F32) + b_ref[t][None]
            value, slope = gelu_pair(pre)
            act[pl.ds(y, rows_per), :, :, t * cout:(t + 1) * cout] = value.reshape(rows_per, side, slots, cout)
            slope_ref[pl.ds(y, rows_per), :, :, t * cout:(t + 1) * cout] = slope.astype(BF16).reshape(rows_per, side, slots, cout)
    lax.fori_loop(0, side // rows_per, lambda k, _: (row(k * rows_per), 0)[1], 0)
    for i in range(pool):
        s3 = act[2 * i] + act[2 * i + 1] + act[2 * i + 2]
        for j in range(pool):
            p9 = (s3[2 * j] + s3[2 * j + 1] + s3[2 * j + 2]) * (1.0 / 9.0)
            pooled_ref[i * pool + j] = p9
            for t in range(towers):
                m = mix_ref[t, 0][None] * p9[:, :cout] + mix_ref[t, 1][None] * p9[:, cout:]
                fbuf[t, :, (i * pool + j) * cout:(i * pool + j + 1) * cout] = m.astype(BF16)
    nb = feat_ref.shape[1]
    per = fbuf.shape[2] // nb
    flags = (lax.broadcasted_iota(jnp.int32, (slots, feat_ref.shape[3] - per), 0) < live_ref[0]).astype(F32).astype(BF16)
    for t in range(towers):
        for b in range(nb):
            feat_ref[t, b, :, :per] = fbuf[t, :, b * per:(b + 1) * per]
            feat_ref[t, b, :, per:] = flags

def conv_fwd(live, x, w, bias, mix, nb, rows_per=1):
    slots, side, _, cin = x.shape
    towers, _, _, _, cout = w.shape
    pool = (side - 3) // 2 + 1
    nf = pool * pool * cout
    V = pl.BlockSpec(memory_space=pltpu.VMEM)
    return pl.pallas_call(
        functools.partial(conv_fwd_kernel, rows_per),
        out_shape=[jax.ShapeDtypeStruct((towers, nb, slots, nf // nb // 128 * 128 + 128), BF16),
                   jax.ShapeDtypeStruct((pool * pool, slots, towers * cout), F32),
                   jax.ShapeDtypeStruct((side, side, slots, towers * cout), BF16),
                   jax.ShapeDtypeStruct((side + 2, side + 2, slots, cin), BF16)],
        in_specs=[pl.BlockSpec(memory_space=pltpu.SMEM)] + [V] * 4, out_specs=[V] * 4,
        scratch_shapes=[pltpu.VMEM((cin // 128, slots * side * 16, 128), F32),
                        pltpu.VMEM((side, side, slots, towers * cout), F32),
                        pltpu.VMEM((towers, slots, nf), BF16)],
        compiler_params=pltpu.CompilerParams(vmem_limit_bytes=60 * 2**20),
    )(live, x, w.reshape(towers, 9 * cin, cout), bias, mix)


MESH_ID = pl.DeviceIdType.MESH


def torus(nb):
    return {16: (4, 2, 2), 64: (4, 4, 4)}.get(nb, (nb, 1, 1))


class Place:
    def __init__(self, nb):
        self.dims = torus(nb)
        self.b, self.t = lax.axis_index("batch"), lax.axis_index("tower")
        d0, d1, d2 = self.dims
        self.at = (self.b // (d1 * d2), (self.b // d2) % d1, self.b % d2)

    def peer(self, dim, k):
        c = list(self.at)
        c[dim] = k
        return ((c[0] * self.dims[1] + c[1]) * self.dims[2] + c[2], self.t)


def send(src, dst, ssem, rsem, device):
    copy = pltpu.make_async_remote_copy(src_ref=src, dst_ref=dst, send_sem=ssem, recv_sem=rsem, device_id=device, device_id_type=MESH_ID)
    copy.start()
    return copy


class Sum:
    def __init__(self, place, p, s, r1, t1, r2, t2, r3, g, ssem, rsem):
        self.place, self.p, self.q = place, p, 3 - p
        self.s, self.r1, self.t1, self.r2, self.t2, self.r3, self.g = s, r1, t1, r2, t2, r3, g
        self.ssem, self.rsem = ssem, rsem
        self.sent = []
        self.used = 0

    def pick(self, ref, k):
        return ref.at[:, :, k] if self.p == 2 else ref.at[:, k]

    def post(self, dim, src_of, dst_of):
        n = self.place.dims[dim]
        self.flight = []
        for j in range(1, n):
            k = lax.rem(self.place.at[dim] + j, n)
            i = self.used
            self.used += 1
            self.flight.append(send(src_of(k), dst_of(j - 1), self.ssem.at[i], self.rsem.at[i], self.place.peer(dim, k)))
        self.sent += self.flight

    def arrive(self):
        for c in self.flight:
            c.wait_recv()

    def add(self, mine, got, n):
        v = mine.astype(F32)
        for j in range(n):
            v = v + got[j].astype(F32)
        return v

    def send1(self):
        self.post(self.p, lambda k: self.pick(self.s, k), lambda j: self.r1.at[j])

    def send2(self):
        self.arrive()
        n = self.place.dims[self.p]
        self.t1[...] = self.add(self.pick(self.s, self.place.at[self.p])[...], self.r1, n - 1).astype(BF16)
        self.post(self.q, lambda k: self.t1.at[:, k], lambda j: self.r2.at[j])

    def send3(self):
        self.arrive()
        n = self.place.dims[self.q]
        self.t2[...] = self.add(self.t1[:, self.place.at[self.q]], self.r2, n - 1).astype(BF16)
        self.post(0, lambda k: self.t2.at[k], lambda j: self.r3.at[j])

    def result(self):
        self.arrive()
        return self.add(self.t2[self.place.at[0]], self.r3, self.place.dims[0] - 1)

    def gather1(self):
        mine = self.g.at[self.place.at[0], self.place.at[1], self.place.at[2]]
        self.post(0, lambda k: mine, lambda j: mine)

    def gather2(self):
        self.arrive()
        mine = self.g.at[:, self.place.at[1], self.place.at[2]]
        self.post(self.q, lambda k: mine, lambda j: mine)

    def gather3(self):
        self.arrive()
        mine = self.pick(self.g, self.place.at[self.p])
        self.post(self.p, lambda k: mine, lambda j: mine)

    def close(self):
        for c in self.sent:
            c.wait_send()


def hops(nb):
    return 2 * sum(d - 1 for d in torus(nb))


def conv_bwd_kernel(dm_ref, pooled_ref, slope_ref, p_ref, w_ref, mix_ref, dx_ref, dw_ref, small_ref,
                    fbuf, z, dpad, d2, dt, stage):
    towers, nb, slots, _ = dm_ref.shape
    per = fbuf.shape[2] // nb
    side = slope_ref.shape[0]
    cout = w_ref.shape[2]
    cin = p_ref.shape[3]
    pool = (side - 3) // 2 + 1
    wide = towers * cout
    cells = side * side
    for t in range(towers):
        for b in range(nb):
            fbuf[t, :, b * per:(b + 1) * per] = dm_ref[t, b, :, :per]
    z[0] = jnp.zeros(z.shape[1:], F32)
    z[pool + 1] = jnp.zeros(z.shape[1:], F32)
    acc = [[jnp.zeros((slots, cout), F32)] * 2 for _ in range(2)]
    for i in range(pool):
        z[i + 1, 0] = jnp.zeros(z.shape[2:], F32)
        z[i + 1, pool + 1] = jnp.zeros(z.shape[2:], F32)
        for j in range(pool):
            q = i * pool + j
            dm = [fbuf[t, :, q * cout:(q + 1) * cout].astype(F32) for t in range(towers)]
            for u in range(towers):
                pu = pooled_ref[q, :, u * cout:(u + 1) * cout]
                for t in range(towers):
                    acc[t][u] = acc[t][u] + dm[t] * pu
                z[i + 1, j + 1, :, u * cout:(u + 1) * cout] = (mix_ref[0, u][None] * dm[0] + mix_ref[1, u][None] * dm[1]) * (1.0 / 9.0)
    dpad[0] = jnp.zeros(dpad.shape[1:], BF16)
    dpad[side + 1] = jnp.zeros(dpad.shape[1:], BF16)
    d2[cells:] = jnp.zeros((d2.shape[0] - cells, slots, wide), BF16)
    def drow(y, src):
        dpad[y + 1, 0] = jnp.zeros((slots, wide), BF16)
        dpad[y + 1, side + 1] = jnp.zeros((slots, wide), BF16)
        for x in range(side):
            j = x // 2
            v = src(j + 1) if x % 2 else src(j) + src(j + 1)
            d = (v * slope_ref[y, x].astype(F32)).astype(BF16)
            dpad[y + 1, x + 1] = d
            d2[y * side + x] = d
    def pair(i, _):
        drow(2 * i, lambda j: z[i, j] + z[i + 1, j])
        drow(2 * i + 1, lambda j: z[i + 1, j])
        return 0
    lax.fori_loop(0, pool, pair, 0)
    drow(side - 1, lambda j: z[pool, j] + z[pool + 1, j])
    step = 256 // slots
    def flip(k, _):
        dt[:, pl.ds(pl.multiple_of(k * 256, 256), 256)] = d2[pl.ds(k * step, step)].reshape(256, wide).T
        return 0
    lax.fori_loop(0, d2.shape[0] // step, flip, 0)
    tail = (d2.shape[0] - cells) * slots
    for a in range(3):
        win = jnp.concatenate([p_ref[a:a + side, b:b + side].reshape(cells * slots, cin) for b in range(3)], axis=1)
        win = jnp.concatenate([win, jnp.zeros((tail, 3 * cin), BF16)], axis=0)
        dw_ref[a] = jnp.dot(dt[...], win, preferred_element_type=F32)
    ones = jnp.ones((d2.shape[0] * slots, 128), BF16)
    small_ref[:, 0:128] = jnp.dot(dt[...], ones, preferred_element_type=F32)
    rows = jnp.concatenate([jnp.concatenate([jnp.sum(acc[t][u], axis=0, keepdims=True) for u in range(2)], axis=1) for t in range(2)], axis=0)
    small_ref[:, 128:256] = jnp.concatenate([rows, jnp.zeros((126, wide), F32)], axis=0).T
    pitch = 16
    def xrow(y):
        lhs = jnp.concatenate([dpad[y + 2 - a, 2 - b:2 - b + side, :, t * cout:(t + 1) * cout].reshape(side * slots, cout)
                               for t in range(towers) for a in range(3) for b in range(3)], axis=1)
        rhs = jnp.concatenate([w_ref[t, (a * 3 + b) * cin:(a * 3 + b + 1) * cin, :]
                               for t in range(towers) for a in range(3) for b in range(3)], axis=1)
        out = lax.dot_general(lhs, rhs, (((1,), (1,)), ((), ())), preferred_element_type=F32).reshape(side, slots, cin)
        for x in range(side):
            for l in range(cin // 128):
                stage[l, pl.ds(y * pitch + x, slots, stride=side * pitch), :] = out[x, :, l * 128:(l + 1) * 128]
    lax.fori_loop(0, side, lambda y, _: (xrow(y), 0)[1], 0)
    def put(k, _):
        r = k // side
        i = k % side
        dx_ref[r, i] = jnp.concatenate([stage[l, pl.ds(pl.multiple_of(k * pitch, pitch), side), :] for l in range(cin // 128)], axis=1).astype(BF16)
        return 0
    lax.fori_loop(0, slots * side, put, 0, unroll=4)

def conv_bwd(dm, pooled, slope, p, w, mix, per):
    towers, nb, slots, _ = dm.shape
    side = slope.shape[0]
    cin = p.shape[3]
    cout = w.shape[4]
    pool = (side - 3) // 2 + 1
    wide = towers * cout
    V = pl.BlockSpec(memory_space=pltpu.VMEM)
    cells = -(-side * side * slots // 256) * 256 // slots
    return pl.pallas_call(
        conv_bwd_kernel,
        out_shape=[jax.ShapeDtypeStruct((slots, side, side, cin), BF16),
                   jax.ShapeDtypeStruct((3, wide, 3 * cin), F32),
                   jax.ShapeDtypeStruct((wide, 256), F32)],
        in_specs=[V] * 6, out_specs=[V] * 3,
        scratch_shapes=[pltpu.VMEM((towers, slots, nb * per), BF16),
                        pltpu.VMEM((pool + 2, pool + 2, slots, wide), F32),
                        pltpu.VMEM((side + 2, side + 2, slots, wide), BF16),
                        pltpu.VMEM((cells, slots, wide), BF16),
                        pltpu.VMEM((wide, cells * slots), BF16),
                        pltpu.VMEM((cin // 128, slots * side * 16, 128), F32)],
        compiler_params=pltpu.CompilerParams(vmem_limit_bytes=62 * 2**20),
    )(dm, pooled, slope, p, w.reshape(towers, 9 * cin, cout), mix)


def swap(block):
    return lax.ppermute(block, "tower", [(0, 1), (1, 0)])


def plain_shards(crop_pixels, live_rows, conv_weight, conv_bias, stitch_conv, fc_weight, fc_bias, stitch_fc, cotangent):
    slots = crop_pixels.shape[0]
    nb = lax.axis_size("batch")
    b, t = lax.axis_index("batch"), lax.axis_index("tower")
    rows = 2 * slots * nb
    live = rows // 2
    fc = fc_weight.shape[2]
    per = fc_weight.shape[1]
    cols = fc // nb
    w = fc_weight[0]
    feat, pooled, slope, padded = conv_fwd(live_rows, crop_pixels, conv_weight, conv_bias, stitch_conv, nb)
    both = ("batch", "tower")
    counts = lax.all_gather(live_rows, both, axis=0, tiled=True)
    got = lax.all_to_all(feat[..., :per].transpose(1, 0, 2, 3).reshape(2 * nb, slots, per), both, 0, 0).reshape(rows, per)
    slot = jnp.arange(rows, dtype=jnp.int32)
    start = jnp.cumsum(counts) - counts
    place = jnp.where(slot % slots < counts[slot // slots], start[slot // slots] + slot % slots, -1)
    spread = (place[:, None] == jnp.arange(live, dtype=jnp.int32)[None]).astype(BF16)
    compact = lambda x: lax.dot_general(spread, x, (((0,), (0,)), ((), ())), preferred_element_type=F32).astype(BF16)
    expand = lambda x: jnp.dot(spread, x, preferred_element_type=F32).astype(BF16)
    f = compact(got)
    part = jnp.dot(f, w, preferred_element_type=F32)
    hidden = lax.psum_scatter(part, "batch", scatter_dimension=1, tiled=True)
    hidden = hidden + lax.dynamic_slice_in_dim(fc_bias[0], b * cols, cols)[None]
    value, slope_fc = gelu_pair(hidden)
    gate = value.astype(BF16)
    cot = compact(lax.all_to_all(cotangent[0].reshape(2 * slots, nb, cols).transpose(1, 0, 2), "batch", 0, 0).reshape(rows, cols))
    gate_other, cot_other = swap(gate).astype(F32), swap(cot).astype(F32)
    gate_own, cot_own = gate.astype(F32), cot.astype(F32)
    mix = lax.dynamic_slice_in_dim(stitch_fc, b * cols, cols, axis=2)
    own = jnp.where(t == 0, mix[0, 0], mix[1, 1])
    cross = jnp.where(t == 0, mix[0, 1], mix[1, 0])
    back = jnp.where(t == 0, mix[1, 0], mix[0, 1])
    stitched = (own[None] * gate_own + cross[None] * gate_other).astype(BF16)
    stitched = lax.all_to_all(expand(stitched).reshape(nb, 2 * slots, cols), "batch", 0, 0)
    stitched = stitched.transpose(1, 0, 2).reshape(1, 2 * slots, fc)
    d_own = jnp.sum(cot_own * gate_own, axis=0)
    d_cross = jnp.sum(cot_own * gate_other, axis=0)
    dh = ((own[None] * cot_own + back[None] * cot_other) * slope_fc).astype(BF16)
    sums = jnp.stack([d_own, d_cross, jnp.sum(dh.astype(F32), axis=0)])
    sums = lax.all_gather(sums, both, axis=0).reshape(nb, 2, 3, cols).transpose(1, 2, 0, 3).reshape(2, 3, fc)
    d_stitch_fc = jnp.stack([sums[0, :2], sums[1, 1::-1]])
    d_fc_bias = sums[:, 2]
    dh = lax.all_gather(dh, "batch", axis=1, tiled=True)
    d_fc_weight = lax.dot_general(f, dh, (((0,), (0,)), ((), ())), preferred_element_type=F32)[None]
    df = lax.dot_general(dh, w, (((1,), (1,)), ((), ())), preferred_element_type=F32).astype(BF16)
    dm = lax.all_to_all(expand(df).reshape(2 * nb, slots, per), both, 0, 0)
    dm = dm.reshape(nb, 2, slots, per).transpose(1, 0, 2, 3)
    dx, dw, small = conv_bwd(dm, pooled, slope, padded, conv_weight, stitch_conv, per)
    dw = lax.psum(dw, both)
    cin, cout = conv_weight.shape[3:]
    dw = dw.reshape(3, 2, cout, 3, cin).transpose(1, 0, 3, 4, 2)
    small = lax.psum(small, both)
    d_conv_bias = small[:, 0].reshape(2, cout)
    d_stitch_conv = small[:, 128:130].T.reshape(2, 2, cout)
    return stitched, dx, dw, d_conv_bias, d_stitch_conv, d_fc_weight, d_fc_bias, d_stitch_fc


def whole_kernel(parts, per, live_ref, x_hbm, cw_hbm, cbias_ref, cmix_ref, cot_ref, w_hbm, bias_ref, fmix_ref,
                 out_ref, dx_hbm, f_ref, g, grad_ref, stitch_ref, fbias_ref,
                 xin, cw, stage, act, p, slope, pooled, fbuf, feat, fin, dm, w, cin, cgot, sgot, spread,
                 s, r1, t1, r2, t2, r3, gates, cots, wide, acc,
                 z, dpad, d2, dt, keep, cs_, cr1, ct1, cr2, ct2, cr3, sums_t,
                 xsem, lsem, wsem, fs, fr, cs, cr, xs, xr, ss, sr, ms, mr, gs, gr, ds, dr, ks, kr, hs, hr):
    nb = cin.shape[0]
    place = Place(nb)
    b, t = place.b, place.t
    me = b * 2 + t
    total = 2 * nb
    slots, side, _, chan = xin.shape
    towers, _, cout = cw.shape
    pool = (side - 3) // 2 + 1
    wide_c = towers * cout
    pitch = 16
    lanes = chan // 128
    padded = feat.shape[2]
    rows = total * slots
    live = rows // 2
    cols = cin.shape[2]
    other = (b, 1 - t)
    device = lambda d: (d // 2, d % 2)

    groups = xsem.shape[0]
    crops = slots // groups
    loads = [pltpu.make_async_copy(x_hbm.at[pl.ds(k * crops, crops)], xin.at[pl.ds(k * crops, crops)], xsem.at[k]) for k in range(groups)]
    for c in loads:
        c.start()
    cw_load = pltpu.make_async_copy(cw_hbm, cw, lsem)
    cw_load.start()
    w_loads = [pltpu.make_async_copy(w_hbm.at[:, pl.ds(k * cols, cols)], w.at[k], wsem.at[k]) for k in range(nb)]
    for c in w_loads:
        c.start()
    bar = pltpu.get_barrier_semaphore()
    def hail(k, _):
        pl.semaphore_signal(bar, inc=1, device_id=device(lax.rem(me + k, total)), device_id_type=MESH_ID)
        return 0
    lax.fori_loop(1, total, hail, 0)
    for k in range(nb):
        cin[k] = cot_ref[:, k * cols:(k + 1) * cols]
    cgot[b] = cin[b]

    p[0] = jnp.zeros(p.shape[1:], BF16)
    p[side + 1] = jnp.zeros(p.shape[1:], BF16)
    for q in range(groups):
        loads[q].wait()
        def put(k, _):
            v = xin[k // side, k % side].astype(F32)
            for l in range(lanes):
                stage[l, pl.ds(pl.multiple_of(k * pitch, pitch), side), :] = v[:, l * 128:(l + 1) * 128]
            return 0
        lax.fori_loop(q * crops * side, (q + 1) * crops * side, put, 0, unroll=4)
    def take_row(i, _):
        p[i + 1, 0] = jnp.zeros((slots, chan), BF16)
        p[i + 1, side + 1] = jnp.zeros((slots, chan), BF16)
        for j in range(side):
            for l in range(lanes):
                v = stage[l, pl.ds(i * pitch + j, slots, stride=side * pitch), :]
                p[i + 1, j + 1, :, l * 128:(l + 1) * 128] = v.astype(BF16)
        return 0
    lax.fori_loop(0, side, take_row, 0)

    pl.semaphore_wait(bar, total - 1)
    def cot_copy(k):
        d = lax.rem(b + k, nb)
        return pltpu.make_async_remote_copy(
            src_ref=cin.at[d], dst_ref=cgot.at[b], send_sem=cs.at[k], recv_sem=cr.at[k],
            device_id=(d, t), device_id_type=MESH_ID)
    lax.fori_loop(1, nb, lambda k, _: (cot_copy(k).start(), 0)[1], 0)

    cw_load.wait()
    turn = place.at[0] * 2 < place.dims[0]
    flags = (lax.broadcasted_iota(jnp.int32, (slots, padded - per), 0) < live_ref[0]).astype(F32).astype(BF16)
    m_rows = side * slots
    def conv_row(k):
        y = jnp.where(turn, side - 1 - k, k)
        window = jnp.concatenate([p[y + a, c:c + side].reshape(m_rows, chan) for a in range(3) for c in range(3)], axis=1)
        for u in range(towers):
            pre = jnp.dot(window, cw[u], preferred_element_type=F32) + cbias_ref[u][None]
            value, inc = gelu_pair(pre)
            act[lax.rem(k, 3), :, :, u * cout:(u + 1) * cout] = value.reshape(side, slots, cout)
            slope[y, :, :, u * cout:(u + 1) * cout] = inc.astype(slope.dtype).reshape(side, slots, cout)
    def feature_copy(d):
        return pltpu.make_async_remote_copy(
            src_ref=feat.at[d], dst_ref=fin.at[me], send_sem=fs.at[d], recv_sem=fr.at[me],
            device_id=device(d), device_id_type=MESH_ID)
    def feature_wait(d):
        return pltpu.make_async_remote_copy(
            src_ref=feat.at[d], dst_ref=fin.at[d], send_sem=fs.at[d], recv_sem=fr.at[d],
            device_id=device(d), device_id_type=MESH_ID)
    pairs = nb // 2
    conv_row(0)
    def pooled_row(n, _):
        lax.fori_loop(2 * n + 1, 2 * n + 3, lambda k, _: (conv_row(k), 0)[1], 0)
        i = jnp.where(turn, pool - 1 - n, n)
        s3 = act[0] + act[1] + act[2]
        for j in range(pool):
            p9 = (s3[2 * j] + s3[2 * j + 1] + s3[2 * j + 2]) * (1.0 / 9.0)
            pooled[i * pool + j] = p9
            at = pl.ds(pl.multiple_of((i * pool + j) * cout, cout), cout)
            for u in range(towers):
                m = cmix_ref[u, 0][None] * p9[:, :cout] + cmix_ref[u, 1][None] * p9[:, cout:]
                fbuf[u, :, at] = m.astype(BF16)
        def pair(q, _):
            c = jnp.where(turn, pairs - 1 - q, q)
            for u in range(towers):
                v = fbuf[u, :, pl.ds(pl.multiple_of(c * 2 * per, 128), 2 * per)]
                for h in range(2):
                    d = (2 * c + h) * 2 + u
                    feat[d, :, :per] = v[:, h * per:(h + 1) * per]
                    feat[d, :, per:] = flags
                    @pl.when(d != me)
                    def _():
                        feature_copy(d).start()
            return 0
        lax.fori_loop(n * pairs // pool, (n + 1) * pairs // pool, pair, 0)
        return 0
    lax.fori_loop(0, pool, pooled_row, 0)
    fin[me] = feat[me]
    def others(body):
        lax.fori_loop(1, total, lambda k, _: (body(lax.rem(me + k, total)), 0)[1], 0)
    others(lambda d: feature_wait(d).wait_recv())

    got = fin[...].reshape(rows, padded)
    flag = got[:, per:per + 1]
    lower = (lax.broadcasted_iota(jnp.int32, (rows, rows), 1) < lax.broadcasted_iota(jnp.int32, (rows, rows), 0)).astype(BF16)
    index = jnp.dot(lower, jnp.broadcast_to(flag, (rows, 128)), preferred_element_type=F32)[:, :1].astype(jnp.int32)
    hit = (index == lax.broadcasted_iota(jnp.int32, (rows, live), 1)) & (flag.astype(F32) > 0.5)
    spread[...] = hit.astype(F32).astype(BF16)
    pack = lambda v: lax.dot_general(spread[...], v, (((0,), (0,)), ((), ())), preferred_element_type=F32)
    f_ref[...] = pack(got[:, :per]).astype(BF16)
    for c in w_loads:
        c.wait()
    chips = [((k // (place.dims[1] * place.dims[2])), (k // place.dims[2]) % place.dims[1], k % place.dims[2]) for k in range(nb)]
    for k, i in enumerate(chips):
        s[i] = jnp.dot(f_ref[...], w[k], preferred_element_type=F32).astype(BF16)
    size = live // (2 * parts)
    pieces = []
    for n in range(2 * parts):
        half = n % 2
        low = pl.ds(((n // 2) + half * parts) * size, size)
        pieces.append((Sum(place, 2 - half, s.at[:, :, :, low], r1.at[n], t1.at[n], r2.at[n], t2.at[n], r3.at[n],
                           g.at[:, :, :, low], gs.at[n], gr.at[n]), low))
    for piece, _ in pieces:
        piece.send1()
    lax.fori_loop(1, nb, lambda k, _: (cot_copy(k).wait_recv(), 0)[1], 0)
    cots[0] = pack(cgot[...].reshape(rows, cols)).astype(BF16)
    cot_swap = send(cots.at[0], cots.at[1], xs.at[0], xr.at[0], other)
    mine_cols = pl.ds(pl.multiple_of(b * cols, 128), cols)
    mixes = lambda i, j: fmix_ref[i, j:j + 1, mine_cols]
    first = t == 0
    own = jnp.where(first, mixes(0, 0), mixes(1, 1))
    cross = jnp.where(first, mixes(0, 1), mixes(1, 0))
    back = jnp.where(first, mixes(1, 0), mixes(0, 1))
    here = place.at
    def gate_piece(piece, low):
        value, inc = gelu_pair(piece.result() + bias_ref[:, mine_cols])
        gates[0, low, :] = value.astype(BF16)
        d_gate = own * cots[0, low, :].astype(F32) + back * cots[1, low, :].astype(F32)
        g[here[0], here[1], here[2], low, :] = (d_gate * inc).astype(BF16)
        piece.gather1()
    todo = [lambda q, low: q.send2(), lambda q, low: q.send3(), gate_piece]
    for step in range(parts + 2):
        for k in range(3):
            c = step - k
            if 0 <= c < parts:
                if k == 2 and c == 0:
                    cot_swap.wait_recv()
                for piece, low in pieces[2 * c:2 * c + 2]:
                    todo[k](piece, low)
    gate_swap = send(gates.at[0], gates.at[1], xs.at[1], xr.at[1], other)
    for piece, low in pieces[:2]:
        piece.gather2()
    gate_swap.wait_recv()
    gate, cot, gate_other = gates[0].astype(F32), cots[0].astype(F32), gates[1].astype(F32)
    total_rows = [jnp.sum(cot * gate, axis=0, keepdims=True), jnp.sum(cot * gate_other, axis=0, keepdims=True),
                  jnp.sum(g[here[0], here[1], here[2]].astype(F32), axis=0, keepdims=True)]
    wide[me] = jnp.concatenate(total_rows + [jnp.zeros((5, cols), F32)], axis=0)
    def sums_copy(k):
        d = lax.rem(me + k, total)
        return pltpu.make_async_remote_copy(
            src_ref=wide.at[me], dst_ref=wide.at[me], send_sem=ms.at[k], recv_sem=mr.at[k],
            device_id=device(d), device_id_type=MESH_ID)
    def drain(k, _):
        cot_copy(k).wait_send()
        return 0
    lax.fori_loop(1, nb, drain, 0)
    stitched = (own * gate + cross * gate_other).astype(BF16)
    cin[...] = jnp.dot(spread[...], stitched, preferred_element_type=F32).astype(BF16).reshape(cin.shape)
    def stitched_copy(k):
        d = lax.rem(b + k, nb)
        return pltpu.make_async_remote_copy(
            src_ref=cin.at[d], dst_ref=sgot.at[b], send_sem=ss.at[k], recv_sem=sr.at[k],
            device_id=(d, t), device_id_type=MESH_ID)
    lax.fori_loop(1, total, lambda k, _: (sums_copy(k).start(), 0)[1], 0)
    lax.fori_loop(1, nb, lambda k, _: (stitched_copy(k).start(), 0)[1], 0)
    sgot[b] = cin[b]
    for c in range(1, parts):
        for piece, low in pieces[2 * c:2 * c + 2]:
            piece.gather2()
        for piece, low in pieces[2 * c - 2:2 * c]:
            piece.gather3()
    for piece, low in pieces[-2:]:
        piece.gather3()
    for piece, low in pieces:
        piece.arrive()
    acc[...] = jnp.zeros(acc.shape, F32)
    for k, i in enumerate(chips):
        acc[...] += lax.dot_general(g[i], w[k], (((1,), (1,)), ((), ())), preferred_element_type=F32)
    others(lambda d: feature_wait(d).wait_send())
    feat[:, :, :per] = jnp.dot(spread[...], acc[...].astype(BF16), preferred_element_type=F32).astype(BF16).reshape(total, slots, per)
    def grad_copy(k):
        d = lax.rem(me + k, total)
        return pltpu.make_async_remote_copy(
            src_ref=feat.at[d], dst_ref=dm.at[t, b], send_sem=ds.at[k], recv_sem=dr.at[k],
            device_id=device(d), device_id_type=MESH_ID)
    lax.fori_loop(1, total, lambda k, _: (grad_copy(k).start(), 0)[1], 0)
    dm[t, b] = feat[me]
    lax.fori_loop(1, nb, lambda k, _: (stitched_copy(k).wait_recv(), 0)[1], 0)
    for k in range(nb):
        out_ref[0, :, k * cols:(k + 1) * cols] = sgot[k]
    lax.fori_loop(1, total, lambda k, _: (sums_copy(k).wait_recv(), 0)[1], 0)
    for k in range(nb):
        at = slice(k * cols, (k + 1) * cols)
        for u in range(2):
            stitch_ref[u, u:u + 1, at] = wide[2 * k + u, 0:1]
            stitch_ref[u, 1 - u:2 - u, at] = wide[2 * k + u, 1:2]
            fbias_ref[u:u + 1, at] = wide[2 * k + u, 2:3]
    lax.fori_loop(1, total, lambda k, _: (grad_copy(k).wait_recv(), 0)[1], 0)

    for u in range(towers):
        for k in range(nb):
            fbuf[u, :, k * per:(k + 1) * per] = dm[u, k, :, :per]
    z[0] = jnp.zeros(z.shape[1:], F32)
    z[pool + 1] = jnp.zeros(z.shape[1:], F32)
    mixed = [[jnp.zeros((slots, cout), F32)] * 2 for _ in range(2)]
    for i in range(pool):
        z[i + 1, 0] = jnp.zeros(z.shape[2:], F32)
        z[i + 1, pool + 1] = jnp.zeros(z.shape[2:], F32)
        for j in range(pool):
            q = i * pool + j
            dmx = [fbuf[u, :, q * cout:(q + 1) * cout].astype(F32) for u in range(towers)]
            for u in range(towers):
                pu = pooled[q, :, u * cout:(u + 1) * cout]
                for v in range(towers):
                    mixed[v][u] = mixed[v][u] + dmx[v] * pu
                z[i + 1, j + 1, :, u * cout:(u + 1) * cout] = (cmix_ref[0, u][None] * dmx[0] + cmix_ref[1, u][None] * dmx[1]) * (1.0 / 9.0)
    lines = [jnp.concatenate([jnp.sum(mixed[v][u], axis=0, keepdims=True) for u in range(2)], axis=1) for v in range(2)]
    sums_t[...] = jnp.concatenate([jnp.zeros((1, wide_c), F32)] + lines + [jnp.zeros((125, wide_c), F32)], axis=0).T
    cells = side * side
    dpad[0] = jnp.zeros(dpad.shape[1:], BF16)
    dpad[side + 1] = jnp.zeros(dpad.shape[1:], BF16)
    d2[cells:] = jnp.zeros((d2.shape[0] - cells, slots, wide_c), BF16)
    def drow(y, src):
        dpad[y + 1, 0] = jnp.zeros((slots, wide_c), BF16)
        dpad[y + 1, side + 1] = jnp.zeros((slots, wide_c), BF16)
        for x in range(side):
            j = x // 2
            v = src(j + 1) if x % 2 else src(j) + src(j + 1)
            d = (v * slope[y, x].astype(F32)).astype(BF16)
            dpad[y + 1, x + 1] = d
            d2[y * side + x] = d
    def two(i, _):
        drow(2 * i, lambda j: z[i, j] + z[i + 1, j])
        drow(2 * i + 1, lambda j: z[i + 1, j])
        return 0
    lax.fori_loop(0, pool, two, 0)
    drow(side - 1, lambda j: z[pool, j] + z[pool + 1, j])
    block = 256 // slots
    def flip(k, _):
        dt[:, pl.ds(pl.multiple_of(k * 256, 256), 256)] = d2[pl.ds(k * block, block)].reshape(256, wide_c).T
        return 0
    lax.fori_loop(0, d2.shape[0] // block, flip, 0)

    chunks, span = grad_ref.shape[1], grad_ref.shape[-1]
    tail = dt.shape[1] - cells * slots
    give = w.at[0:chunks, 0:cout]
    take = w.at[0:chunks, cout:2 * cout]

    def window(n):
        parts_ = []
        low = n * span
        while low < (n + 1) * span:
            k = low // chan
            if k < 9:
                high = min((n + 1) * span, (k + 1) * chan)
                a, c = k // 3, k % 3
                parts_.append(p[a:a + side, c:c + side, :, low - k * chan:high - k * chan].reshape(cells * slots, high - low))
                low = high
            else:
                parts_.append(jnp.ones((cells * slots, (n + 1) * span - low), BF16))
                low = (n + 1) * span
        win = parts_[0] if len(parts_) == 1 else jnp.concatenate(parts_, axis=1)
        return jnp.concatenate([win, jnp.zeros((tail, span), BF16)], axis=0)

    lots = [Sum(place, 2 - n % 2, cs_.at[n], cr1.at[n], ct1.at[n], cr2.at[n], ct2.at[n], cr3.at[n], grad_ref.at[t, n], ks.at[n], kr.at[n])
            for n in range(chunks)]
    core, share_back = {}, {}

    def compute(n):
        win = window(n)
        def half(u):
            at = pl.ds(pl.multiple_of(u * cout, cout), cout)
            v = jnp.dot(dt[at, :], win, preferred_element_type=F32)
            if n == chunks - 1:
                extra = sums_t[at, :]
                lane = lax.broadcasted_iota(jnp.int32, extra.shape, 1)
                v = jnp.concatenate([v[:, :span - 128], jnp.where(lane == 0, v[:, span - 128:], extra)], axis=1)
            return v
        give[n] = half(1 - t).astype(BF16)
        core[n] = send(give.at[n], take.at[n], hs.at[n, 0], hr.at[n, 0], other)
        keep[n % keep.shape[0]] = half(t)

    def merge(n):
        core[n].wait_recv()
        cs_[n] = (keep[n % keep.shape[0]] + take[n].astype(F32)).astype(BF16).reshape(cs_.shape[1:])
        lots[n].send1()

    def finish(n):
        grad_ref[t, n, here[0], here[1], here[2]] = lots[n].result().astype(BF16)
        lots[n].gather1()

    def share(n):
        lots[n].arrive()
        share_back[n] = send(grad_ref.at[t, n], grad_ref.at[t, n], hs.at[n, 1], hr.at[n, 1], other)

    def xrow(y):
        lhs = jnp.concatenate([dpad[y + 2 - a, 2 - c:2 - c + side, :, u * cout:(u + 1) * cout].reshape(m_rows, cout)
                               for u in range(towers) for a in range(3) for c in range(3)], axis=1)
        rhs = jnp.concatenate([cw[u, (a * 3 + c) * chan:(a * 3 + c + 1) * chan, :]
                               for u in range(towers) for a in range(3) for c in range(3)], axis=1)
        o = lax.dot_general(lhs, rhs, (((1,), (1,)), ((), ())), preferred_element_type=F32).reshape(side, slots, chan)
        for x in range(side):
            for l in range(lanes):
                stage[l, pl.ds(y * pitch + x, slots, stride=side * pitch), :] = o[x, :, l * 128:(l + 1) * 128]

    stores = []
    def flush(q):
        def put(k, _):
            xin[k // side, k % side] = jnp.concatenate(
                [stage[l, pl.ds(pl.multiple_of(k * pitch, pitch), side), :] for l in range(lanes)], axis=1).astype(BF16)
            return 0
        lax.fori_loop(q * crops * side, (q + 1) * crops * side, put, 0, unroll=4)
        c = pltpu.make_async_copy(xin.at[pl.ds(q * crops, crops)], dx_hbm.at[pl.ds(q * crops, crops)], xsem.at[q])
        c.start()
        stores.append(c)

    side_work = [functools.partial(xrow, y) for y in range(side)] + [functools.partial(flush, q) for q in range(groups)]
    work = [merge, lambda n: lots[n].send2(), lambda n: lots[n].send3(), finish,
            lambda n: lots[n].gather2(), lambda n: lots[n].gather3(), share, lambda n: share_back[n].wait_recv()]
    for step in range(chunks + 3 * (len(work) - 1) + 1):
        if step < chunks:
            compute(step)
        if step >= 14 and side_work:
            side_work.pop(0)()
        for k, job in enumerate(work):
            n = step - 1 - 3 * k
            if 0 <= n < chunks:
                job(n)
    for job in side_work:
        job()
    for c in stores:
        c.wait()
    for piece, _ in pieces:
        piece.close()
    cot_swap.wait_send()
    gate_swap.wait_send()
    for n in range(chunks):
        lots[n].close()
        core[n].wait_send()
        share_back[n].wait_send()
    def drain_all(k, _):
        grad_copy(k).wait_send()
        sums_copy(k).wait_send()
        return 0
    lax.fori_loop(1, total, drain_all, 0)
    lax.fori_loop(1, nb, lambda k, _: (stitched_copy(k).wait_send(), 0)[1], 0)


def whole_layer(live_rows, x, cw, cbias, cmix, cot, w, fbias, fmix, nb, parts=2):
    slots, side, _, chan = x.shape
    towers, _, cout = cw.shape
    per, fc = w.shape
    cols = fc // nb
    total = 2 * nb
    rows = total * slots
    live = rows // 2
    pool = (side - 3) // 2 + 1
    padded = per // 128 * 128 + 128
    wide = towers * cout
    d0, d1, d2 = torus(nb)
    size = live // (2 * parts)
    n = 2 * parts
    span = 256
    chunks = (9 * chan + 128) // span
    h = cout // nb
    cells = -(-side * side * slots // 256) * 256 // slots
    V = pl.BlockSpec(memory_space=pltpu.VMEM)
    A = pl.BlockSpec(memory_space=pl.ANY)
    vm = lambda *shape: pltpu.VMEM(shape, BF16)
    vf = lambda *shape: pltpu.VMEM(shape, F32)
    dma = lambda *shape: pltpu.SemaphoreType.DMA(shape)
    shape = jax.ShapeDtypeStruct
    return pl.pallas_call(
        functools.partial(whole_kernel, parts, per),
        out_shape=[shape((1, 2 * slots, fc), BF16), shape(x.shape, BF16), shape((live, per), BF16),
                   shape((d0, d1, d2, live, cols), BF16), shape((towers, chunks, d0, d1, d2, h, span), BF16),
                   shape((2, 2, fc), F32), shape((2, fc), F32)],
        in_specs=[pl.BlockSpec(memory_space=pltpu.SMEM), A, A, V, V, V, A, V, V],
        out_specs=[V, A, V, V, V, V, V],
        scratch_shapes=[
            vm(*x.shape), vm(*cw.shape), vf(chan // 128, slots * side * 16, 128), vf(3, side, slots, wide),
            vm(side + 2, side + 2, slots, chan), vm(side, side, slots, wide), vf(pool * pool, slots, wide),
            vm(towers, slots, nb * per), vm(total, slots, padded), vm(total, slots, padded), vm(towers, nb, slots, padded),
            vm(nb, per, cols), vm(nb, 2 * slots, cols), vm(nb, 2 * slots, cols), vm(nb, 2 * slots, cols), vm(rows, live),
            vm(d0, d1, d2, live, cols), vm(n, d1 - 1, d0, d1, size, cols), vm(n, d0, d1, size, cols),
            vm(n, d1 - 1, d0, size, cols), vm(n, d0, size, cols), vm(n, d0 - 1, size, cols),
            vm(2, live, cols), vm(2, live, cols), vf(total, 8, cols), vf(live, per),
            vf(pool + 2, pool + 2, slots, wide), vm(side + 2, side + 2, slots, wide), vm(cells, slots, wide), vm(wide, cells * slots),
            vf(2, cout, span), vm(chunks, d0, d1, d2, h, span), vm(chunks, d1 - 1, d0, d1, h, span), vm(chunks, d0, d1, h, span),
            vm(chunks, d1 - 1, d0, h, span), vm(chunks, d0, h, span), vm(chunks, d0 - 1, h, span), vf(wide, 128),
            dma(4), pltpu.SemaphoreType.DMA, dma(nb), dma(total), dma(total), dma(nb), dma(nb), dma(2), dma(2), dma(nb), dma(nb),
            dma(total), dma(total), dma(n, hops(nb)), dma(n, hops(nb)), dma(total), dma(total),
            dma(chunks, hops(nb)), dma(chunks, hops(nb)), dma(chunks, 2), dma(chunks, 2)],
        compiler_params=pltpu.CompilerParams(collective_id=1, has_side_effects=True, vmem_limit_bytes=63 * 2**20),
    )(live_rows, x, cw, cbias, cmix, cot, w, fbias, fmix)


def write_kernel(f_ref, g_ref, dw_ref, fc_ref, conv_ref, bias_ref, mix_ref):
    fc_ref[0] = lax.dot_general(f_ref[...], g_ref[0], (((0,), (0,)), ((), ())), preferred_element_type=F32)
    flat = [dw_ref[u, 0].astype(F32).T for u in range(dw_ref.shape[0])]
    half = dw_ref.shape[-1] - 128
    for u, v in enumerate(flat):
        conv_ref[u] = v
        bias_ref[u:u + 1] = v[half:half + 1]
        mix_ref[0, u:u + 1] = v[half + 1:half + 2]
        mix_ref[1, u:u + 1] = v[half + 2:half + 3]


def write_grads(f, g, dw, nb, cols, ktaps):
    live, per = f.shape
    towers, chunks, cout, span = dw.shape
    last = chunks - 1
    shape = jax.ShapeDtypeStruct
    return pl.pallas_call(
        write_kernel,
        grid=(nb,),
        out_shape=[shape((1, per, nb * cols), F32), shape((towers, ktaps, cout), F32), shape((towers, cout), F32), shape((2, towers, cout), F32)],
        in_specs=[pl.BlockSpec((live, per), lambda k: (0, 0)), pl.BlockSpec((1, live, cols), lambda k: (k, 0, 0)),
                  pl.BlockSpec((towers, 1, cout, span), lambda k: (0, jnp.minimum(k, last), 0, 0))],
        out_specs=[pl.BlockSpec((1, per, cols), lambda k: (0, 0, k)),
                   pl.BlockSpec((towers, span, cout), lambda k: (0, jnp.minimum(k, last), 0)),
                   pl.BlockSpec((towers, cout), lambda k: (0, 0)), pl.BlockSpec((2, towers, cout), lambda k: (0, 0, 0))],
        compiler_params=pltpu.CompilerParams(vmem_limit_bytes=32 * 2**20),
    )(f, g, dw)


def shards(crop_pixels, live_rows, conv_weight, conv_bias, stitch_conv, fc_weight, fc_bias, stitch_fc, cotangent):
    slots = crop_pixels.shape[0]
    nb = lax.axis_size("batch")
    fc = fc_weight.shape[2]
    cols = fc // nb
    cin, cout = conv_weight.shape[3:]
    live = slots * nb
    stitched, dx, f, dh, dw, d_stitch_fc, d_fc_bias = whole_layer(
        live_rows, crop_pixels, conv_weight.reshape(2, 9 * cin, cout), conv_bias, stitch_conv, cotangent[0], fc_weight[0], fc_bias, stitch_fc, nb)
    dw = dw.reshape(2, dw.shape[1], cout, dw.shape[-1])
    d_fc_weight, d_kernel, d_conv_bias, d_stitch_conv = write_grads(f, dh.reshape(nb, live, cols), dw, nb, cols, 9 * cin)
    return stitched, dx, d_kernel.reshape(conv_weight.shape), d_conv_bias, d_stitch_conv, d_fc_weight, d_fc_bias, d_stitch_fc


def solution(mesh):
    in_specs = (
        P(("batch", "tower"), None, None, None), P(("batch", "tower")), P(), P(), P(),
        P("tower", "batch", None), P("tower", None), P(), P("tower", "batch", None),
    )
    out_specs = (
        P("tower", "batch", None), P(("batch", "tower"), None, None, None), P(), P(), P(),
        P("tower", "batch", None), P(), P(),
    )
    body = shards if mesh.shape["batch"] == 16 else plain_shards
    return jax.shard_map(body, mesh=mesh, in_specs=in_specs, out_specs=out_specs, check_vma=False)
```

```python
import functools, math
import jax, jax.numpy as jnp
from jax import lax
from jax.experimental import pallas as pl
from jax.experimental.pallas import tpu as pltpu
from jax.sharding import PartitionSpec as P
F32, BF16 = jnp.float32, jnp.bfloat16
CG = math.sqrt(2.0 / math.pi)

def gelu_pair(v):
    sq = v * v
    t = jnp.tanh(v * (CG + (CG * 0.044715) * sq))
    half = 0.5 + 0.5 * t
    value = v * half
    slope = half + value * (1.0 - half) * (2.0 * CG + (6.0 * CG * 0.044715) * sq)
    return value, slope

def conv_fwd_kernel(rows_per, live_ref, x_ref, w_ref, b_ref, mix_ref, feat_ref, pooled_ref, slope_ref, p_ref, stage, act, fbuf):
    slots, side, _, cin = x_ref.shape
    towers, _, cout = w_ref.shape
    pool = (side - 3) // 2 + 1
    pitch = 16
    lanes = cin // 128
    p_ref[0] = jnp.zeros(p_ref.shape[1:], BF16)
    p_ref[side + 1] = jnp.zeros(p_ref.shape[1:], BF16)
    def put(k, _):
        r = k // side
        i = k % side
        v = x_ref[r, i].astype(F32)
        for l in range(lanes):
            stage[l, pl.ds(pl.multiple_of(k * pitch, pitch), side), :] = v[:, l * 128:(l + 1) * 128]
        return 0
    lax.fori_loop(0, slots * side, put, 0, unroll=4)
    def take(i, _):
        p_ref[i + 1, 0] = jnp.zeros((slots, cin), BF16)
        p_ref[i + 1, side + 1] = jnp.zeros((slots, cin), BF16)
        for j in range(side):
            for l in range(lanes):
                v = stage[l, pl.ds(i * pitch + j, slots, stride=side * pitch), :]
                p_ref[i + 1, j + 1, :, l * 128:(l + 1) * 128] = v.astype(BF16)
        return 0
    lax.fori_loop(0, side, take, 0)
    rows = rows_per * side * slots
    def row(y):
        window = jnp.concatenate(
            [p_ref[pl.ds(y + a, rows_per), b:b + side].reshape(rows, cin) for a in range(3) for b in range(3)], axis=1)
        for t in range(towers):
            pre = jnp.dot(window, w_ref[t], preferred_element_type=F32) + b_ref[t][None]
            value, slope = gelu_pair(pre)
            act[pl.ds(y, rows_per), :, :, t * cout:(t + 1) * cout] = value.reshape(rows_per, side, slots, cout)
            slope_ref[pl.ds(y, rows_per), :, :, t * cout:(t + 1) * cout] = slope.astype(BF16).reshape(rows_per, side, slots, cout)
    lax.fori_loop(0, side // rows_per, lambda k, _: (row(k * rows_per), 0)[1], 0)
    for i in range(pool):
        s3 = act[2 * i] + act[2 * i + 1] + act[2 * i + 2]
        for j in range(pool):
            p9 = (s3[2 * j] + s3[2 * j + 1] + s3[2 * j + 2]) * (1.0 / 9.0)
            pooled_ref[i * pool + j] = p9
            for t in range(towers):
                m = mix_ref[t, 0][None] * p9[:, :cout] + mix_ref[t, 1][None] * p9[:, cout:]
                fbuf[t, :, (i * pool + j) * cout:(i * pool + j + 1) * cout] = m.astype(BF16)
    nb = feat_ref.shape[1]
    per = fbuf.shape[2] // nb
    flags = (lax.broadcasted_iota(jnp.int32, (slots, feat_ref.shape[3] - per), 0) < live_ref[0]).astype(F32).astype(BF16)
    for t in range(towers):
        for b in range(nb):
            feat_ref[t, b, :, :per] = fbuf[t, :, b * per:(b + 1) * per]
            feat_ref[t, b, :, per:] = flags

def conv_fwd(live, x, w, bias, mix, nb, rows_per=1):
    slots, side, _, cin = x.shape
    towers, _, _, _, cout = w.shape
    pool = (side - 3) // 2 + 1
    nf = pool * pool * cout
    V = pl.BlockSpec(memory_space=pltpu.VMEM)
    return pl.pallas_call(
        functools.partial(conv_fwd_kernel, rows_per),
        out_shape=[jax.ShapeDtypeStruct((towers, nb, slots, nf // nb // 128 * 128 + 128), BF16),
                   jax.ShapeDtypeStruct((pool * pool, slots, towers * cout), F32),
                   jax.ShapeDtypeStruct((side, side, slots, towers * cout), BF16),
                   jax.ShapeDtypeStruct((side + 2, side + 2, slots, cin), BF16)],
        in_specs=[pl.BlockSpec(memory_space=pltpu.SMEM)] + [V] * 4, out_specs=[V] * 4,
        scratch_shapes=[pltpu.VMEM((cin // 128, slots * side * 16, 128), F32),
                        pltpu.VMEM((side, side, slots, towers * cout), F32),
                        pltpu.VMEM((towers, slots, nf), BF16)],
        compiler_params=pltpu.CompilerParams(vmem_limit_bytes=60 * 2**20),
    )(live, x, w.reshape(towers, 9 * cin, cout), bias, mix)


MESH_ID = pl.DeviceIdType.MESH


def torus(nb):
    return {16: (4, 2, 2), 64: (4, 4, 4)}.get(nb, (nb, 1, 1))


class Place:
    def __init__(self, nb):
        self.dims = torus(nb)
        self.b, self.t = lax.axis_index("batch"), lax.axis_index("tower")
        d0, d1, d2 = self.dims
        self.at = (self.b // (d1 * d2), (self.b // d2) % d1, self.b % d2)

    def peer(self, dim, k):
        c = list(self.at)
        c[dim] = k
        return ((c[0] * self.dims[1] + c[1]) * self.dims[2] + c[2], self.t)


def send(src, dst, ssem, rsem, device):
    copy = pltpu.make_async_remote_copy(src_ref=src, dst_ref=dst, send_sem=ssem, recv_sem=rsem, device_id=device, device_id_type=MESH_ID)
    copy.start()
    return copy


class Sum:
    def __init__(self, place, p, s, r1, t1, r2, t2, r3, g, ssem, rsem):
        self.place, self.p, self.q = place, p, 3 - p
        self.s, self.r1, self.t1, self.r2, self.t2, self.r3, self.g = s, r1, t1, r2, t2, r3, g
        self.ssem, self.rsem = ssem, rsem
        self.sent = []
        self.used = 0

    def pick(self, ref, k):
        return ref.at[:, :, k] if self.p == 2 else ref.at[:, k]

    def post(self, dim, src_of, dst_of):
        n = self.place.dims[dim]
        self.flight = []
        for j in range(1, n):
            k = lax.rem(self.place.at[dim] + j, n)
            i = self.used
            self.used += 1
            self.flight.append(send(src_of(k), dst_of(j - 1), self.ssem.at[i], self.rsem.at[i], self.place.peer(dim, k)))
        self.sent += self.flight

    def arrive(self):
        for c in self.flight:
            c.wait_recv()

    def add(self, mine, got, n):
        v = mine.astype(F32)
        for j in range(n):
            v = v + got[j].astype(F32)
        return v

    def send1(self):
        self.post(self.p, lambda k: self.pick(self.s, k), lambda j: self.r1.at[j])

    def send2(self):
        self.arrive()
        n = self.place.dims[self.p]
        self.t1[...] = self.add(self.pick(self.s, self.place.at[self.p])[...], self.r1, n - 1).astype(BF16)
        self.post(self.q, lambda k: self.t1.at[:, k], lambda j: self.r2.at[j])

    def send3(self):
        self.arrive()
        n = self.place.dims[self.q]
        self.t2[...] = self.add(self.t1[:, self.place.at[self.q]], self.r2, n - 1).astype(BF16)
        self.post(0, lambda k: self.t2.at[k], lambda j: self.r3.at[j])

    def result(self):
        self.arrive()
        return self.add(self.t2[self.place.at[0]], self.r3, self.place.dims[0] - 1)

    def gather1(self):
        mine = self.g.at[self.place.at[0], self.place.at[1], self.place.at[2]]
        self.post(0, lambda k: mine, lambda j: mine)

    def gather2(self):
        self.arrive()
        mine = self.g.at[:, self.place.at[1], self.place.at[2]]
        self.post(self.q, lambda k: mine, lambda j: mine)

    def gather3(self):
        self.arrive()
        mine = self.pick(self.g, self.place.at[self.p])
        self.post(self.p, lambda k: mine, lambda j: mine)

    def close(self):
        for c in self.sent:
            c.wait_send()


def hops(nb):
    return 2 * sum(d - 1 for d in torus(nb))


def conv_bwd_kernel(dm_ref, pooled_ref, slope_ref, p_ref, w_ref, mix_ref, dx_ref, dw_ref, small_ref,
                    fbuf, z, dpad, d2, dt, stage):
    towers, nb, slots, _ = dm_ref.shape
    per = fbuf.shape[2] // nb
    side = slope_ref.shape[0]
    cout = w_ref.shape[2]
    cin = p_ref.shape[3]
    pool = (side - 3) // 2 + 1
    wide = towers * cout
    cells = side * side
    for t in range(towers):
        for b in range(nb):
            fbuf[t, :, b * per:(b + 1) * per] = dm_ref[t, b, :, :per]
    z[0] = jnp.zeros(z.shape[1:], F32)
    z[pool + 1] = jnp.zeros(z.shape[1:], F32)
    acc = [[jnp.zeros((slots, cout), F32)] * 2 for _ in range(2)]
    for i in range(pool):
        z[i + 1, 0] = jnp.zeros(z.shape[2:], F32)
        z[i + 1, pool + 1] = jnp.zeros(z.shape[2:], F32)
        for j in range(pool):
            q = i * pool + j
            dm = [fbuf[t, :, q * cout:(q + 1) * cout].astype(F32) for t in range(towers)]
            for u in range(towers):
                pu = pooled_ref[q, :, u * cout:(u + 1) * cout]
                for t in range(towers):
                    acc[t][u] = acc[t][u] + dm[t] * pu
                z[i + 1, j + 1, :, u * cout:(u + 1) * cout] = (mix_ref[0, u][None] * dm[0] + mix_ref[1, u][None] * dm[1]) * (1.0 / 9.0)
    dpad[0] = jnp.zeros(dpad.shape[1:], BF16)
    dpad[side + 1] = jnp.zeros(dpad.shape[1:], BF16)
    d2[cells:] = jnp.zeros((d2.shape[0] - cells, slots, wide), BF16)
    def drow(y, src):
        dpad[y + 1, 0] = jnp.zeros((slots, wide), BF16)
        dpad[y + 1, side + 1] = jnp.zeros((slots, wide), BF16)
        for x in range(side):
            j = x // 2
            v = src(j + 1) if x % 2 else src(j) + src(j + 1)
            d = (v * slope_ref[y, x].astype(F32)).astype(BF16)
            dpad[y + 1, x + 1] = d
            d2[y * side + x] = d
    def pair(i, _):
        drow(2 * i, lambda j: z[i, j] + z[i + 1, j])
        drow(2 * i + 1, lambda j: z[i + 1, j])
        return 0
    lax.fori_loop(0, pool, pair, 0)
    drow(side - 1, lambda j: z[pool, j] + z[pool + 1, j])
    step = 256 // slots
    def flip(k, _):
        dt[:, pl.ds(pl.multiple_of(k * 256, 256), 256)] = d2[pl.ds(k * step, step)].reshape(256, wide).T
        return 0
    lax.fori_loop(0, d2.shape[0] // step, flip, 0)
    tail = (d2.shape[0] - cells) * slots
    for a in range(3):
        win = jnp.concatenate([p_ref[a:a + side, b:b + side].reshape(cells * slots, cin) for b in range(3)], axis=1)
        win = jnp.concatenate([win, jnp.zeros((tail, 3 * cin), BF16)], axis=0)
        dw_ref[a] = jnp.dot(dt[...], win, preferred_element_type=F32)
    ones = jnp.ones((d2.shape[0] * slots, 128), BF16)
    small_ref[:, 0:128] = jnp.dot(dt[...], ones, preferred_element_type=F32)
    rows = jnp.concatenate([jnp.concatenate([jnp.sum(acc[t][u], axis=0, keepdims=True) for u in range(2)], axis=1) for t in range(2)], axis=0)
    small_ref[:, 128:256] = jnp.concatenate([rows, jnp.zeros((126, wide), F32)], axis=0).T
    pitch = 16
    def xrow(y, n=1):
        lhs = jnp.concatenate([dpad[pl.ds(y + 2 - a, n), 2 - b:2 - b + side, :, t * cout:(t + 1) * cout].reshape(n * side * slots, cout)
                               for t in range(towers) for a in range(3) for b in range(3)], axis=1)
        rhs = jnp.concatenate([w_ref[t, (a * 3 + b) * cin:(a * 3 + b + 1) * cin, :]
                               for t in range(towers) for a in range(3) for b in range(3)], axis=1)
        out = lax.dot_general(lhs, rhs, (((1,), (1,)), ((), ())), preferred_element_type=F32).reshape(n * side, slots, cin)
        for x in range(side):
            for l in range(cin // 128):
                stage[l, pl.ds(y * pitch + x, slots, stride=side * pitch), :] = out[x, :, l * 128:(l + 1) * 128]
    lax.fori_loop(0, side, lambda y, _: (xrow(y), 0)[1], 0)
    def put(k, _):
        r = k // side
        i = k % side
        dx_ref[r, i] = jnp.concatenate([stage[l, pl.ds(pl.multiple_of(k * pitch, pitch), side), :] for l in range(cin // 128)], axis=1).astype(BF16)
        return 0
    lax.fori_loop(0, slots * side, put, 0, unroll=4)

def conv_bwd(dm, pooled, slope, p, w, mix, per):
    towers, nb, slots, _ = dm.shape
    side = slope.shape[0]
    cin = p.shape[3]
    cout = w.shape[4]
    pool = (side - 3) // 2 + 1
    wide = towers * cout
    V = pl.BlockSpec(memory_space=pltpu.VMEM)
    cells = -(-side * side * slots // 256) * 256 // slots
    return pl.pallas_call(
        conv_bwd_kernel,
        out_shape=[jax.ShapeDtypeStruct((slots, side, side, cin), BF16),
                   jax.ShapeDtypeStruct((3, wide, 3 * cin), F32),
                   jax.ShapeDtypeStruct((wide, 256), F32)],
        in_specs=[V] * 6, out_specs=[V] * 3,
        scratch_shapes=[pltpu.VMEM((towers, slots, nb * per), BF16),
                        pltpu.VMEM((pool + 2, pool + 2, slots, wide), F32),
                        pltpu.VMEM((side + 2, side + 2, slots, wide), BF16),
                        pltpu.VMEM((cells, slots, wide), BF16),
                        pltpu.VMEM((wide, cells * slots), BF16),
                        pltpu.VMEM((cin // 128, slots * side * 16, 128), F32)],
        compiler_params=pltpu.CompilerParams(vmem_limit_bytes=62 * 2**20),
    )(dm, pooled, slope, p, w.reshape(towers, 9 * cin, cout), mix)


def swap(block):
    return lax.ppermute(block, "tower", [(0, 1), (1, 0)])


def plain_shards(crop_pixels, live_rows, conv_weight, conv_bias, stitch_conv, fc_weight, fc_bias, stitch_fc, cotangent):
    slots = crop_pixels.shape[0]
    nb = lax.axis_size("batch")
    b, t = lax.axis_index("batch"), lax.axis_index("tower")
    rows = 2 * slots * nb
    live = rows // 2
    fc = fc_weight.shape[2]
    per = fc_weight.shape[1]
    cols = fc // nb
    w = fc_weight[0]
    feat, pooled, slope, padded = conv_fwd(live_rows, crop_pixels, conv_weight, conv_bias, stitch_conv, nb)
    both = ("batch", "tower")
    counts = lax.all_gather(live_rows, both, axis=0, tiled=True)
    got = lax.all_to_all(feat[..., :per].transpose(1, 0, 2, 3).reshape(2 * nb, slots, per), both, 0, 0).reshape(rows, per)
    slot = jnp.arange(rows, dtype=jnp.int32)
    start = jnp.cumsum(counts) - counts
    place = jnp.where(slot % slots < counts[slot // slots], start[slot // slots] + slot % slots, -1)
    spread = (place[:, None] == jnp.arange(live, dtype=jnp.int32)[None]).astype(BF16)
    compact = lambda x: lax.dot_general(spread, x, (((0,), (0,)), ((), ())), preferred_element_type=F32).astype(BF16)
    expand = lambda x: jnp.dot(spread, x, preferred_element_type=F32).astype(BF16)
    f = compact(got)
    part = jnp.dot(f, w, preferred_element_type=F32)
    hidden = lax.psum_scatter(part, "batch", scatter_dimension=1, tiled=True)
    hidden = hidden + lax.dynamic_slice_in_dim(fc_bias[0], b * cols, cols)[None]
    value, slope_fc = gelu_pair(hidden)
    gate = value.astype(BF16)
    cot = compact(lax.all_to_all(cotangent[0].reshape(2 * slots, nb, cols).transpose(1, 0, 2), "batch", 0, 0).reshape(rows, cols))
    gate_other, cot_other = swap(gate).astype(F32), swap(cot).astype(F32)
    gate_own, cot_own = gate.astype(F32), cot.astype(F32)
    mix = lax.dynamic_slice_in_dim(stitch_fc, b * cols, cols, axis=2)
    own = jnp.where(t == 0, mix[0, 0], mix[1, 1])
    cross = jnp.where(t == 0, mix[0, 1], mix[1, 0])
    back = jnp.where(t == 0, mix[1, 0], mix[0, 1])
    stitched = (own[None] * gate_own + cross[None] * gate_other).astype(BF16)
    stitched = lax.all_to_all(expand(stitched).reshape(nb, 2 * slots, cols), "batch", 0, 0)
    stitched = stitched.transpose(1, 0, 2).reshape(1, 2 * slots, fc)
    d_own = jnp.sum(cot_own * gate_own, axis=0)
    d_cross = jnp.sum(cot_own * gate_other, axis=0)
    dh = ((own[None] * cot_own + back[None] * cot_other) * slope_fc).astype(BF16)
    sums = jnp.stack([d_own, d_cross, jnp.sum(dh.astype(F32), axis=0)])
    sums = lax.all_gather(sums, both, axis=0).reshape(nb, 2, 3, cols).transpose(1, 2, 0, 3).reshape(2, 3, fc)
    d_stitch_fc = jnp.stack([sums[0, :2], sums[1, 1::-1]])
    d_fc_bias = sums[:, 2]
    dh = lax.all_gather(dh, "batch", axis=1, tiled=True)
    d_fc_weight = lax.dot_general(f, dh, (((0,), (0,)), ((), ())), preferred_element_type=F32)[None]
    df = lax.dot_general(dh, w, (((1,), (1,)), ((), ())), preferred_element_type=F32).astype(BF16)
    dm = lax.all_to_all(expand(df).reshape(2 * nb, slots, per), both, 0, 0)
    dm = dm.reshape(nb, 2, slots, per).transpose(1, 0, 2, 3)
    dx, dw, small = conv_bwd(dm, pooled, slope, padded, conv_weight, stitch_conv, per)
    dw = lax.psum(dw, both)
    cin, cout = conv_weight.shape[3:]
    dw = dw.reshape(3, 2, cout, 3, cin).transpose(1, 0, 3, 4, 2)
    small = lax.psum(small, both)
    d_conv_bias = small[:, 0].reshape(2, cout)
    d_stitch_conv = small[:, 128:130].T.reshape(2, 2, cout)
    return stitched, dx, dw, d_conv_bias, d_stitch_conv, d_fc_weight, d_fc_bias, d_stitch_fc


def whole_kernel(parts, per, live_ref, x_hbm, cw_hbm, cbias_ref, cmix_ref, cot_ref, w_hbm, bias_ref, fmix_ref,
                 out_ref, dx_hbm, f_ref, g, grad_ref, stitch_ref, fbias_ref,
                 dxv, cw, act, p, slope, pooled, fbuf, feat, fin, dm, w, cin, cgot, sgot, spread,
                 s, r1, t1, r2, t2, r3, gates, cots, wide, acc,
                 z, dpad, d2, dt, keep, cs_, cr1, ct1, cr2, ct2, cr3, sums_t,
                 xsem, lsem, wsem, fs, fr, cs, cr, xs, xr, ss, sr, ms, mr, gs, gr, ds, dr, ks, kr, hs, hr):
    nb = cin.shape[0]
    place = Place(nb)
    b, t = place.b, place.t
    me = b * 2 + t
    total = 2 * nb
    side, _, slots, chan = dxv.shape
    towers, _, cout = cw.shape
    pool = (side - 3) // 2 + 1
    wide_c = towers * cout
    padded = feat.shape[2]
    rows = total * slots
    live = rows // 2
    cols = cin.shape[2]
    other = (b, 1 - t)
    device = lambda d: (d // 2, d % 2)

    load = pltpu.make_async_copy(x_hbm, p.at[pl.ds(1, side), pl.ds(1, side)], xsem.at[0])
    load.start()
    cw_load = pltpu.make_async_copy(cw_hbm, cw, lsem)
    cw_load.start()
    w_loads = [pltpu.make_async_copy(w_hbm.at[:, pl.ds(k * cols, cols)], w.at[k], wsem.at[k]) for k in range(nb)]
    for c in w_loads:
        c.start()
    bar = pltpu.get_barrier_semaphore()
    def hail(k, _):
        pl.semaphore_signal(bar, inc=1, device_id=device(lax.rem(me + k, total)), device_id_type=MESH_ID)
        return 0
    lax.fori_loop(1, total, hail, 0)
    for k in range(nb):
        cin[k] = cot_ref[:, k * cols:(k + 1) * cols]
    cgot[b] = cin[b]

    p[0] = jnp.zeros(p.shape[1:], BF16)
    p[side + 1] = jnp.zeros(p.shape[1:], BF16)
    for i in range(side):
        p[i + 1, 0] = jnp.zeros((slots, chan), BF16)
        p[i + 1, side + 1] = jnp.zeros((slots, chan), BF16)

    pl.semaphore_wait(bar, total - 1)
    def cot_copy(k):
        d = lax.rem(b + k, nb)
        return pltpu.make_async_remote_copy(
            src_ref=cin.at[d], dst_ref=cgot.at[b], send_sem=cs.at[k], recv_sem=cr.at[k],
            device_id=(d, t), device_id_type=MESH_ID)
    lax.fori_loop(1, nb, lambda k, _: (cot_copy(k).start(), 0)[1], 0)

    load.wait()
    cw_load.wait()
    turn = place.at[0] * 2 < place.dims[0]
    flags = (lax.broadcasted_iota(jnp.int32, (slots, padded - per), 0) < live_ref[0]).astype(F32).astype(BF16)
    m_rows = side * slots
    def conv_row(k):
        y = jnp.where(turn, side - 1 - k, k)
        window = jnp.concatenate([p[y + a, c:c + side].reshape(m_rows, chan) for a in range(3) for c in range(3)], axis=1)
        for u in range(towers):
            pre = jnp.dot(window, cw[u], preferred_element_type=F32) + cbias_ref[u][None]
            value, inc = gelu_pair(pre)
            act[lax.rem(k, 3), :, :, u * cout:(u + 1) * cout] = value.reshape(side, slots, cout)
            slope[y, :, :, u * cout:(u + 1) * cout] = inc.astype(slope.dtype).reshape(side, slots, cout)
    def feature_copy(d):
        return pltpu.make_async_remote_copy(
            src_ref=feat.at[d], dst_ref=fin.at[me], send_sem=fs.at[d], recv_sem=fr.at[me],
            device_id=device(d), device_id_type=MESH_ID)
    def feature_wait(d):
        return pltpu.make_async_remote_copy(
            src_ref=feat.at[d], dst_ref=fin.at[d], send_sem=fs.at[d], recv_sem=fr.at[d],
            device_id=device(d), device_id_type=MESH_ID)
    pairs = nb // 2
    conv_row(0)
    def pooled_row(n, _):
        lax.fori_loop(2 * n + 1, 2 * n + 3, lambda k, _: (conv_row(k), 0)[1], 0)
        i = jnp.where(turn, pool - 1 - n, n)
        s3 = act[0] + act[1] + act[2]
        for j in range(pool):
            p9 = (s3[2 * j] + s3[2 * j + 1] + s3[2 * j + 2]) * (1.0 / 9.0)
            pooled[i * pool + j] = p9
            at = pl.ds(pl.multiple_of((i * pool + j) * cout, cout), cout)
            for u in range(towers):
                m = cmix_ref[u, 0][None] * p9[:, :cout] + cmix_ref[u, 1][None] * p9[:, cout:]
                fbuf[u, :, at] = m.astype(BF16)
        def pair(q, _):
            c = jnp.where(turn, pairs - 1 - q, q)
            for u in range(towers):
                v = fbuf[u, :, pl.ds(pl.multiple_of(c * 2 * per, 128), 2 * per)]
                for h in range(2):
                    d = (2 * c + h) * 2 + u
                    feat[d, :, :per] = v[:, h * per:(h + 1) * per]
                    feat[d, :, per:] = flags
                    @pl.when(d != me)
                    def _():
                        feature_copy(d).start()
            return 0
        lax.fori_loop(n * pairs // pool, (n + 1) * pairs // pool, pair, 0)
        return 0
    lax.fori_loop(0, pool, pooled_row, 0)
    fin[me] = feat[me]
    def others(body):
        lax.fori_loop(1, total, lambda k, _: (body(lax.rem(me + k, total)), 0)[1], 0)
    others(lambda d: feature_wait(d).wait_recv())

    got = fin[...].reshape(rows, padded)
    flag = got[:, per:per + 1]
    lower = (lax.broadcasted_iota(jnp.int32, (rows, rows), 1) < lax.broadcasted_iota(jnp.int32, (rows, rows), 0)).astype(BF16)
    index = jnp.dot(lower, jnp.broadcast_to(flag, (rows, 128)), preferred_element_type=F32)[:, :1].astype(jnp.int32)
    hit = (index == lax.broadcasted_iota(jnp.int32, (rows, live), 1)) & (flag.astype(F32) > 0.5)
    spread[...] = hit.astype(F32).astype(BF16)
    pack = lambda v: lax.dot_general(spread[...], v, (((0,), (0,)), ((), ())), preferred_element_type=F32)
    f = pack(got[:, :per]).astype(BF16)
    for c in w_loads:
        c.wait()
    chips = [((k // (place.dims[1] * place.dims[2])), (k // place.dims[2]) % place.dims[1], k % place.dims[2]) for k in range(nb)]
    for k, i in enumerate(chips):
        s[i] = jnp.dot(f, w[k], preferred_element_type=F32).astype(BF16)
    size = live // (2 * parts)
    pieces = []
    for n in range(2 * parts):
        half = n % 2
        low = pl.ds(((n // 2) + half * parts) * size, size)
        pieces.append((Sum(place, 2 - half, s.at[:, :, :, low], r1.at[n], t1.at[n], r2.at[n], t2.at[n], r3.at[n],
                           g.at[:, :, :, low], gs.at[n], gr.at[n]), low))
    for piece, _ in pieces:
        piece.send1()
    f_ref[...] = f.T
    lax.fori_loop(1, nb, lambda k, _: (cot_copy(k).wait_recv(), 0)[1], 0)
    cots[0] = pack(cgot[...].reshape(rows, cols)).astype(BF16)
    cot_swap = send(cots.at[0], cots.at[1], xs.at[0], xr.at[0], other)
    mine_cols = pl.ds(pl.multiple_of(b * cols, 128), cols)
    mixes = lambda i, j: fmix_ref[i, j:j + 1, mine_cols]
    first = t == 0
    own = jnp.where(first, mixes(0, 0), mixes(1, 1))
    cross = jnp.where(first, mixes(0, 1), mixes(1, 0))
    back = jnp.where(first, mixes(1, 0), mixes(0, 1))
    here = place.at
    def gate_piece(piece, low):
        value, inc = gelu_pair(piece.result() + bias_ref[:, mine_cols])
        gates[0, low, :] = value.astype(BF16)
        d_gate = own * cots[0, low, :].astype(F32) + back * cots[1, low, :].astype(F32)
        g[here[0], here[1], here[2], low, :] = (d_gate * inc).astype(BF16)
        piece.gather1()
    todo = [lambda q, low: q.send2(), lambda q, low: q.send3(), gate_piece]
    for step in range(parts + 2):
        for k in range(3):
            c = step - k
            if 0 <= c < parts:
                if k == 2 and c == 0:
                    cot_swap.wait_recv()
                for piece, low in pieces[2 * c:2 * c + 2]:
                    todo[k](piece, low)
    gate_swap = send(gates.at[0], gates.at[1], xs.at[1], xr.at[1], other)
    for piece, low in pieces[:2]:
        piece.gather2()
    gate_swap.wait_recv()
    gate, cot, gate_other = gates[0].astype(F32), cots[0].astype(F32), gates[1].astype(F32)
    total_rows = [jnp.sum(cot * gate, axis=0, keepdims=True), jnp.sum(cot * gate_other, axis=0, keepdims=True),
                  jnp.sum(g[here[0], here[1], here[2]].astype(F32), axis=0, keepdims=True)]
    wide[me] = jnp.concatenate(total_rows + [jnp.zeros((5, cols), F32)], axis=0)
    def sums_copy(k):
        d = lax.rem(me + k, total)
        return pltpu.make_async_remote_copy(
            src_ref=wide.at[me], dst_ref=wide.at[me], send_sem=ms.at[k], recv_sem=mr.at[k],
            device_id=device(d), device_id_type=MESH_ID)
    def drain(k, _):
        cot_copy(k).wait_send()
        return 0
    lax.fori_loop(1, nb, drain, 0)
    stitched = (own * gate + cross * gate_other).astype(BF16)
    cin[...] = jnp.dot(spread[...], stitched, preferred_element_type=F32).astype(BF16).reshape(cin.shape)
    def stitched_copy(k):
        d = lax.rem(b + k, nb)
        return pltpu.make_async_remote_copy(
            src_ref=cin.at[d], dst_ref=sgot.at[b], send_sem=ss.at[k], recv_sem=sr.at[k],
            device_id=(d, t), device_id_type=MESH_ID)
    lax.fori_loop(1, total, lambda k, _: (sums_copy(k).start(), 0)[1], 0)
    lax.fori_loop(1, nb, lambda k, _: (stitched_copy(k).start(), 0)[1], 0)
    sgot[b] = cin[b]
    for c in range(1, parts):
        for piece, low in pieces[2 * c:2 * c + 2]:
            piece.gather2()
        for piece, low in pieces[2 * c - 2:2 * c]:
            piece.gather3()
    for piece, low in pieces[-2:]:
        piece.gather3()
    for piece, low in pieces:
        piece.arrive()
    acc[...] = jnp.zeros(acc.shape, F32)
    for k, i in enumerate(chips):
        acc[...] += lax.dot_general(g[i], w[k], (((1,), (1,)), ((), ())), preferred_element_type=F32)
    others(lambda d: feature_wait(d).wait_send())
    feat[:, :, :per] = jnp.dot(spread[...], acc[...].astype(BF16), preferred_element_type=F32).astype(BF16).reshape(total, slots, per)
    def grad_copy(k):
        d = lax.rem(me + k, total)
        return pltpu.make_async_remote_copy(
            src_ref=feat.at[d], dst_ref=dm.at[t, b], send_sem=ds.at[k], recv_sem=dr.at[k],
            device_id=device(d), device_id_type=MESH_ID)
    lax.fori_loop(1, total, lambda k, _: (grad_copy(k).start(), 0)[1], 0)
    dm[t, b] = feat[me]
    lax.fori_loop(1, nb, lambda k, _: (stitched_copy(k).wait_recv(), 0)[1], 0)
    for k in range(nb):
        out_ref[0, :, k * cols:(k + 1) * cols] = sgot[k]
    lax.fori_loop(1, total, lambda k, _: (sums_copy(k).wait_recv(), 0)[1], 0)
    for k in range(nb):
        at = slice(k * cols, (k + 1) * cols)
        for u in range(2):
            stitch_ref[u, u:u + 1, at] = wide[2 * k + u, 0:1]
            stitch_ref[u, 1 - u:2 - u, at] = wide[2 * k + u, 1:2]
            fbias_ref[u:u + 1, at] = wide[2 * k + u, 2:3]
    lax.fori_loop(1, total, lambda k, _: (grad_copy(k).wait_recv(), 0)[1], 0)

    for u in range(towers):
        for k in range(nb):
            fbuf[u, :, k * per:(k + 1) * per] = dm[u, k, :, :per]
    z[0] = jnp.zeros(z.shape[1:], F32)
    z[pool + 1] = jnp.zeros(z.shape[1:], F32)
    mixed = [[jnp.zeros((slots, cout), F32)] * 2 for _ in range(2)]
    for i in range(pool):
        z[i + 1, 0] = jnp.zeros(z.shape[2:], F32)
        z[i + 1, pool + 1] = jnp.zeros(z.shape[2:], F32)
        for j in range(pool):
            q = i * pool + j
            dmx = [fbuf[u, :, q * cout:(q + 1) * cout].astype(F32) for u in range(towers)]
            for u in range(towers):
                pu = pooled[q, :, u * cout:(u + 1) * cout]
                for v in range(towers):
                    mixed[v][u] = mixed[v][u] + dmx[v] * pu
                z[i + 1, j + 1, :, u * cout:(u + 1) * cout] = (cmix_ref[0, u][None] * dmx[0] + cmix_ref[1, u][None] * dmx[1]) * (1.0 / 9.0)
    lines = [jnp.concatenate([jnp.sum(mixed[v][u], axis=0, keepdims=True) for u in range(2)], axis=1) for v in range(2)]
    sums_t[...] = jnp.concatenate([jnp.zeros((1, wide_c), F32)] + lines + [jnp.zeros((125, wide_c), F32)], axis=0).T
    cells = side * side
    dpad[0] = jnp.zeros(dpad.shape[1:], BF16)
    dpad[side + 1] = jnp.zeros(dpad.shape[1:], BF16)
    d2[cells:] = jnp.zeros((d2.shape[0] - cells, slots, wide_c), BF16)
    def drow(y, src):
        dpad[y + 1, 0] = jnp.zeros((slots, wide_c), BF16)
        dpad[y + 1, side + 1] = jnp.zeros((slots, wide_c), BF16)
        for x in range(side):
            j = x // 2
            v = src(j + 1) if x % 2 else src(j) + src(j + 1)
            d = (v * slope[y, x].astype(F32)).astype(BF16)
            dpad[y + 1, x + 1] = d
            d2[y * side + x] = d
    def two(i, _):
        drow(2 * i, lambda j: z[i, j] + z[i + 1, j])
        drow(2 * i + 1, lambda j: z[i + 1, j])
        return 0
    lax.fori_loop(0, pool, two, 0)
    drow(side - 1, lambda j: z[pool, j] + z[pool + 1, j])
    block = 256 // slots
    def flip(k, _):
        dt[:, pl.ds(pl.multiple_of(k * 256, 256), 256)] = d2[pl.ds(k * block, block)].reshape(256, wide_c).T
        return 0
    lax.fori_loop(0, d2.shape[0] // block, flip, 0)

    chunks, span = grad_ref.shape[1], grad_ref.shape[-1]
    tail = dt.shape[1] - cells * slots
    give = w.at[0:chunks, 0:cout]
    take = w.at[0:chunks, cout:2 * cout]

    def window(n):
        parts_ = []
        low = n * span
        while low < (n + 1) * span:
            k = low // chan
            if k < 9:
                high = min((n + 1) * span, (k + 1) * chan)
                a, c = k // 3, k % 3
                parts_.append(p[a:a + side, c:c + side, :, low - k * chan:high - k * chan].reshape(cells * slots, high - low))
                low = high
            else:
                parts_.append(jnp.ones((cells * slots, (n + 1) * span - low), BF16))
                low = (n + 1) * span
        win = parts_[0] if len(parts_) == 1 else jnp.concatenate(parts_, axis=1)
        return jnp.concatenate([win, jnp.zeros((tail, span), BF16)], axis=0)

    lots = [Sum(place, 2 - n % 2, cs_.at[n], cr1.at[n], ct1.at[n], cr2.at[n], ct2.at[n], cr3.at[n], grad_ref.at[t, n], ks.at[n], kr.at[n])
            for n in range(chunks)]
    core, share_back = {}, {}

    def compute(n):
        win = window(n)
        def half(u):
            at = pl.ds(pl.multiple_of(u * cout, cout), cout)
            v = jnp.dot(dt[at, :], win, preferred_element_type=F32)
            if n == chunks - 1:
                extra = sums_t[at, :]
                lane = lax.broadcasted_iota(jnp.int32, extra.shape, 1)
                v = jnp.concatenate([v[:, :span - 128], jnp.where(lane == 0, v[:, span - 128:], extra)], axis=1)
            return v
        give[n] = half(1 - t).astype(BF16)
        core[n] = send(give.at[n], take.at[n], hs.at[n, 0], hr.at[n, 0], other)
        keep[n % keep.shape[0]] = half(t)

    def merge(n):
        core[n].wait_recv()
        cs_[n] = (keep[n % keep.shape[0]] + take[n].astype(F32)).astype(BF16).reshape(cs_.shape[1:])
        lots[n].send1()

    def finish(n):
        grad_ref[t, n, here[0], here[1], here[2]] = lots[n].result().astype(BF16)
        lots[n].gather1()

    def share(n):
        lots[n].arrive()
        share_back[n] = send(grad_ref.at[t, n], grad_ref.at[t, n], hs.at[n, 1], hr.at[n, 1], other)

    def xrow(y):
        lhs = jnp.concatenate([dpad[y + 2 - a, 2 - c:2 - c + side, :, u * cout:(u + 1) * cout].reshape(m_rows, cout)
                               for u in range(towers) for a in range(3) for c in range(3)], axis=1)
        rhs = jnp.concatenate([cw[u, (a * 3 + c) * chan:(a * 3 + c + 1) * chan, :]
                               for u in range(towers) for a in range(3) for c in range(3)], axis=1)
        o = lax.dot_general(lhs, rhs, (((1,), (1,)), ((), ())), preferred_element_type=F32).reshape(side, slots, chan)
        dxv[y] = o.astype(BF16)
        c = pltpu.make_async_copy(dxv.at[y], dx_hbm.at[y], xsem.at[y])
        c.start()
        stores.append(c)

    stores = []
    side_work = [functools.partial(xrow, y) for y in range(side)]
    work = [merge, lambda n: lots[n].send2(), lambda n: lots[n].send3(), finish,
            lambda n: lots[n].gather2(), lambda n: lots[n].gather3(), share, lambda n: share_back[n].wait_recv()]
    for step in range(chunks + 3 * (len(work) - 1) + 1):
        if step < chunks:
            compute(step)
        if step >= 14 and side_work:
            side_work.pop(0)()
        for k, job in enumerate(work):
            n = step - 1 - 3 * k
            if 0 <= n < chunks:
                job(n)
    for job in side_work:
        job()
    for c in stores:
        c.wait()
    for piece, _ in pieces:
        piece.close()
    cot_swap.wait_send()
    gate_swap.wait_send()
    for n in range(chunks):
        lots[n].close()
        core[n].wait_send()
        share_back[n].wait_send()
    def drain_all(k, _):
        grad_copy(k).wait_send()
        sums_copy(k).wait_send()
        return 0
    lax.fori_loop(1, total, drain_all, 0)
    lax.fori_loop(1, nb, lambda k, _: (stitched_copy(k).wait_send(), 0)[1], 0)


def whole_layer(live_rows, x, cw, cbias, cmix, cot, w, fbias, fmix, nb, parts=2):
    side, _, slots, chan = x.shape
    towers, _, cout = cw.shape
    per, fc = w.shape
    cols = fc // nb
    total = 2 * nb
    rows = total * slots
    live = rows // 2
    pool = (side - 3) // 2 + 1
    padded = per // 128 * 128 + 128
    wide = towers * cout
    d0, d1, d2 = torus(nb)
    size = live // (2 * parts)
    n = 2 * parts
    span = 256
    chunks = (9 * chan + 128) // span
    h = cout // nb
    cells = -(-side * side * slots // 256) * 256 // slots
    V = pl.BlockSpec(memory_space=pltpu.VMEM)
    A = pl.BlockSpec(memory_space=pl.ANY)
    vm = lambda *shape: pltpu.VMEM(shape, BF16)
    vf = lambda *shape: pltpu.VMEM(shape, F32)
    dma = lambda *shape: pltpu.SemaphoreType.DMA(shape)
    shape = jax.ShapeDtypeStruct
    return pl.pallas_call(
        functools.partial(whole_kernel, parts, per),
        out_shape=[shape((1, 2 * slots, fc), BF16), shape(x.shape, BF16), shape((per, live), BF16),
                   shape((d0, d1, d2, live, cols), BF16), shape((towers, chunks, d0, d1, d2, h, span), BF16),
                   shape((2, 2, fc), F32), shape((2, fc), F32)],
        in_specs=[pl.BlockSpec(memory_space=pltpu.SMEM), A, A, V, V, V, A, V, V],
        out_specs=[V, A, V, V, V, V, V],
        scratch_shapes=[
            vm(*x.shape), vm(*cw.shape), vf(3, side, slots, wide),
            vm(side + 2, side + 2, slots, chan), vf(side, side, slots, wide), vf(pool * pool, slots, wide),
            vm(towers, slots, nb * per), vm(total, slots, padded), vm(total, slots, padded), vm(towers, nb, slots, padded),
            vm(nb, per, cols), vm(nb, 2 * slots, cols), vm(nb, 2 * slots, cols), vm(nb, 2 * slots, cols), vm(rows, live),
            vm(d0, d1, d2, live, cols), vm(n, d1 - 1, d0, d1, size, cols), vm(n, d0, d1, size, cols),
            vm(n, d1 - 1, d0, size, cols), vm(n, d0, size, cols), vm(n, d0 - 1, size, cols),
            vm(2, live, cols), vm(2, live, cols), vf(total, 8, cols), vf(live, per),
            vf(pool + 2, pool + 2, slots, wide), vm(side + 2, side + 2, slots, wide), vm(cells, slots, wide), vm(wide, cells * slots),
            vf(2, cout, span), vm(chunks, d0, d1, d2, h, span), vm(chunks, d1 - 1, d0, d1, h, span), vm(chunks, d0, d1, h, span),
            vm(chunks, d1 - 1, d0, h, span), vm(chunks, d0, h, span), vm(chunks, d0 - 1, h, span), vf(wide, 128),
            dma(side), pltpu.SemaphoreType.DMA, dma(nb), dma(total), dma(total), dma(nb), dma(nb), dma(2), dma(2), dma(nb), dma(nb),
            dma(total), dma(total), dma(n, hops(nb)), dma(n, hops(nb)), dma(total), dma(total),
            dma(chunks, hops(nb)), dma(chunks, hops(nb)), dma(chunks, 2), dma(chunks, 2)],
        compiler_params=pltpu.CompilerParams(collective_id=1, has_side_effects=True, vmem_limit_bytes=63 * 2**20),
    )(live_rows, x, cw, cbias, cmix, cot, w, fbias, fmix)


def write_kernel(f_ref, g_ref, dw_ref, st_ref, fs_ref, fb_ref, fc_ref, conv_ref, bias_ref, mix_ref, st_out, fs_out, fb_out):
    cols = g_ref.shape[2]
    for i in range(g_ref.shape[0]):
        fc_ref[0, :, i * cols:(i + 1) * cols] = jnp.dot(f_ref[...], g_ref[i], preferred_element_type=F32)
    flat = [jnp.concatenate([dw_ref[u, k].T for k in range(dw_ref.shape[1])], axis=0).astype(F32) for u in range(dw_ref.shape[0])]
    half = flat[0].shape[0] - 128
    for u, v in enumerate(flat):
        conv_ref[u] = v
        bias_ref[u:u + 1] = v[half:half + 1]
        mix_ref[0, u:u + 1] = v[half + 1:half + 2]
        mix_ref[1, u:u + 1] = v[half + 2:half + 3]
    st_out[...] = st_ref[...]
    fs_out[...] = fs_ref[...]
    fb_out[...] = fb_ref[...]


def write_grads(f, g, dw, stitched, d_stitch, d_bias, nb, cols, ktaps):
    per, live = f.shape
    towers, chunks, cout, span = dw.shape
    group = 512 // span
    last = chunks // group - 1
    fold = 512 // cols
    shape = jax.ShapeDtypeStruct
    fixed = lambda v: pl.BlockSpec(v.shape, lambda k: (0,) * v.ndim)
    small = [stitched, d_stitch, d_bias]
    return pl.pallas_call(
        write_kernel,
        grid=(nb // fold,),
        out_shape=[shape((1, per, nb * cols), F32), shape((towers, ktaps, cout), F32), shape((towers, cout), F32),
                   shape((2, towers, cout), F32)] + [shape(v.shape, v.dtype) for v in small],
        in_specs=[pl.BlockSpec((per, live), lambda k: (0, 0)), pl.BlockSpec((fold, live, cols), lambda k: (k, 0, 0)),
                  pl.BlockSpec((towers, group, cout, span), lambda k: (0, jnp.minimum(k, last), 0, 0))] + [fixed(v) for v in small],
        out_specs=[pl.BlockSpec((1, per, fold * cols), lambda k: (0, 0, k)),
                   pl.BlockSpec((towers, group * span, cout), lambda k: (0, jnp.minimum(k, last), 0)),
                   pl.BlockSpec((towers, cout), lambda k: (0, 0)), pl.BlockSpec((2, towers, cout), lambda k: (0, 0, 0))] + [fixed(v) for v in small],
        compiler_params=pltpu.CompilerParams(vmem_limit_bytes=60 * 2**20),
    )(f, g, dw, *small)


def shards(crop_pixels, live_rows, conv_weight, conv_bias, stitch_conv, fc_weight, fc_bias, stitch_fc, cotangent):
    slots = crop_pixels.shape[0]
    nb = lax.axis_size("batch")
    fc = fc_weight.shape[2]
    cols = fc // nb
    cin, cout = conv_weight.shape[3:]
    live = slots * nb
    stitched, dx, f, dh, dw, d_stitch_fc, d_fc_bias = whole_layer(
        live_rows, crop_pixels.transpose(1, 2, 0, 3), conv_weight.reshape(2, 9 * cin, cout), conv_bias, stitch_conv, cotangent[0], fc_weight[0], fc_bias, stitch_fc, nb)
    dw = dw.reshape(2, dw.shape[1], cout, dw.shape[-1])
    d_fc_weight, d_kernel, d_conv_bias, d_stitch_conv, stitched, d_stitch_fc, d_fc_bias = write_grads(
        f, dh.reshape(nb, live, cols), dw, stitched, d_stitch_fc, d_fc_bias, nb, cols, 9 * cin)
    return stitched, dx.transpose(2, 0, 1, 3), d_kernel.reshape(conv_weight.shape), d_conv_bias, d_stitch_conv, d_fc_weight, d_fc_bias, d_stitch_fc


def solution(mesh):
    in_specs = (
        P(("batch", "tower"), None, None, None), P(("batch", "tower")), P(), P(), P(),
        P("tower", "batch", None), P("tower", None), P(), P("tower", "batch", None),
    )
    out_specs = (
        P("tower", "batch", None), P(("batch", "tower"), None, None, None), P(), P(), P(),
        P("tower", "batch", None), P(), P(),
    )
    body = shards if mesh.shape["batch"] == 16 else plain_shards
    return jax.shard_map(body, mesh=mesh, in_specs=in_specs, out_specs=out_specs, check_vma=False)
```

```python
import functools, math
import jax, jax.numpy as jnp
from jax import lax
from jax.experimental import pallas as pl
from jax.experimental.pallas import tpu as pltpu
from jax.sharding import PartitionSpec as P
F32, BF16 = jnp.float32, jnp.bfloat16
CG = math.sqrt(2.0 / math.pi)

def gelu_pair(v):
    sq = v * v
    t = jnp.tanh(v * (CG + (CG * 0.044715) * sq))
    half = 0.5 + 0.5 * t
    value = v * half
    slope = half + value * (1.0 - half) * (2.0 * CG + (6.0 * CG * 0.044715) * sq)
    return value, slope

def conv_fwd_kernel(rows_per, live_ref, x_ref, w_ref, b_ref, mix_ref, feat_ref, pooled_ref, slope_ref, p_ref, stage, act, fbuf):
    slots, side, _, cin = x_ref.shape
    towers, _, cout = w_ref.shape
    pool = (side - 3) // 2 + 1
    pitch = 16
    lanes = cin // 128
    p_ref[0] = jnp.zeros(p_ref.shape[1:], BF16)
    p_ref[side + 1] = jnp.zeros(p_ref.shape[1:], BF16)
    def put(k, _):
        r = k // side
        i = k % side
        v = x_ref[r, i].astype(F32)
        for l in range(lanes):
            stage[l, pl.ds(pl.multiple_of(k * pitch, pitch), side), :] = v[:, l * 128:(l + 1) * 128]
        return 0
    lax.fori_loop(0, slots * side, put, 0, unroll=4)
    def take(i, _):
        p_ref[i + 1, 0] = jnp.zeros((slots, cin), BF16)
        p_ref[i + 1, side + 1] = jnp.zeros((slots, cin), BF16)
        for j in range(side):
            for l in range(lanes):
                v = stage[l, pl.ds(i * pitch + j, slots, stride=side * pitch), :]
                p_ref[i + 1, j + 1, :, l * 128:(l + 1) * 128] = v.astype(BF16)
        return 0
    lax.fori_loop(0, side, take, 0)
    rows = rows_per * side * slots
    def row(y):
        window = jnp.concatenate(
            [p_ref[pl.ds(y + a, rows_per), b:b + side].reshape(rows, cin) for a in range(3) for b in range(3)], axis=1)
        for t in range(towers):
            pre = jnp.dot(window, w_ref[t], preferred_element_type=F32) + b_ref[t][None]
            value, slope = gelu_pair(pre)
            act[pl.ds(y, rows_per), :, :, t * cout:(t + 1) * cout] = value.reshape(rows_per, side, slots, cout)
            slope_ref[pl.ds(y, rows_per), :, :, t * cout:(t + 1) * cout] = slope.astype(BF16).reshape(rows_per, side, slots, cout)
    lax.fori_loop(0, side // rows_per, lambda k, _: (row(k * rows_per), 0)[1], 0)
    for i in range(pool):
        s3 = act[2 * i] + act[2 * i + 1] + act[2 * i + 2]
        for j in range(pool):
            p9 = (s3[2 * j] + s3[2 * j + 1] + s3[2 * j + 2]) * (1.0 / 9.0)
            pooled_ref[i * pool + j] = p9
            for t in range(towers):
                m = mix_ref[t, 0][None] * p9[:, :cout] + mix_ref[t, 1][None] * p9[:, cout:]
                fbuf[t, :, (i * pool + j) * cout:(i * pool + j + 1) * cout] = m.astype(BF16)
    nb = feat_ref.shape[1]
    per = fbuf.shape[2] // nb
    flags = (lax.broadcasted_iota(jnp.int32, (slots, feat_ref.shape[3] - per), 0) < live_ref[0]).astype(F32).astype(BF16)
    for t in range(towers):
        for b in range(nb):
            feat_ref[t, b, :, :per] = fbuf[t, :, b * per:(b + 1) * per]
            feat_ref[t, b, :, per:] = flags

def conv_fwd(live, x, w, bias, mix, nb, rows_per=1):
    slots, side, _, cin = x.shape
    towers, _, _, _, cout = w.shape
    pool = (side - 3) // 2 + 1
    nf = pool * pool * cout
    V = pl.BlockSpec(memory_space=pltpu.VMEM)
    return pl.pallas_call(
        functools.partial(conv_fwd_kernel, rows_per),
        out_shape=[jax.ShapeDtypeStruct((towers, nb, slots, nf // nb // 128 * 128 + 128), BF16),
                   jax.ShapeDtypeStruct((pool * pool, slots, towers * cout), F32),
                   jax.ShapeDtypeStruct((side, side, slots, towers * cout), BF16),
                   jax.ShapeDtypeStruct((side + 2, side + 2, slots, cin), BF16)],
        in_specs=[pl.BlockSpec(memory_space=pltpu.SMEM)] + [V] * 4, out_specs=[V] * 4,
        scratch_shapes=[pltpu.VMEM((cin // 128, slots * side * 16, 128), F32),
                        pltpu.VMEM((side, side, slots, towers * cout), F32),
                        pltpu.VMEM((towers, slots, nf), BF16)],
        compiler_params=pltpu.CompilerParams(vmem_limit_bytes=60 * 2**20),
    )(live, x, w.reshape(towers, 9 * cin, cout), bias, mix)


MESH_ID = pl.DeviceIdType.MESH


def torus(nb):
    return {16: (4, 2, 2), 64: (4, 4, 4)}.get(nb, (nb, 1, 1))


class Place:
    def __init__(self, nb):
        self.dims = torus(nb)
        self.b, self.t = lax.axis_index("batch"), lax.axis_index("tower")
        d0, d1, d2 = self.dims
        self.at = (self.b // (d1 * d2), (self.b // d2) % d1, self.b % d2)

    def peer(self, dim, k):
        c = list(self.at)
        c[dim] = k
        return ((c[0] * self.dims[1] + c[1]) * self.dims[2] + c[2], self.t)


def send(src, dst, ssem, rsem, device):
    copy = pltpu.make_async_remote_copy(src_ref=src, dst_ref=dst, send_sem=ssem, recv_sem=rsem, device_id=device, device_id_type=MESH_ID)
    copy.start()
    return copy


class Sum:
    def __init__(self, place, p, s, r1, t1, r2, t2, r3, g, ssem, rsem):
        self.place, self.p, self.q = place, p, 3 - p
        self.s, self.r1, self.t1, self.r2, self.t2, self.r3, self.g = s, r1, t1, r2, t2, r3, g
        self.ssem, self.rsem = ssem, rsem
        self.sent = []
        self.used = 0

    def pick(self, ref, k):
        return ref.at[:, :, k] if self.p == 2 else ref.at[:, k]

    def post(self, dim, src_of, dst_of):
        n = self.place.dims[dim]
        self.flight = []
        for j in range(1, n):
            k = lax.rem(self.place.at[dim] + j, n)
            i = self.used
            self.used += 1
            self.flight.append(send(src_of(k), dst_of(j - 1), self.ssem.at[i], self.rsem.at[i], self.place.peer(dim, k)))
        self.sent += self.flight

    def arrive(self):
        for c in self.flight:
            c.wait_recv()

    def add(self, mine, got, n):
        v = mine.astype(F32)
        for j in range(n):
            v = v + got[j].astype(F32)
        return v

    def send1(self):
        self.post(self.p, lambda k: self.pick(self.s, k), lambda j: self.r1.at[j])

    def send2(self):
        self.arrive()
        n = self.place.dims[self.p]
        self.t1[...] = self.add(self.pick(self.s, self.place.at[self.p])[...], self.r1, n - 1).astype(BF16)
        self.post(self.q, lambda k: self.t1.at[:, k], lambda j: self.r2.at[j])

    def send3(self):
        self.arrive()
        n = self.place.dims[self.q]
        self.t2[...] = self.add(self.t1[:, self.place.at[self.q]], self.r2, n - 1).astype(BF16)
        self.post(0, lambda k: self.t2.at[k], lambda j: self.r3.at[j])

    def result(self):
        self.arrive()
        return self.add(self.t2[self.place.at[0]], self.r3, self.place.dims[0] - 1)

    def gather1(self):
        mine = self.g.at[self.place.at[0], self.place.at[1], self.place.at[2]]
        self.post(0, lambda k: mine, lambda j: mine)

    def gather2(self):
        self.arrive()
        mine = self.g.at[:, self.place.at[1], self.place.at[2]]
        self.post(self.q, lambda k: mine, lambda j: mine)

    def gather3(self):
        self.arrive()
        mine = self.pick(self.g, self.place.at[self.p])
        self.post(self.p, lambda k: mine, lambda j: mine)

    def close(self):
        for c in self.sent:
            c.wait_send()


def hops(nb):
    return 2 * sum(d - 1 for d in torus(nb))


def conv_bwd_kernel(dm_ref, pooled_ref, slope_ref, p_ref, w_ref, mix_ref, dx_ref, dw_ref, small_ref,
                    fbuf, z, dpad, d2, dt, stage):
    towers, nb, slots, _ = dm_ref.shape
    per = fbuf.shape[2] // nb
    side = slope_ref.shape[0]
    cout = w_ref.shape[2]
    cin = p_ref.shape[3]
    pool = (side - 3) // 2 + 1
    wide = towers * cout
    cells = side * side
    for t in range(towers):
        for b in range(nb):
            fbuf[t, :, b * per:(b + 1) * per] = dm_ref[t, b, :, :per]
    z[0] = jnp.zeros(z.shape[1:], F32)
    z[pool + 1] = jnp.zeros(z.shape[1:], F32)
    acc = [[jnp.zeros((slots, cout), F32)] * 2 for _ in range(2)]
    for i in range(pool):
        z[i + 1, 0] = jnp.zeros(z.shape[2:], F32)
        z[i + 1, pool + 1] = jnp.zeros(z.shape[2:], F32)
        for j in range(pool):
            q = i * pool + j
            dm = [fbuf[t, :, q * cout:(q + 1) * cout].astype(F32) for t in range(towers)]
            for u in range(towers):
                pu = pooled_ref[q, :, u * cout:(u + 1) * cout]
                for t in range(towers):
                    acc[t][u] = acc[t][u] + dm[t] * pu
                z[i + 1, j + 1, :, u * cout:(u + 1) * cout] = (mix_ref[0, u][None] * dm[0] + mix_ref[1, u][None] * dm[1]) * (1.0 / 9.0)
    dpad[0] = jnp.zeros(dpad.shape[1:], BF16)
    dpad[side + 1] = jnp.zeros(dpad.shape[1:], BF16)
    d2[cells:] = jnp.zeros((d2.shape[0] - cells, slots, wide), BF16)
    def drow(y, src):
        dpad[y + 1, 0] = jnp.zeros((slots, wide), BF16)
        dpad[y + 1, side + 1] = jnp.zeros((slots, wide), BF16)
        for x in range(side):
            j = x // 2
            v = src(j + 1) if x % 2 else src(j) + src(j + 1)
            d = (v * slope_ref[y, x].astype(F32)).astype(BF16)
            dpad[y + 1, x + 1] = d
            d2[y * side + x] = d
    def pair(i, _):
        drow(2 * i, lambda j: z[i, j] + z[i + 1, j])
        drow(2 * i + 1, lambda j: z[i + 1, j])
        return 0
    lax.fori_loop(0, pool, pair, 0)
    drow(side - 1, lambda j: z[pool, j] + z[pool + 1, j])
    step = 256 // slots
    def flip(k, _):
        dt[:, pl.ds(pl.multiple_of(k * 256, 256), 256)] = d2[pl.ds(k * step, step)].reshape(256, wide).T
        return 0
    lax.fori_loop(0, d2.shape[0] // step, flip, 0)
    tail = (d2.shape[0] - cells) * slots
    for a in range(3):
        win = jnp.concatenate([p_ref[a:a + side, b:b + side].reshape(cells * slots, cin) for b in range(3)], axis=1)
        win = jnp.concatenate([win, jnp.zeros((tail, 3 * cin), BF16)], axis=0)
        dw_ref[a] = jnp.dot(dt[...], win, preferred_element_type=F32)
    ones = jnp.ones((d2.shape[0] * slots, 128), BF16)
    small_ref[:, 0:128] = jnp.dot(dt[...], ones, preferred_element_type=F32)
    rows = jnp.concatenate([jnp.concatenate([jnp.sum(acc[t][u], axis=0, keepdims=True) for u in range(2)], axis=1) for t in range(2)], axis=0)
    small_ref[:, 128:256] = jnp.concatenate([rows, jnp.zeros((126, wide), F32)], axis=0).T
    pitch = 16
    def xrow(y, n=1):
        lhs = jnp.concatenate([dpad[pl.ds(y + 2 - a, n), 2 - b:2 - b + side, :, t * cout:(t + 1) * cout].reshape(n * side * slots, cout)
                               for t in range(towers) for a in range(3) for b in range(3)], axis=1)
        rhs = jnp.concatenate([w_ref[t, (a * 3 + b) * cin:(a * 3 + b + 1) * cin, :]
                               for t in range(towers) for a in range(3) for b in range(3)], axis=1)
        out = lax.dot_general(lhs, rhs, (((1,), (1,)), ((), ())), preferred_element_type=F32).reshape(n * side, slots, cin)
        for x in range(side):
            for l in range(cin // 128):
                stage[l, pl.ds(y * pitch + x, slots, stride=side * pitch), :] = out[x, :, l * 128:(l + 1) * 128]
    lax.fori_loop(0, side, lambda y, _: (xrow(y), 0)[1], 0)
    def put(k, _):
        r = k // side
        i = k % side
        dx_ref[r, i] = jnp.concatenate([stage[l, pl.ds(pl.multiple_of(k * pitch, pitch), side), :] for l in range(cin // 128)], axis=1).astype(BF16)
        return 0
    lax.fori_loop(0, slots * side, put, 0, unroll=4)

def conv_bwd(dm, pooled, slope, p, w, mix, per):
    towers, nb, slots, _ = dm.shape
    side = slope.shape[0]
    cin = p.shape[3]
    cout = w.shape[4]
    pool = (side - 3) // 2 + 1
    wide = towers * cout
    V = pl.BlockSpec(memory_space=pltpu.VMEM)
    cells = -(-side * side * slots // 256) * 256 // slots
    return pl.pallas_call(
        conv_bwd_kernel,
        out_shape=[jax.ShapeDtypeStruct((slots, side, side, cin), BF16),
                   jax.ShapeDtypeStruct((3, wide, 3 * cin), F32),
                   jax.ShapeDtypeStruct((wide, 256), F32)],
        in_specs=[V] * 6, out_specs=[V] * 3,
        scratch_shapes=[pltpu.VMEM((towers, slots, nb * per), BF16),
                        pltpu.VMEM((pool + 2, pool + 2, slots, wide), F32),
                        pltpu.VMEM((side + 2, side + 2, slots, wide), BF16),
                        pltpu.VMEM((cells, slots, wide), BF16),
                        pltpu.VMEM((wide, cells * slots), BF16),
                        pltpu.VMEM((cin // 128, slots * side * 16, 128), F32)],
        compiler_params=pltpu.CompilerParams(vmem_limit_bytes=62 * 2**20),
    )(dm, pooled, slope, p, w.reshape(towers, 9 * cin, cout), mix)


def swap(block):
    return lax.ppermute(block, "tower", [(0, 1), (1, 0)])


def plain_shards(crop_pixels, live_rows, conv_weight, conv_bias, stitch_conv, fc_weight, fc_bias, stitch_fc, cotangent):
    slots = crop_pixels.shape[0]
    nb = lax.axis_size("batch")
    b, t = lax.axis_index("batch"), lax.axis_index("tower")
    rows = 2 * slots * nb
    live = rows // 2
    fc = fc_weight.shape[2]
    per = fc_weight.shape[1]
    cols = fc // nb
    w = fc_weight[0]
    feat, pooled, slope, padded = conv_fwd(live_rows, crop_pixels, conv_weight, conv_bias, stitch_conv, nb)
    both = ("batch", "tower")
    counts = lax.all_gather(live_rows, both, axis=0, tiled=True)
    got = lax.all_to_all(feat[..., :per].transpose(1, 0, 2, 3).reshape(2 * nb, slots, per), both, 0, 0).reshape(rows, per)
    slot = jnp.arange(rows, dtype=jnp.int32)
    start = jnp.cumsum(counts) - counts
    place = jnp.where(slot % slots < counts[slot // slots], start[slot // slots] + slot % slots, -1)
    spread = (place[:, None] == jnp.arange(live, dtype=jnp.int32)[None]).astype(BF16)
    compact = lambda x: lax.dot_general(spread, x, (((0,), (0,)), ((), ())), preferred_element_type=F32).astype(BF16)
    expand = lambda x: jnp.dot(spread, x, preferred_element_type=F32).astype(BF16)
    f = compact(got)
    part = jnp.dot(f, w, preferred_element_type=F32)
    hidden = lax.psum_scatter(part, "batch", scatter_dimension=1, tiled=True)
    hidden = hidden + lax.dynamic_slice_in_dim(fc_bias[0], b * cols, cols)[None]
    value, slope_fc = gelu_pair(hidden)
    gate = value.astype(BF16)
    cot = compact(lax.all_to_all(cotangent[0].reshape(2 * slots, nb, cols).transpose(1, 0, 2), "batch", 0, 0).reshape(rows, cols))
    gate_other, cot_other = swap(gate).astype(F32), swap(cot).astype(F32)
    gate_own, cot_own = gate.astype(F32), cot.astype(F32)
    mix = lax.dynamic_slice_in_dim(stitch_fc, b * cols, cols, axis=2)
    own = jnp.where(t == 0, mix[0, 0], mix[1, 1])
    cross = jnp.where(t == 0, mix[0, 1], mix[1, 0])
    back = jnp.where(t == 0, mix[1, 0], mix[0, 1])
    stitched = (own[None] * gate_own + cross[None] * gate_other).astype(BF16)
    stitched = lax.all_to_all(expand(stitched).reshape(nb, 2 * slots, cols), "batch", 0, 0)
    stitched = stitched.transpose(1, 0, 2).reshape(1, 2 * slots, fc)
    d_own = jnp.sum(cot_own * gate_own, axis=0)
    d_cross = jnp.sum(cot_own * gate_other, axis=0)
    dh = ((own[None] * cot_own + back[None] * cot_other) * slope_fc).astype(BF16)
    sums = jnp.stack([d_own, d_cross, jnp.sum(dh.astype(F32), axis=0)])
    sums = lax.all_gather(sums, both, axis=0).reshape(nb, 2, 3, cols).transpose(1, 2, 0, 3).reshape(2, 3, fc)
    d_stitch_fc = jnp.stack([sums[0, :2], sums[1, 1::-1]])
    d_fc_bias = sums[:, 2]
    dh = lax.all_gather(dh, "batch", axis=1, tiled=True)
    d_fc_weight = lax.dot_general(f, dh, (((0,), (0,)), ((), ())), preferred_element_type=F32)[None]
    df = lax.dot_general(dh, w, (((1,), (1,)), ((), ())), preferred_element_type=F32).astype(BF16)
    dm = lax.all_to_all(expand(df).reshape(2 * nb, slots, per), both, 0, 0)
    dm = dm.reshape(nb, 2, slots, per).transpose(1, 0, 2, 3)
    dx, dw, small = conv_bwd(dm, pooled, slope, padded, conv_weight, stitch_conv, per)
    dw = lax.psum(dw, both)
    cin, cout = conv_weight.shape[3:]
    dw = dw.reshape(3, 2, cout, 3, cin).transpose(1, 0, 3, 4, 2)
    small = lax.psum(small, both)
    d_conv_bias = small[:, 0].reshape(2, cout)
    d_stitch_conv = small[:, 128:130].T.reshape(2, 2, cout)
    return stitched, dx, dw, d_conv_bias, d_stitch_conv, d_fc_weight, d_fc_bias, d_stitch_fc


def whole_kernel(parts, per, live_ref, x_hbm, cw_hbm, cbias_ref, cmix_ref, cot_ref, w_hbm, bias_ref, fmix_ref,
                 out_ref, dx_hbm, f_ref, g, grad_ref, stitch_ref, fbias_ref,
                 dxv, cw, act, p, slope, pooled, fbuf, feat, fin, dm, w, cin, cgot, sgot, spread,
                 s, r1, t1, r2, t2, r3, gates, cots, wide, acc,
                 z, dpad, d2, dt, keep, cs_, cr1, ct1, cr2, ct2, cr3, sums_t,
                 xsem, lsem, wsem, fs, fr, cs, cr, xs, xr, ss, sr, ms, mr, gs, gr, ds, dr, ks, kr, hs, hr):
    nb = cin.shape[0]
    place = Place(nb)
    b, t = place.b, place.t
    me = b * 2 + t
    total = 2 * nb
    side, _, slots, chan = dxv.shape
    towers, _, cout = cw.shape
    pool = (side - 3) // 2 + 1
    wide_c = towers * cout
    padded = feat.shape[2]
    rows = total * slots
    live = rows // 2
    cols = cin.shape[2]
    other = (b, 1 - t)
    device = lambda d: (d // 2, d % 2)

    load = pltpu.make_async_copy(x_hbm, p.at[pl.ds(1, side), pl.ds(1, side)], xsem.at[0])
    load.start()
    cw_load = pltpu.make_async_copy(cw_hbm, cw, lsem)
    cw_load.start()
    w_loads = [pltpu.make_async_copy(w_hbm.at[:, pl.ds(k * cols, cols)], w.at[k], wsem.at[k]) for k in range(nb)]
    for c in w_loads:
        c.start()
    bar = pltpu.get_barrier_semaphore()
    def hail(k, _):
        pl.semaphore_signal(bar, inc=1, device_id=device(lax.rem(me + k, total)), device_id_type=MESH_ID)
        return 0
    lax.fori_loop(1, total, hail, 0)
    for k in range(nb):
        cin[k] = cot_ref[:, k * cols:(k + 1) * cols]
    cgot[b] = cin[b]

    p[0] = jnp.zeros(p.shape[1:], BF16)
    p[side + 1] = jnp.zeros(p.shape[1:], BF16)
    for i in range(side):
        p[i + 1, 0] = jnp.zeros((slots, chan), BF16)
        p[i + 1, side + 1] = jnp.zeros((slots, chan), BF16)

    pl.semaphore_wait(bar, total - 1)
    def cot_copy(k):
        d = lax.rem(b + k, nb)
        return pltpu.make_async_remote_copy(
            src_ref=cin.at[d], dst_ref=cgot.at[b], send_sem=cs.at[k], recv_sem=cr.at[k],
            device_id=(d, t), device_id_type=MESH_ID)
    lax.fori_loop(1, nb, lambda k, _: (cot_copy(k).start(), 0)[1], 0)

    load.wait()
    cw_load.wait()
    turn = place.at[0] * 2 < place.dims[0]
    flags = (lax.broadcasted_iota(jnp.int32, (slots, padded - per), 0) < live_ref[0]).astype(F32).astype(BF16)
    m_rows = side * slots
    def conv_row(k):
        y = jnp.where(turn, side - 1 - k, k)
        window = jnp.concatenate([p[y + a, c:c + side].reshape(m_rows, chan) for a in range(3) for c in range(3)], axis=1)
        for u in range(towers):
            pre = jnp.dot(window, cw[u], preferred_element_type=F32) + cbias_ref[u][None]
            value, inc = gelu_pair(pre)
            act[lax.rem(k, 3), :, :, u * cout:(u + 1) * cout] = value.reshape(side, slots, cout)
            slope[y, :, :, u * cout:(u + 1) * cout] = inc.astype(slope.dtype).reshape(side, slots, cout)
    def feature_copy(d):
        return pltpu.make_async_remote_copy(
            src_ref=feat.at[d], dst_ref=fin.at[me], send_sem=fs.at[d], recv_sem=fr.at[me],
            device_id=device(d), device_id_type=MESH_ID)
    def feature_wait(d):
        return pltpu.make_async_remote_copy(
            src_ref=feat.at[d], dst_ref=fin.at[d], send_sem=fs.at[d], recv_sem=fr.at[d],
            device_id=device(d), device_id_type=MESH_ID)
    pairs = nb // 2
    conv_row(0)
    def pooled_row(n, _):
        lax.fori_loop(2 * n + 1, 2 * n + 3, lambda k, _: (conv_row(k), 0)[1], 0)
        i = jnp.where(turn, pool - 1 - n, n)
        s3 = act[0] + act[1] + act[2]
        for j in range(pool):
            p9 = (s3[2 * j] + s3[2 * j + 1] + s3[2 * j + 2]) * (1.0 / 9.0)
            pooled[i * pool + j] = p9
            at = pl.ds(pl.multiple_of((i * pool + j) * cout, cout), cout)
            for u in range(towers):
                m = cmix_ref[u, 0][None] * p9[:, :cout] + cmix_ref[u, 1][None] * p9[:, cout:]
                fbuf[u, :, at] = m.astype(BF16)
        def pair(q, _):
            c = jnp.where(turn, pairs - 1 - q, q)
            for u in range(towers):
                v = fbuf[u, :, pl.ds(pl.multiple_of(c * 2 * per, 128), 2 * per)]
                for h in range(2):
                    d = (2 * c + h) * 2 + u
                    feat[d, :, :per] = v[:, h * per:(h + 1) * per]
                    feat[d, :, per:] = flags
                    @pl.when(d != me)
                    def _():
                        feature_copy(d).start()
            return 0
        lax.fori_loop(n * pairs // pool, (n + 1) * pairs // pool, pair, 0)
        return 0
    lax.fori_loop(0, pool, pooled_row, 0)
    fin[me] = feat[me]
    def others(body):
        lax.fori_loop(1, total, lambda k, _: (body(lax.rem(me + k, total)), 0)[1], 0)
    others(lambda d: feature_wait(d).wait_recv())

    got = fin[...].reshape(rows, padded)
    flag = got[:, per:per + 1]
    lower = (lax.broadcasted_iota(jnp.int32, (rows, rows), 1) < lax.broadcasted_iota(jnp.int32, (rows, rows), 0)).astype(BF16)
    index = jnp.dot(lower, jnp.broadcast_to(flag, (rows, 128)), preferred_element_type=F32)[:, :1].astype(jnp.int32)
    hit = (index == lax.broadcasted_iota(jnp.int32, (rows, live), 1)) & (flag.astype(F32) > 0.5)
    spread[...] = hit.astype(F32).astype(BF16)
    pack = lambda v: lax.dot_general(spread[...], v, (((0,), (0,)), ((), ())), preferred_element_type=F32)
    f = pack(got[:, :per]).astype(BF16)
    for c in w_loads:
        c.wait()
    chips = [((k // (place.dims[1] * place.dims[2])), (k // place.dims[2]) % place.dims[1], k % place.dims[2]) for k in range(nb)]
    for k, i in enumerate(chips):
        s[i] = jnp.dot(f, w[k], preferred_element_type=F32).astype(BF16)
    size = live // (2 * parts)
    pieces = []
    for n in range(2 * parts):
        half = n % 2
        low = pl.ds(((n // 2) + half * parts) * size, size)
        pieces.append((Sum(place, 2 - half, s.at[:, :, :, low], r1.at[n], t1.at[n], r2.at[n], t2.at[n], r3.at[n],
                           g.at[:, :, :, low], gs.at[n], gr.at[n]), low))
    for piece, _ in pieces:
        piece.send1()
    f_ref[...] = f.T
    lax.fori_loop(1, nb, lambda k, _: (cot_copy(k).wait_recv(), 0)[1], 0)
    cots[0] = pack(cgot[...].reshape(rows, cols)).astype(BF16)
    cot_swap = send(cots.at[0], cots.at[1], xs.at[0], xr.at[0], other)
    mine_cols = pl.ds(pl.multiple_of(b * cols, 128), cols)
    mixes = lambda i, j: fmix_ref[i, j:j + 1, mine_cols]
    first = t == 0
    own = jnp.where(first, mixes(0, 0), mixes(1, 1))
    cross = jnp.where(first, mixes(0, 1), mixes(1, 0))
    back = jnp.where(first, mixes(1, 0), mixes(0, 1))
    here = place.at
    def gate_piece(piece, low):
        value, inc = gelu_pair(piece.result() + bias_ref[:, mine_cols])
        gates[0, low, :] = value.astype(BF16)
        d_gate = own * cots[0, low, :].astype(F32) + back * cots[1, low, :].astype(F32)
        g[here[0], here[1], here[2], low, :] = (d_gate * inc).astype(BF16)
        piece.gather1()
    todo = [lambda q, low: q.send2(), lambda q, low: q.send3(), gate_piece]
    for step in range(parts + 2):
        for k in range(3):
            c = step - k
            if 0 <= c < parts:
                if k == 2 and c == 0:
                    cot_swap.wait_recv()
                for piece, low in pieces[2 * c:2 * c + 2]:
                    todo[k](piece, low)
    gate_swap = send(gates.at[0], gates.at[1], xs.at[1], xr.at[1], other)
    for piece, low in pieces[:2]:
        piece.gather2()
    gate_swap.wait_recv()
    gate, cot, gate_other = gates[0].astype(F32), cots[0].astype(F32), gates[1].astype(F32)
    total_rows = [jnp.sum(cot * gate, axis=0, keepdims=True), jnp.sum(cot * gate_other, axis=0, keepdims=True),
                  jnp.sum(g[here[0], here[1], here[2]].astype(F32), axis=0, keepdims=True)]
    fold = cols // 128
    lines = [v[:, k * 128:(k + 1) * 128] for v in total_rows for k in range(fold)]
    wide[me] = jnp.concatenate(lines + [jnp.zeros((8 - len(lines), 128), F32)], axis=0)
    def sums_copy(k):
        d = lax.rem(me + k, total)
        return pltpu.make_async_remote_copy(
            src_ref=wide.at[me], dst_ref=wide.at[me], send_sem=ms.at[k], recv_sem=mr.at[k],
            device_id=device(d), device_id_type=MESH_ID)
    def drain(k, _):
        cot_copy(k).wait_send()
        return 0
    lax.fori_loop(1, nb, drain, 0)
    stitched = (own * gate + cross * gate_other).astype(BF16)
    cin[...] = jnp.dot(spread[...], stitched, preferred_element_type=F32).astype(BF16).reshape(cin.shape)
    def stitched_copy(k):
        d = lax.rem(b + k, nb)
        return pltpu.make_async_remote_copy(
            src_ref=cin.at[d], dst_ref=sgot.at[b], send_sem=ss.at[k], recv_sem=sr.at[k],
            device_id=(d, t), device_id_type=MESH_ID)
    lax.fori_loop(1, total, lambda k, _: (sums_copy(k).start(), 0)[1], 0)
    lax.fori_loop(1, nb, lambda k, _: (stitched_copy(k).start(), 0)[1], 0)
    sgot[b] = cin[b]
    for c in range(1, parts):
        for piece, low in pieces[2 * c:2 * c + 2]:
            piece.gather2()
        for piece, low in pieces[2 * c - 2:2 * c]:
            piece.gather3()
    for piece, low in pieces[-2:]:
        piece.gather3()
    for piece, low in pieces:
        piece.arrive()
    acc[...] = jnp.zeros(acc.shape, F32)
    for k, i in enumerate(chips):
        acc[...] += lax.dot_general(g[i], w[k], (((1,), (1,)), ((), ())), preferred_element_type=F32)
    others(lambda d: feature_wait(d).wait_send())
    feat[:, :, :per] = jnp.dot(spread[...], acc[...].astype(BF16), preferred_element_type=F32).astype(BF16).reshape(total, slots, per)
    def grad_copy(k):
        d = lax.rem(me + k, total)
        return pltpu.make_async_remote_copy(
            src_ref=feat.at[d], dst_ref=dm.at[t, b], send_sem=ds.at[k], recv_sem=dr.at[k],
            device_id=device(d), device_id_type=MESH_ID)
    lax.fori_loop(1, total, lambda k, _: (grad_copy(k).start(), 0)[1], 0)
    dm[t, b] = feat[me]
    lax.fori_loop(1, nb, lambda k, _: (stitched_copy(k).wait_recv(), 0)[1], 0)
    for k in range(nb):
        out_ref[0, :, k * cols:(k + 1) * cols] = sgot[k]
    lax.fori_loop(1, total, lambda k, _: (sums_copy(k).wait_recv(), 0)[1], 0)
    for k in range(nb):
        for u in range(2):
            for j in range(fold):
                at = slice(k * cols + j * 128, k * cols + (j + 1) * 128)
                stitch_ref[u, u:u + 1, at] = wide[2 * k + u, j:j + 1]
                stitch_ref[u, 1 - u:2 - u, at] = wide[2 * k + u, fold + j:fold + j + 1]
                fbias_ref[u:u + 1, at] = wide[2 * k + u, 2 * fold + j:2 * fold + j + 1]
    lax.fori_loop(1, total, lambda k, _: (grad_copy(k).wait_recv(), 0)[1], 0)

    for u in range(towers):
        for k in range(nb):
            fbuf[u, :, k * per:(k + 1) * per] = dm[u, k, :, :per]
    z[0] = jnp.zeros(z.shape[1:], F32)
    z[pool + 1] = jnp.zeros(z.shape[1:], F32)
    mixed = [[jnp.zeros((slots, cout), F32)] * 2 for _ in range(2)]
    for i in range(pool):
        z[i + 1, 0] = jnp.zeros(z.shape[2:], F32)
        z[i + 1, pool + 1] = jnp.zeros(z.shape[2:], F32)
        for j in range(pool):
            q = i * pool + j
            dmx = [fbuf[u, :, q * cout:(q + 1) * cout].astype(F32) for u in range(towers)]
            for u in range(towers):
                pu = pooled[q, :, u * cout:(u + 1) * cout]
                for v in range(towers):
                    mixed[v][u] = mixed[v][u] + dmx[v] * pu
                z[i + 1, j + 1, :, u * cout:(u + 1) * cout] = (cmix_ref[0, u][None] * dmx[0] + cmix_ref[1, u][None] * dmx[1]) * (1.0 / 9.0)
    lines = [jnp.concatenate([jnp.sum(mixed[v][u], axis=0, keepdims=True) for u in range(2)], axis=1) for v in range(2)]
    sums_t[...] = jnp.concatenate([jnp.zeros((1, wide_c), F32)] + lines + [jnp.zeros((125, wide_c), F32)], axis=0).T
    cells = side * side
    dpad[0] = jnp.zeros(dpad.shape[1:], BF16)
    dpad[side + 1] = jnp.zeros(dpad.shape[1:], BF16)
    d2[cells:] = jnp.zeros((d2.shape[0] - cells, slots, wide_c), BF16)
    def drow(y, src):
        dpad[y + 1, 0] = jnp.zeros((slots, wide_c), BF16)
        dpad[y + 1, side + 1] = jnp.zeros((slots, wide_c), BF16)
        for x in range(side):
            j = x // 2
            v = src(j + 1) if x % 2 else src(j) + src(j + 1)
            d = (v * slope[y, x].astype(F32)).astype(BF16)
            dpad[y + 1, x + 1] = d
            d2[y * side + x] = d
    def two(i, _):
        drow(2 * i, lambda j: z[i, j] + z[i + 1, j])
        drow(2 * i + 1, lambda j: z[i + 1, j])
        return 0
    lax.fori_loop(0, pool, two, 0)
    drow(side - 1, lambda j: z[pool, j] + z[pool + 1, j])
    block = 256 // slots
    def flip(k, _):
        dt[:, pl.ds(pl.multiple_of(k * 256, 256), 256)] = d2[pl.ds(k * block, block)].reshape(256, wide_c).T
        return 0
    lax.fori_loop(0, d2.shape[0] // block, flip, 0)

    chunks, span = grad_ref.shape[1], grad_ref.shape[-1]
    tail = dt.shape[1] - cells * slots
    give = w.at[0:chunks, 0:cout]
    take = w.at[0:chunks, cout:2 * cout]

    def window(n):
        parts_ = []
        low = n * span
        while low < (n + 1) * span:
            k = low // chan
            if k < 9:
                high = min((n + 1) * span, (k + 1) * chan)
                a, c = k // 3, k % 3
                parts_.append(p[a:a + side, c:c + side, :, low - k * chan:high - k * chan].reshape(cells * slots, high - low))
                low = high
            else:
                parts_.append(jnp.ones((cells * slots, (n + 1) * span - low), BF16))
                low = (n + 1) * span
        win = parts_[0] if len(parts_) == 1 else jnp.concatenate(parts_, axis=1)
        return jnp.concatenate([win, jnp.zeros((tail, span), BF16)], axis=0)

    lots = [Sum(place, 2 - n % 2, cs_.at[n], cr1.at[n], ct1.at[n], cr2.at[n], ct2.at[n], cr3.at[n], grad_ref.at[t, n], ks.at[n], kr.at[n])
            for n in range(chunks)]
    core, share_back = {}, {}

    def tower(u):
        return pl.ds(pl.multiple_of(u * cout, cout), cout)

    def compute(n):
        slot = n % keep.shape[0]
        v = jnp.dot(dt[...], window(n), preferred_element_type=F32)
        if n == chunks - 1:
            extra = sums_t[...]
            lane = lax.broadcasted_iota(jnp.int32, extra.shape, 1)
            v = jnp.concatenate([v[:, :span - 128], jnp.where(lane == 0, v[:, span - 128:], extra)], axis=1)
        keep[slot] = v
        give[n] = keep[slot, tower(1 - t)].astype(BF16)
        core[n] = send(give.at[n], take.at[n], hs.at[n, 0], hr.at[n, 0], other)

    def merge(n):
        core[n].wait_recv()
        cs_[n] = (keep[n % keep.shape[0], tower(t)] + take[n].astype(F32)).astype(BF16).reshape(cs_.shape[1:])
        lots[n].send1()

    def finish(n):
        grad_ref[t, n, here[0], here[1], here[2]] = lots[n].result().astype(BF16)
        lots[n].gather1()

    def share(n):
        lots[n].arrive()
        share_back[n] = send(grad_ref.at[t, n], grad_ref.at[t, n], hs.at[n, 1], hr.at[n, 1], other)

    def xrow(y):
        lhs = jnp.concatenate([dpad[y + 2 - a, 2 - c:2 - c + side, :, u * cout:(u + 1) * cout].reshape(m_rows, cout)
                               for u in range(towers) for a in range(3) for c in range(3)], axis=1)
        rhs = jnp.concatenate([cw[u, (a * 3 + c) * chan:(a * 3 + c + 1) * chan, :]
                               for u in range(towers) for a in range(3) for c in range(3)], axis=1)
        o = lax.dot_general(lhs, rhs, (((1,), (1,)), ((), ())), preferred_element_type=F32).reshape(side, slots, chan)
        dxv[y] = o.astype(BF16)
        c = pltpu.make_async_copy(dxv.at[y], dx_hbm.at[y], xsem.at[y])
        c.start()
        stores.append(c)

    stores = []
    side_work = [functools.partial(xrow, y) for y in range(side)]
    work = [merge, lambda n: lots[n].send2(), lambda n: lots[n].send3(), finish,
            lambda n: lots[n].gather2(), lambda n: lots[n].gather3(), share, lambda n: share_back[n].wait_recv()]
    for step in range(chunks + 3 * (len(work) - 1) + 1):
        if step < chunks:
            compute(step)
        if step >= 14 and side_work:
            side_work.pop(0)()
        for k, job in enumerate(work):
            n = step - 1 - 3 * k
            if 0 <= n < chunks:
                job(n)
    for job in side_work:
        job()
    for c in stores:
        c.wait()
    for piece, _ in pieces:
        piece.close()
    cot_swap.wait_send()
    gate_swap.wait_send()
    for n in range(chunks):
        lots[n].close()
        core[n].wait_send()
        share_back[n].wait_send()
    def drain_all(k, _):
        grad_copy(k).wait_send()
        sums_copy(k).wait_send()
        return 0
    lax.fori_loop(1, total, drain_all, 0)
    lax.fori_loop(1, nb, lambda k, _: (stitched_copy(k).wait_send(), 0)[1], 0)


def whole_layer(live_rows, x, cw, cbias, cmix, cot, w, fbias, fmix, nb, parts=2):
    side, _, slots, chan = x.shape
    towers, _, cout = cw.shape
    per, fc = w.shape
    cols = fc // nb
    total = 2 * nb
    rows = total * slots
    live = rows // 2
    pool = (side - 3) // 2 + 1
    padded = per // 128 * 128 + 128
    wide = towers * cout
    d0, d1, d2 = torus(nb)
    size = live // (2 * parts)
    n = 2 * parts
    span = 256
    chunks = (9 * chan + 128) // span
    h = cout // nb
    cells = -(-side * side * slots // 256) * 256 // slots
    V = pl.BlockSpec(memory_space=pltpu.VMEM)
    A = pl.BlockSpec(memory_space=pl.ANY)
    vm = lambda *shape: pltpu.VMEM(shape, BF16)
    vf = lambda *shape: pltpu.VMEM(shape, F32)
    dma = lambda *shape: pltpu.SemaphoreType.DMA(shape)
    shape = jax.ShapeDtypeStruct
    return pl.pallas_call(
        functools.partial(whole_kernel, parts, per),
        out_shape=[shape((1, 2 * slots, fc), BF16), shape(x.shape, BF16), shape((per, live), BF16),
                   shape((d0, d1, d2, live, cols), BF16), shape((towers, chunks, d0, d1, d2, h, span), BF16),
                   shape((2, 2, fc), F32), shape((2, fc), F32)],
        in_specs=[pl.BlockSpec(memory_space=pltpu.SMEM), A, A, V, V, V, A, V, V],
        out_specs=[V, A, V, V, V, V, V],
        scratch_shapes=[
            vm(*x.shape), vm(*cw.shape), vf(3, side, slots, wide),
            vm(side + 2, side + 2, slots, chan), vf(side, side, slots, wide), vf(pool * pool, slots, wide),
            vm(towers, slots, nb * per), vm(total, slots, padded), vm(total, slots, padded), vm(towers, nb, slots, padded),
            vm(nb, per, cols), vm(nb, 2 * slots, cols), vm(nb, 2 * slots, cols), vm(nb, 2 * slots, cols), vm(rows, live),
            vm(d0, d1, d2, live, cols), vm(n, d1 - 1, d0, d1, size, cols), vm(n, d0, d1, size, cols),
            vm(n, d1 - 1, d0, size, cols), vm(n, d0, size, cols), vm(n, d0 - 1, size, cols),
            vm(2, live, cols), vm(2, live, cols), vf(total, 8, 128), vf(live, per),
            vf(pool + 2, pool + 2, slots, wide), vm(side + 2, side + 2, slots, wide), vm(cells, slots, wide), vm(wide, cells * slots),
            vf(2, wide, span), vm(chunks, d0, d1, d2, h, span), vm(chunks, d1 - 1, d0, d1, h, span), vm(chunks, d0, d1, h, span),
            vm(chunks, d1 - 1, d0, h, span), vm(chunks, d0, h, span), vm(chunks, d0 - 1, h, span), vf(wide, 128),
            dma(side), pltpu.SemaphoreType.DMA, dma(nb), dma(total), dma(total), dma(nb), dma(nb), dma(2), dma(2), dma(nb), dma(nb),
            dma(total), dma(total), dma(n, hops(nb)), dma(n, hops(nb)), dma(total), dma(total),
            dma(chunks, hops(nb)), dma(chunks, hops(nb)), dma(chunks, 2), dma(chunks, 2)],
        compiler_params=pltpu.CompilerParams(collective_id=1, has_side_effects=True, vmem_limit_bytes=63 * 2**20),
    )(live_rows, x, cw, cbias, cmix, cot, w, fbias, fmix)


def write_kernel(pad, f_ref, g_ref, dw_ref, st_ref, fs_ref, fb_ref, fc_ref, conv_ref, bias_ref, mix_ref, st_out, fs_out, fb_out):
    cols = g_ref.shape[2]
    for i in range(g_ref.shape[0]):
        fc_ref[0, :, i * cols:(i + 1) * cols] = jnp.dot(f_ref[...], g_ref[i], preferred_element_type=F32)
    flat = [jnp.concatenate([dw_ref[u, k].T for k in range(dw_ref.shape[1])], axis=0).astype(F32) for u in range(dw_ref.shape[0])]
    half = flat[0].shape[0] - 128 - pad
    for u, v in enumerate(flat):
        conv_ref[u] = v
        bias_ref[u:u + 1] = v[half:half + 1]
        mix_ref[0, u:u + 1] = v[half + 1:half + 2]
        mix_ref[1, u:u + 1] = v[half + 2:half + 3]
    st_out[...] = st_ref[...]
    fs_out[...] = fs_ref[...]
    fb_out[...] = fb_ref[...]


def write_grads(f, g, dw, stitched, d_stitch, d_bias, nb, cols, ktaps):
    per, live = f.shape
    towers, chunks, cout, span = dw.shape
    group = 1024 // span
    last = -(-chunks // group) - 1
    fold = 1024 // cols
    shape = jax.ShapeDtypeStruct
    fixed = lambda v: pl.BlockSpec(v.shape, lambda k: (0,) * v.ndim)
    small = [stitched, d_stitch, d_bias]
    return pl.pallas_call(
        functools.partial(write_kernel, (last + 1) * group * span - chunks * span),
        grid=(nb // fold,),
        out_shape=[shape((1, per, nb * cols), F32), shape((towers, ktaps, cout), F32), shape((towers, cout), F32),
                   shape((2, towers, cout), F32)] + [shape(v.shape, v.dtype) for v in small],
        in_specs=[pl.BlockSpec((per, live), lambda k: (0, 0)), pl.BlockSpec((fold, live, cols), lambda k: (k, 0, 0)),
                  pl.BlockSpec((towers, group, cout, span), lambda k: (0, jnp.minimum(k, last), 0, 0))] + [fixed(v) for v in small],
        out_specs=[pl.BlockSpec((1, per, fold * cols), lambda k: (0, 0, k)),
                   pl.BlockSpec((towers, group * span, cout), lambda k: (0, jnp.minimum(k, last), 0)),
                   pl.BlockSpec((towers, cout), lambda k: (0, 0)), pl.BlockSpec((2, towers, cout), lambda k: (0, 0, 0))] + [fixed(v) for v in small],
        compiler_params=pltpu.CompilerParams(vmem_limit_bytes=60 * 2**20),
    )(f, g, dw, *small)


def shards(crop_pixels, live_rows, conv_weight, conv_bias, stitch_conv, fc_weight, fc_bias, stitch_fc, cotangent):
    slots = crop_pixels.shape[0]
    nb = lax.axis_size("batch")
    fc = fc_weight.shape[2]
    cols = fc // nb
    cin, cout = conv_weight.shape[3:]
    live = slots * nb
    stitched, dx, f, dh, dw, d_stitch_fc, d_fc_bias = whole_layer(
        live_rows, crop_pixels.transpose(1, 2, 0, 3), conv_weight.reshape(2, 9 * cin, cout), conv_bias, stitch_conv, cotangent[0], fc_weight[0], fc_bias, stitch_fc, nb)
    dw = dw.reshape(2, dw.shape[1], cout, dw.shape[-1])
    d_fc_weight, d_kernel, d_conv_bias, d_stitch_conv, stitched, d_stitch_fc, d_fc_bias = write_grads(
        f, dh.reshape(nb, live, cols), dw, stitched, d_stitch_fc, d_fc_bias, nb, cols, 9 * cin)
    return stitched, dx.transpose(2, 0, 1, 3), d_kernel.reshape(conv_weight.shape), d_conv_bias, d_stitch_conv, d_fc_weight, d_fc_bias, d_stitch_fc


def solution(mesh):
    in_specs = (
        P(("batch", "tower"), None, None, None), P(("batch", "tower")), P(), P(), P(),
        P("tower", "batch", None), P("tower", None), P(), P("tower", "batch", None),
    )
    out_specs = (
        P("tower", "batch", None), P(("batch", "tower"), None, None, None), P(), P(), P(),
        P("tower", "batch", None), P(), P(),
    )
    body = shards if mesh.shape["batch"] == 16 else plain_shards
    return jax.shard_map(body, mesh=mesh, in_specs=in_specs, out_specs=out_specs, check_vma=False)
```
